32 devices in a mesh: dp: 8 (over y, x, core), tp: 4 (over z).
Axes of the slice: x: 2, y: 2, z: 4, core: 2. Of those that a mesh axis runs over, the one named last changes fastest.
Arguments:
- tokens: bfloat16 [16384, 1024], P(('dp', 'tp')), may hold values from -6 to 6
- segments: int32 [16, 1024], P('dp'), may hold values from 0 to 15, never falling along the last dimension, each value on 1 to 512 neighbouring positions
- cotangent: bfloat16 [16384, 1024], P(('dp', 'tp')), may hold values from -6 to 6
- attn_gain: bfloat16 [1024], P('dp'), may hold values from 0.099609375 to 1.8984375
- q_weight: bfloat16 [1024, 1024], P('dp', 'tp'), may hold values from -0.1875 to 0.1875
- k_weight: bfloat16 [1024, 512], P('dp', 'tp'), may hold values from -0.1875 to 0.1875
- v_weight: bfloat16 [1024, 512], P('dp', 'tp'), may hold values from -0.1875 to 0.1875
- query_gain: bfloat16 [64], P('dp'), may hold values from 0.099609375 to 1.8984375
- key_gain: bfloat16 [64], P('dp'), may hold values from 0.099609375 to 1.8984375
- o_weight: bfloat16 [1024, 1024], P('dp', 'tp'), may hold values from -0.75 to 0.75
- ffn_gain: bfloat16 [1024], P('dp'), may hold values from 0.099609375 to 1.8984375
- gate_weight: bfloat16 [1024, 4608], P('dp', 'tp'), may hold values from -0.1875 to 0.1875
- up_weight: bfloat16 [1024, 4608], P('dp', 'tp'), may hold values from -0.1875 to 0.1875
- down_weight: bfloat16 [1024, 4608], P('dp', 'tp'), may hold values from -0.09375 to 0.09375
Outputs:
- output: bfloat16 [16384, 1024], P(('dp', 'tp'))
- tokens_grad: bfloat16 [16384, 1024], P(('dp', 'tp'))
- attn_gain_grad: float32 [1024], P('dp')
- q_weight_grad: float32 [1024, 1024], P('dp', 'tp')
- k_weight_grad: float32 [1024, 512], P('dp', 'tp')
- v_weight_grad: float32 [1024, 512], P('dp', 'tp')
- query_gain_grad: float32 [64], P('dp')
- key_gain_grad: float32 [64], P('dp')
- o_weight_grad: float32 [1024, 1024], P('dp', 'tp')
- ffn_gain_grad: float32 [1024], P('dp')
- gate_weight_grad: float32 [1024, 4608], P('dp', 'tp')
- up_weight_grad: float32 [1024, 4608], P('dp', 'tp')
- down_weight_grad: float32 [1024, 4608], P('dp', 'tp')
The draws below stay inside these ranges and needn't reach their ends.
Inputs may be any that keep to these rules, and one draw needn't show every extreme that they name: `segments`: within a sequence the document numbers never fall; every document has 1 to 512 tokens, and some document has exactly 512.
All inputs are finite; a program needn't handle non-finite values.
Results may differ from the reference program's by a relative error of at most 0.019.
Values may be sent and summed in bfloat16 or wider, within the bound.
No kernel may reach another device: no remote copies, remote signals or barrier semaphores. Data moves between devices by JAX's collectives and lax.ppermute only.
A program may use at most 192 MiB of HBM per device.

```python
import math
import jax
import jax.numpy as jnp
import numpy as np
from jax import lax

D = 1024
HD = 64
FF = 4608
SEQ_DP = 2
LEN = 1024
DOCS = 16
HQD = 1024
KVD = 512
SEQS = 16
TOKENS = 16384


def shard_levels(rng, extent, split, low, high):
    def one(axis_at, blocks):
        steps = jax.random.uniform(jax.random.fold_in(jax.random.fold_in(rng, 6), axis_at), (blocks,), jnp.float32, low / len(split), high / len(split))
        return jnp.repeat(jnp.exp(steps), extent[axis_at] // blocks).reshape((-1,) + (1,) * (len(extent) - axis_at - 1))

    factor_of = one(*split[0])
    for cut in split[1:]:
        factor_of = factor_of * one(*cut)
    return factor_of


def length_profile(number_of, total, limit, skew):
    weights = [(1 << 20) // math.isqrt(grade ** skew) + 1 for grade in range(2, number_of + 1)]
    surplus, given = total - limit - (number_of - 1), [1] * (number_of - 1)
    while surplus > 0:
        candidates = [i for i in range(number_of - 1) if given[i] < limit]
        pool, left = sum([weights[i] for i in candidates]), surplus
        for i in candidates:
            extra = min(limit - given[i], max(1, left * weights[i] // pool), surplus)
            given[i] = given[i] + extra
            surplus = surplus - extra
    return np.array([limit] + given)


def uneven_parts(key, count, total, limit, lean):
    if count == 2:
        one = jax.random.randint(key, (), max(1, total - limit), min(limit, total - 1) + 1)
        return jnp.stack([one, total - one])
    lengths = jnp.asarray(length_profile(count, total, limit, lean), jnp.int32)
    couples = (count - 1) // 2
    donor, taker = lengths[1:1 + 2 * couples:2], lengths[2:2 + 2 * couples:2]
    room = jnp.minimum(donor - 1, limit - taker)
    shifted = jax.random.randint(jax.random.fold_in(key, 1), (couples,), 0, 1 << 20) % (room + 1)
    lengths = lengths.at[1:1 + 2 * couples:2].set(donor - shifted).at[2:2 + 2 * couples:2].set(taker + shifted)
    return lengths[jax.random.permutation(jax.random.fold_in(key, 2), count)]


def centred(stream_key, extent, spread, bound, cuts=(), held_as=jnp.bfloat16):
    array = jax.random.normal(stream_key, extent, jnp.float32) * spread
    if len(cuts) > 0:
        array = shard_levels(stream_key, extent, cuts, -0.22, 0.18) * array
    return jnp.clip(array, min=-bound, max=bound).astype(held_as)


def setup_inputs(seed: int = 0) -> dict:
    streams_of = jax.random.split(jax.random.key(seed), 15)
    return {
        "tokens": centred(streams_of[0], (TOKENS, D), 1.0, 6.0, ((0, 32),)),
        "segments": jax.vmap(lambda own: jnp.searchsorted(jnp.cumsum(uneven_parts(own, DOCS, LEN, LEN // 2, 2)), jnp.arange(LEN), side="right"))(jax.random.split(streams_of[1], SEQS)).reshape((SEQS, LEN)).astype(jnp.int32),
        "cotangent": centred(streams_of[2], (TOKENS, D), 1.0, 6.0, ((0, 32),)),
        "attn_gain": jnp.clip(1.0 + 0.18 * jax.random.normal(streams_of[3], (D,), jnp.float32), 0.099609375, 1.8984375).astype(jnp.bfloat16),
        "q_weight": centred(streams_of[4], (D, HQD), D ** -0.5, 0.1875, ((0, 8), (1, 4))),
        "k_weight": centred(streams_of[5], (D, KVD), D ** -0.5, 0.1875, ((0, 8), (1, 4))),
        "v_weight": centred(streams_of[6], (D, KVD), D ** -0.5, 0.1875, ((0, 8), (1, 4))),
        "query_gain": jnp.clip(1.0 + 0.18 * jax.random.normal(streams_of[7], (HD,), jnp.float32), 0.099609375, 1.8984375).astype(jnp.bfloat16),
        "key_gain": jnp.clip(1.0 + 0.18 * jax.random.normal(streams_of[8], (HD,), jnp.float32), 0.099609375, 1.8984375).astype(jnp.bfloat16),
        "o_weight": centred(streams_of[9], (D, HQD), (D // 16) ** -0.5, 0.75, ((0, 8), (1, 4))),
        "ffn_gain": jnp.clip(1.0 + 0.18 * jax.random.normal(streams_of[10], (D,), jnp.float32), 0.099609375, 1.8984375).astype(jnp.bfloat16),
        "gate_weight": centred(streams_of[11], (D, FF), D ** -0.5, 0.1875, ((0, 8), (1, 4))),
        "up_weight": centred(streams_of[12], (D, FF), D ** -0.5, 0.1875, ((0, 8), (1, 4))),
        "down_weight": centred(streams_of[13], (D, FF), FF ** -0.5, 0.09375, ((0, 8), (1, 4))),
    }


@jax.custom_vjp
def low(v):
    return lax.optimization_barrier(v.astype(jnp.bfloat16)).astype(jnp.float32)

@jax.custom_vjp
def low_back(v):
    return v

def low_keep(v):
    return (low(v), None)

def low_pass(kept, grad):
    return (grad,)

def back_keep(v):
    return (v, None)

def back_low(kept, grad):
    return (low(grad),)
low.defvjp(low_keep, low_pass)
low_back.defvjp(back_keep, back_low)
epsilon = 1e-05
theta_base = 1000000.0
masked_score = -1e+30
highest = lax.Precision.HIGHEST

def product(left, right):
    return jnp.dot(left, right, precision=highest, preferred_element_type=jnp.float32)

def product_back(left, right):
    return lax.dot_general(left, right, (((1,), (1,)), ((), ())), precision=highest, preferred_element_type=jnp.float32)

def row_scale(array_in, scale_gain):
    return array_in * lax.rsqrt(lax.optimization_barrier(jnp.mean(array_in * array_in, axis=-1, keepdims=True)) + epsilon) * scale_gain

def places(segments):
    token_index = lax.broadcasted_iota(jnp.int32, segments.shape, 1)
    previous = jnp.concatenate([segments[:, :1] - 1, segments[:, :-1]], axis=1)
    doc_first = lax.cummax(jnp.where(segments != previous, token_index, 0), axis=1)
    return token_index - doc_first

def rotary(segments, head_dim):
    half_dim = head_dim // 2
    frequency = theta_base ** (-2.0 * jnp.arange(half_dim, dtype=jnp.float32) / head_dim)
    angles = places(segments).astype(jnp.float32)[..., None] * frequency
    return (jnp.cos(angles)[:, :, None, :], jnp.sin(angles)[:, :, None, :])

def rotate(array_in, cosine_table, sine_table):
    half_dim = array_in.shape[-1] // 2
    first_half = array_in[..., :half_dim]
    second_half = array_in[..., half_dim:]
    return jnp.concatenate([first_half * cosine_table - second_half * sine_table, second_half * cosine_table + first_half * sine_table], axis=-1)

def attend(operands):
    queries, key_rot, values, segment = operands
    length, kv_heads, head_dim = key_rot.shape
    grouped = queries.reshape(length, kv_heads, -1, head_dim)
    raw_scores = jnp.einsum('qkgd,skd->kgqs', grouped, key_rot, precision=highest)
    scores = low_back(raw_scores * head_dim ** (-0.5))
    row_index = lax.broadcasted_iota(jnp.int32, (length, length), 0)
    col_index = lax.broadcasted_iota(jnp.int32, (length, length), 1)
    allowed = (segment[:, None] == segment[None, :]) & (row_index >= col_index)
    scores = jnp.where(allowed, scores, masked_score)
    row_top = lax.optimization_barrier(jnp.max(scores, axis=-1, keepdims=True))
    exponent = jnp.exp(scores - row_top)
    probability = low(exponent / lax.optimization_barrier(jnp.sum(exponent, axis=-1, keepdims=True)))
    context = jnp.einsum('kgqs,skd->qkgd', probability, values, precision=highest)
    return context.reshape(length, -1)

def forward(params, inputs, segments, cosine_table, sine_table):
    gain_one, query_full, key_full, value_full, gain_query, gain_key, out_full, gain_two, gate_full, up_full, down_full = params
    seq_count, length = segments.shape
    head_dim = gain_query.shape[0]
    normed_one = low(row_scale(inputs, gain_one))
    queries = low_back(product(normed_one, query_full)).reshape(seq_count, length, -1, head_dim)
    keys_raw = low_back(product(normed_one, key_full)).reshape(seq_count, length, -1, head_dim)
    values = low_back(low(product(normed_one, value_full))).reshape(seq_count, length, -1, head_dim)
    query_rot = low(rotate(row_scale(queries, gain_query), cosine_table, sine_table))
    key_rot = low(rotate(row_scale(keys_raw, gain_key), cosine_table, sine_table))
    context = lax.map(jax.checkpoint(attend), (query_rot, key_rot, values, segments))
    context = low_back(low(context.reshape(seq_count * length, -1)))
    mid = inputs + low_back(product_back(context, out_full))
    normed_two = low(row_scale(mid, gain_two))
    gate_pre = low_back(product(normed_two, gate_full))
    up_pre = low_back(product(normed_two, up_full))
    hidden = low(gate_pre * jax.nn.sigmoid(gate_pre) * up_pre)
    return mid + low_back(product_back(hidden, down_full))

def reference(tokens, segments, cotangent, attn_gain, q_weight, k_weight, v_weight, query_gain, key_gain, o_weight, ffn_gain, gate_weight, up_weight, down_weight):
    params = tuple((piece.astype(jnp.float32) for piece in (attn_gain, q_weight, k_weight, v_weight, query_gain, key_gain, o_weight, ffn_gain, gate_weight, up_weight, down_weight)))
    block_count = SEQS // SEQ_DP
    inputs = tokens.astype(jnp.float32).reshape(block_count, SEQ_DP * LEN, D)
    backs = cotangent.astype(jnp.float32).reshape(block_count, SEQ_DP * LEN, D)
    groups = segments.reshape(block_count, SEQ_DP, LEN)

    def block_step(totals, operands):
        token_rows, back_rows, seg_rows = operands
        cosine_table, sine_table = rotary(seg_rows, HD)

        def apply_block(weights, rows_in):
            return forward(weights, rows_in, seg_rows, cosine_table, sine_table)
        result, pullback = jax.vjp(apply_block, params, token_rows)
        gradients, row_grads = pullback(back_rows)
        totals = jax.tree.map(jnp.add, totals, gradients)
        return (totals, (result.astype(jnp.bfloat16), row_grads.astype(jnp.bfloat16)))
    zero_grads = tuple((jnp.zeros_like(piece) for piece in params))
    totals, (results, row_grads) = lax.scan(block_step, zero_grads, (inputs, backs, groups))
    return (results.reshape(TOKENS, D), row_grads.reshape(TOKENS, D), totals[0], totals[1], totals[2], totals[3], totals[4], totals[5], totals[6], totals[7], totals[8], totals[9], totals[10])
```

```python
import functools

import jax
import jax.numpy as jnp
from jax import lax
from jax.experimental import pallas as pl
from jax.experimental.pallas import tpu as pltpu
from jax.sharding import Mesh, PartitionSpec as P

epsilon = 1e-05
theta_base = 1000000.0
bf16 = jnp.bfloat16
f32 = jnp.float32
tile = 256
span = 512


def dot(left, right, left_dim, right_dim):
    return lax.dot_general(
        left, right, (((left_dim,), (right_dim,)), ((), ())), preferred_element_type=f32
    )


def group_sum(value, ones):
    high = value.astype(bf16)
    low = (value - high.astype(f32)).astype(bf16)
    return dot(high, ones, 1, 0) + dot(low, ones, 1, 0)


def ones_by_head(lanes, head):
    row = lax.broadcasted_iota(jnp.int32, (lanes, lanes), 0) // head
    col = lax.broadcasted_iota(jnp.int32, (lanes, lanes), 1) // head
    return jnp.where(row == col, 1.0, 0.0).astype(bf16)


def half_swap(value, head):
    lanes = value.shape[-1]
    lane = lax.broadcasted_iota(jnp.int32, value.shape, 1) % head
    return jnp.where(
        lane < head // 2,
        pltpu.roll(value, lanes - head // 2, 1),
        pltpu.roll(value, head // 2, 1),
    )


def head_norm(raw, ones, head):
    root = lax.rsqrt(group_sum(raw * raw, ones) * (1.0 / head) + epsilon)
    return raw * root, root


def split_block(block, head):
    lanes = 2 * head
    queries = block[:, :lanes]
    both = block[:, lanes:]
    other = pltpu.roll(both, head, 1)
    first = lax.broadcasted_iota(jnp.int32, both.shape, 1) < head
    keys = jnp.where(first, both, other)
    values = jnp.where(first, other, both)
    return queries, keys, values


def stack_heads(block, head):
    first = lax.broadcasted_iota(jnp.int32, block.shape, 1) < head
    zero = jnp.zeros_like(block)
    return jnp.concatenate([jnp.where(first, block, zero), jnp.where(first, zero, block)], axis=0)


def merge_heads(stacked, head):
    half = stacked.shape[0] // 2
    first = lax.broadcasted_iota(jnp.int32, (half, stacked.shape[1]), 1) < head
    return jnp.where(first, stacked[:half], stacked[half:])


def attend_kernel(head, qkv_ref, cos_ref, sin_ref, seg_col, seg_row, gain_ref, ctx_ref, q_s, k_s, v_s):
    length = qkv_ref.shape[0]
    lanes = 2 * head
    ones = ones_by_head(lanes, head)
    queries, keys, values = split_block(qkv_ref[...], head)
    cosine, sine = cos_ref[...], sin_ref[...]

    def rotated(raw, gain):
        hat, _ = head_norm(raw, ones, head)
        scaled = hat * gain
        return (scaled * cosine + half_swap(scaled, head) * sine).astype(bf16)

    q_s[...] = rotated(queries, gain_ref[0:1, :]) * jnp.asarray(head**-0.5, bf16)
    k_s[...] = rotated(keys, gain_ref[1:2, :])
    v_s[...] = values.astype(bf16)
    for top in range(0, length, tile):
        low, high = max(0, top - span), top + tile
        stacked = stack_heads(q_s[top:high, :], head)
        scores = dot(stacked, k_s[low:high, :], 1, 1)
        row = lax.broadcasted_iota(jnp.int32, (tile, high - low), 0) + top
        col = lax.broadcasted_iota(jnp.int32, (tile, high - low), 1) + low
        allowed = (seg_col[top:high, 0:1] == seg_row[0:1, low:high]) & (row >= col)
        allowed = jnp.concatenate([allowed, allowed], axis=0)
        exponent = jnp.where(allowed, jnp.exp(scores), 0.0)
        total = jnp.sum(exponent, axis=1, keepdims=True)
        mixed = dot(exponent.astype(bf16), v_s[low:high, :], 1, 0) / total
        ctx_ref[top:high, :] = merge_heads(mixed, head).astype(bf16)


def attend(qkv, cosine, sine, seg_col, seg_row, gains, head):
    length, width = qkv.shape
    groups = width // (4 * head)
    lanes = 2 * head
    whole = lambda shape: pl.BlockSpec(shape, lambda j: (0, 0))
    return pl.pallas_call(
        functools.partial(attend_kernel, head),
        grid=(groups,),
        in_specs=[
            pl.BlockSpec((length, 2 * lanes), lambda j: (0, j)),
            whole((length, lanes)),
            whole((length, lanes)),
            whole((length, 1)),
            whole((1, length)),
            whole((8, lanes)),
        ],
        out_specs=pl.BlockSpec((length, lanes), lambda j: (0, j)),
        out_shape=jax.ShapeDtypeStruct((length, groups * lanes), bf16),
        scratch_shapes=[pltpu.VMEM((length, lanes), bf16)] * 3,
        compiler_params=pltpu.CompilerParams(vmem_limit_bytes=40 * 2**20),
        cost_estimate=pl.CostEstimate(flops=12 * 10**9, bytes_accessed=8 * 10**6, transcendentals=0),
        name="attend",
    )(qkv, cosine, sine, seg_col, seg_row, gains)


def attend_back_kernel(
    head, qkv_ref, cos_ref, sin_ref, seg_col, seg_row, gain_ref, do_ref, out_ref, sums_ref,
    q_s, k_s, v_s, dk_s, dv_s, dq_s,
):
    length = qkv_ref.shape[0]
    lanes = 2 * head
    ones = ones_by_head(lanes, head)
    queries, keys, values = split_block(qkv_ref[...], head)
    cosine, sine = cos_ref[...], sin_ref[...]

    def rotated(raw, gain):
        hat, _ = head_norm(raw, ones, head)
        scaled = hat * gain
        return (scaled * cosine + half_swap(scaled, head) * sine).astype(bf16)

    scale = jnp.asarray(head**-0.5, bf16)
    q_s[...] = rotated(queries, gain_ref[0:1, :]) * scale
    k_s[...] = rotated(keys, gain_ref[1:2, :])
    v_s[...] = values.astype(bf16)
    dk_s[...] = jnp.zeros_like(dk_s)
    dv_s[...] = jnp.zeros_like(dv_s)
    for top in range(0, length, tile):
        low, high = max(0, top - span), top + tile
        stacked = stack_heads(q_s[top:high, :], head)
        grads = stack_heads(do_ref[top:high, :], head)
        near_k, near_v = k_s[low:high, :], v_s[low:high, :]
        scores = dot(near_k, stacked, 1, 1)
        col = lax.broadcasted_iota(jnp.int32, (high - low, tile), 0) + low
        row = lax.broadcasted_iota(jnp.int32, (high - low, tile), 1) + top
        allowed = (seg_col[low:high, 0:1] == seg_row[0:1, top:high]) & (row >= col)
        allowed = jnp.concatenate([allowed, allowed], axis=1)
        exponent = jnp.where(allowed, jnp.exp(scores), 0.0)
        probs = exponent * (1.0 / jnp.sum(exponent, axis=0, keepdims=True))
        grad_probs = dot(near_v, grads, 1, 1)
        weighted = probs * grad_probs
        delta = jnp.sum(weighted, axis=0, keepdims=True)
        grad_scores = (weighted - probs * delta).astype(bf16)
        dv_s[low:high, :] += dot(probs.astype(bf16), grads, 1, 0)
        dk_s[low:high, :] += dot(grad_scores, stacked, 1, 0)
        dq_s[top:high, :] = merge_heads(dot(grad_scores, near_k, 0, 0), head) * head**-0.5

    def back(raw, gain, grad):
        hat, root = head_norm(raw, ones, head)
        normed = grad * cosine - half_swap(grad, head) * sine
        gain_part = jnp.sum(normed * hat, axis=0, keepdims=True)
        scaled = normed * gain
        mean = group_sum(scaled * hat, ones) * (1.0 / head)
        return root * (scaled - hat * mean), gain_part

    grad_q, q_sum = back(queries, gain_ref[0:1, :], dq_s[...])
    folded_k = dk_s[...] + pltpu.roll(dk_s[...], head, 1)
    grad_k, k_sum = back(keys, gain_ref[1:2, :], folded_k)
    folded_v = dv_s[...] + pltpu.roll(dv_s[...], head, 1)
    first = lax.broadcasted_iota(jnp.int32, (length, lanes), 1) < head
    out_ref[:, :lanes] = grad_q.astype(bf16)
    out_ref[:, lanes:] = jnp.where(first, grad_k, folded_v).astype(bf16)
    which = lax.broadcasted_iota(jnp.int32, sums_ref.shape, 0)
    sums_ref[...] = jnp.where(which == 0, q_sum, jnp.where(which == 1, k_sum, 0.0))


def attend_back(qkv, cosine, sine, seg_col, seg_row, gains, grad_context, head):
    length, width = qkv.shape
    groups = width // (4 * head)
    lanes = 2 * head
    whole = lambda shape: pl.BlockSpec(shape, lambda j: (0, 0))
    return pl.pallas_call(
        functools.partial(attend_back_kernel, head),
        grid=(groups,),
        in_specs=[
            pl.BlockSpec((length, 2 * lanes), lambda j: (0, j)),
            whole((length, lanes)),
            whole((length, lanes)),
            whole((length, 1)),
            whole((1, length)),
            whole((8, lanes)),
            pl.BlockSpec((length, lanes), lambda j: (0, j)),
        ],
        out_specs=(
            pl.BlockSpec((length, 2 * lanes), lambda j: (0, j)),
            pl.BlockSpec((8, lanes), lambda j: (j, 0)),
        ),
        out_shape=(
            jax.ShapeDtypeStruct((length, width), bf16),
            jax.ShapeDtypeStruct((8 * groups, lanes), f32),
        ),
        scratch_shapes=[pltpu.VMEM((length, lanes), bf16)] * 3 + [pltpu.VMEM((length, lanes), f32)] * 3,
        compiler_params=pltpu.CompilerParams(vmem_limit_bytes=48 * 2**20),
        cost_estimate=pl.CostEstimate(flops=30 * 10**9, bytes_accessed=10 * 10**6, transcendentals=0),
        name="attend_back",
    )(qkv, cosine, sine, seg_col, seg_row, gains, grad_context)


def ffn_kernel(w_ref, rows_ref, cot_ref, hid_ref, gate_ref, up_ref):
    rows, cot = rows_ref[...], cot_ref[...]
    gate = dot(w_ref[0], rows, 1, 1)
    up = dot(w_ref[1], rows, 1, 1)
    back = dot(w_ref[2], cot, 1, 1)
    sig = 1.0 / (1.0 + jnp.exp(-gate))
    act = gate * sig
    hid_ref[...] = (act * up).astype(bf16)
    gate_ref[...] = (back * up * (sig + act * (1.0 - sig))).astype(bf16)
    up_ref[...] = (back * act).astype(bf16)


def ffn_hidden(weights, rows, cot):
    _, hidden, width = weights.shape
    count = rows.shape[0]
    h_tile = 384 if hidden % 384 == 0 else hidden
    t_tile = 512
    out = jax.ShapeDtypeStruct((hidden, count), bf16)
    return pl.pallas_call(
        ffn_kernel,
        grid=(hidden // h_tile, count // t_tile),
        in_specs=[
            pl.BlockSpec((3, h_tile, width), lambda i, j: (0, i, 0)),
            pl.BlockSpec((t_tile, width), lambda i, j: (j, 0)),
            pl.BlockSpec((t_tile, width), lambda i, j: (j, 0)),
        ],
        out_specs=[pl.BlockSpec((h_tile, t_tile), lambda i, j: (i, j))] * 3,
        out_shape=[out] * 3,
        compiler_params=pltpu.CompilerParams(vmem_limit_bytes=40 * 2**20),
        cost_estimate=pl.CostEstimate(
            flops=6 * hidden * count * width, bytes_accessed=30 * 10**6, transcendentals=hidden * count
        ),
        name="ffn_hidden",
    )(weights, rows, cot)


def ring(size):
    return [(i, (i + 1) % size) for i in range(size)]


def swap(value, axis):
    return lax.ppermute(value, axis, [(0, 1), (1, 0)])


def gather_parts(value, axis, size):
    at = lax.axis_index(axis)
    if size > 4:
        full = lax.all_gather(value, axis, axis=0)
        return [(i, full[i]) for i in range(size)]
    parts = [(at, value)]
    for step in range(1, size):
        value = lax.ppermute(value, axis, ring(size))
        parts.append(((at - step) % size, value))
    return parts


def assemble(shape, blocks):
    full = jnp.zeros(shape, bf16)
    for start, value in blocks:
        full = lax.dynamic_update_slice(full, value, start)
    return full


def by_index(index, first, second, axis):
    return jnp.where(
        index == 0,
        jnp.concatenate([first, second], axis=axis),
        jnp.concatenate([second, first], axis=axis),
    )


def lane_block(value, index, width):
    start = [0] * (value.ndim - 1) + [index * width]
    return lax.dynamic_slice(value, start, (*value.shape[:-1], width))


def plus(left, right):
    return left.astype(f32) + right.astype(f32)


def scatter_ring(pick, axis, size):
    total = pick(1) if size > 1 else pick(0)
    for step in range(size - 1):
        arrived = lax.ppermute(total.astype(bf16), axis, ring(size))
        total = plus(arrived, pick((step + 2) % size))
    return total


def scatter_axis(block_of, axis, size):
    at = lax.axis_index(axis)
    if size > 4:
        stacked = jnp.stack([block_of(i) for i in range(size)]).astype(bf16)
        return lax.psum_scatter(stacked, axis, scatter_dimension=0, tiled=False).astype(f32)
    return scatter_ring(lambda i: block_of((at - i) % size), axis, size)


def shards(
    sizes,
    tokens,
    segments,
    cotangent,
    attn_gain,
    q_weight,
    k_weight,
    v_weight,
    query_gain,
    key_gain,
    o_weight,
    ffn_gain,
    gate_weight,
    up_weight,
    down_weight,
):
    y_size, x_size, c_size, z_size = sizes
    y, x, c, z = (lax.axis_index(name) for name in "yxcz")
    own_rows, width = tokens.shape
    part = q_weight.shape[0]
    parts = width // part
    head = query_gain.shape[0] * parts
    gain_part = query_gain.shape[0]
    seq_count, length = segments.shape

    pairs = []
    for low in range(0, z_size, 2):
        pairs += [(z_size + low, low + 1), (low + 1, z_size + low)]
    trades = (c + z) % 2 == 1

    def trade(value):
        return jnp.where(trades, lax.ppermute(value, ("c", "z"), pairs), value)

    qt, kt, vt, ot = q_weight.T, k_weight.T, v_weight.T, o_weight.T
    q_rows, k_rows = qt.shape[0] // 2, kt.shape[0] // 2
    gain_rows = jnp.concatenate(
        [attn_gain[None], ffn_gain[None]]
        + [jnp.pad(g, (0, part - gain_part))[None] for g in (query_gain, key_gain)]
        + [jnp.zeros((12, part), bf16)],
        axis=0,
    )
    qkv_pack = jnp.concatenate(
        [v.reshape(2, -1, part) for v in (qt, kt, vt)]
        + [jnp.broadcast_to(gain_rows, (2, 16, part))],
        axis=1,
    )
    o_pack = ot.reshape(2, q_rows, part)

    def core_join(pack):
        mine = lax.dynamic_index_in_dim(pack, c, 0, keepdims=False)
        other = lax.dynamic_index_in_dim(pack, 1 - c, 0, keepdims=False)
        return by_index(c, mine, swap(other, "c"), -1)

    qkv_own = core_join(qkv_pack)
    o_own = core_join(o_pack)
    qkv_rows = q_rows + 2 * k_rows
    qkv_block, o_block, gain_block = [], [], []
    for slot, (_, piece) in enumerate(gather_parts(qkv_own[:qkv_rows], "z", z_size)):
        if slot == 0:
            piece = qkv_own
        for y_at, y_piece in gather_parts(piece, "y", y_size):
            for x_at, x_piece in gather_parts(y_piece, "x", x_size):
                lane = (y_at * x_size + x_at) * c_size * part
                if slot == 0:
                    gain_block.append(((0, lane), x_piece[qkv_rows:]))
                    x_piece = x_piece[:qkv_rows]
                qkv_block.append(((slot * qkv_rows, lane), x_piece))
    for slot, (_, piece) in enumerate(gather_parts(o_own, "z", z_size)):
        for y_at, y_piece in gather_parts(piece, "y", y_size):
            for x_at, x_piece in gather_parts(y_piece, "x", x_size):
                o_block.append(((slot * q_rows, (y_at * x_size + x_at) * c_size * part), x_piece))
    qkv_full = assemble((z_size * qkv_rows, width), qkv_block)
    o_full = assemble((z_size * q_rows, width), o_block)
    gains = assemble((16, width), gain_block).astype(f32)
    gain_one, gain_two = gains[0:1], gains[1:2]
    gain_query, gain_key = (
        gains[i].reshape(parts, part)[:, :gain_part].reshape(1, head) for i in (2, 3)
    )
    head_gains = jnp.concatenate(
        [jnp.tile(gain_query, (1, 2)), jnp.tile(gain_key, (1, 2)), jnp.zeros((6, 2 * head), f32)], axis=0
    )

    sub = gate_weight.shape[1] // (x_size * c_size)
    ffn_pack = jnp.stack([gate_weight.T, up_weight.T, down_weight.T]).reshape(
        3, x_size, c_size, sub, part
    )
    mine = lax.dynamic_index_in_dim(ffn_pack, c, 2, keepdims=False)
    other = lax.dynamic_index_in_dim(ffn_pack, 1 - c, 2, keepdims=False)
    ffn_pack = by_index(c, mine, swap(other, "c"), -1)
    mine = lax.dynamic_index_in_dim(ffn_pack, x, 1, keepdims=False)
    other = lax.dynamic_index_in_dim(ffn_pack, 1 - x, 1, keepdims=False)
    ffn_own = by_index(x, mine, swap(other, "x"), -1)
    ffn_block = []
    quad = x_size * c_size * part
    for slot, (_, piece) in enumerate(gather_parts(ffn_own, "z", z_size)):
        for y_at, y_piece in gather_parts(piece, "y", y_size):
            ffn_block.append(((0, slot * sub, y_at * quad), y_piece))
    ffn_full = assemble((3, z_size * sub, width), ffn_block)

    tokens = trade(tokens)
    cotangent = trade(cotangent)
    other_segments = swap(segments, "c")
    segment = lax.dynamic_index_in_dim(
        jnp.where(c == z % 2, segments, other_segments), z // 2, 0, keepdims=False
    )
    place = lax.broadcasted_iota(jnp.int32, (length,), 0) - jnp.sum(
        (segment[None, :] < segment[:, None]).astype(jnp.int32), axis=1
    )
    frequency = theta_base ** (-2.0 * jnp.arange(head // 2, dtype=f32) / head)
    angles = place.astype(f32)[:, None] * frequency
    cosine, sine = jnp.cos(angles), jnp.sin(angles)
    cosine = jnp.concatenate([cosine] * 4, axis=1)
    sine = jnp.concatenate([-sine, sine] * 2, axis=1)
    seg_col, seg_row = segment[:, None], segment[None, :]

    inputs = tokens.astype(f32)
    root_one = lax.rsqrt(jnp.mean(inputs * inputs, axis=-1, keepdims=True) + epsilon)
    hat_one = inputs * root_one
    normed_own = (hat_one * gain_one).astype(bf16)
    normed_one = by_index(c, normed_own, swap(normed_own, "c"), 0)
    qkv = dot(normed_one, qkv_full, 1, 1)
    context = attend(qkv, cosine, sine, seg_col, seg_row, head_gains, head)

    def half_rows(value, index):
        return lax.dynamic_slice_in_dim(value, index * own_rows, own_rows, 0)

    def core_reduce(left, right, right_dim):
        sent = dot(half_rows(left, 1 - c), right, 1, right_dim).astype(bf16)
        kept = dot(half_rows(left, c), right, 1, right_dim)
        return kept + swap(sent, "c").astype(f32)

    mid = inputs + core_reduce(context, o_full, 0)
    root_two = lax.rsqrt(jnp.mean(mid * mid, axis=-1, keepdims=True) + epsilon)
    hat_two = mid * root_two
    normed_two = (hat_two * gain_two).astype(bf16)

    def spread(value):
        across = swap(value, "x")
        return jnp.concatenate([value, swap(value, "c"), across, swap(across, "c")], axis=0)

    def collect(value):
        quarter = [value[i * own_rows : (i + 1) * own_rows] for i in range(4)]
        across = plus(quarter[2], swap(quarter[3], "c")).astype(bf16)
        return plus(quarter[0], swap(quarter[1], "c")) + swap(across, "x").astype(f32)

    rows_two = spread(normed_two)
    back_rows = spread(cotangent)
    hidden, gate_grad, up_grad = ffn_hidden(ffn_full, rows_two, back_rows)
    ffn_back = (dot(gate_grad, ffn_full[0], 0, 0) + dot(up_grad, ffn_full[1], 0, 0)).astype(bf16)
    ffn_part = dot(hidden, ffn_full[2], 0, 0).astype(bf16)
    grad_normed_two = collect(ffn_back)
    output = (mid + collect(ffn_part)).astype(bf16)
    wgrads = jnp.stack(
        [
            dot(gate_grad, rows_two, 1, 0).astype(bf16),
            dot(up_grad, rows_two, 1, 0).astype(bf16),
            dot(hidden, back_rows, 1, 0).astype(bf16),
        ]
    )
    wgrads = scatter_axis(lambda i: lane_block(wgrads, i, quad), "y", y_size)
    wgrads = wgrads.astype(bf16)
    wgrads = scatter_ring(lambda i: wgrads[:, i * sub : (i + 1) * sub], "z", z_size).astype(bf16)
    kept = lane_block(wgrads, x, c_size * part)
    sent = swap(lane_block(wgrads, 1 - x, c_size * part), "x")
    wgrads = jnp.where(x == 0, jnp.stack([kept, sent], 1), jnp.stack([sent, kept], 1))
    kept = lane_block(wgrads, c, part)
    sent = swap(lane_block(wgrads, 1 - c, part), "c")
    wgrads = jnp.where(c == 0, jnp.stack([kept, sent], 2), jnp.stack([sent, kept], 2))
    wgrads = wgrads.reshape(3, x_size * c_size * sub, part)
    gate_wgrad, up_wgrad, down_wgrad = (wgrads[i].astype(f32).T for i in range(3))

    def norm_back(grad, hat, root):
        return root * (grad - hat * jnp.mean(grad * hat, axis=-1, keepdims=True))

    gain_two_part = jnp.sum(grad_normed_two * hat_two, axis=0)
    grad_mid = cotangent.astype(f32) + norm_back(grad_normed_two * gain_two, hat_two, root_two)

    branch_own = grad_mid.astype(bf16)
    branch = by_index(c, branch_own, swap(branch_own, "c"), 0)
    grad_context = dot(branch, o_full, 1, 1).astype(bf16)
    o_grad = dot(context, branch, 0, 0).astype(bf16)
    grad_qkv, head_sums = attend_back(
        qkv, cosine, sine, seg_col, seg_row, head_gains, grad_context, head
    )
    head_sums = jnp.sum(head_sums.reshape(-1, 8, 2 * head), axis=0)
    gain_query_part = head_sums[0, :head] + head_sums[0, head:]
    gain_key_part = head_sums[1, :head]
    grad_normed_one = core_reduce(grad_qkv, qkv_full, 0)
    qkv_grad = dot(grad_qkv, normed_one, 0, 0).astype(bf16)

    def attn_scatter(value, rows):
        pair = c_size * part
        per_y = []
        for y_at in range(y_size):
            sent = swap(lane_block(value, y_at * x_size + 1 - x, pair), "x")
            per_y.append(plus(lane_block(value, y_at * x_size + x, pair), sent).astype(bf16))
        joined = jnp.stack(per_y)
        value = scatter_axis(
            lambda i: lax.dynamic_index_in_dim(joined, i, 0, keepdims=False), "y", y_size
        ).astype(bf16)
        value = scatter_ring(lambda i: value[i * rows : (i + 1) * rows], "z", z_size).astype(bf16)
        kept = lane_block(value, c, part)
        sent = swap(lane_block(value, 1 - c, part), "c")
        return jnp.where(c == 0, jnp.stack([kept, sent]), jnp.stack([sent, kept])).astype(f32)

    o_wgrad = attn_scatter(o_grad, q_rows).reshape(2 * q_rows, part).T
    qkv_grad = attn_scatter(qkv_grad, qkv_rows)
    q_wgrad = qkv_grad[:, :q_rows].reshape(-1, part).T
    k_wgrad = qkv_grad[:, q_rows : q_rows + k_rows].reshape(-1, part).T
    v_wgrad = qkv_grad[:, q_rows + k_rows :].reshape(-1, part).T

    gain_one_part = jnp.sum(grad_normed_one * hat_one, axis=0)
    tokens_grad = (grad_mid + norm_back(grad_normed_one * gain_one, hat_one, root_one)).astype(bf16)
    sums = lax.psum(
        jnp.concatenate([gain_one_part, gain_two_part, gain_query_part, gain_key_part]),
        ("y", "x", "c", "z"),
    )
    mine = (y * x_size + x) * c_size + c
    gain_one_sum = lax.dynamic_slice(sums, (mine * part,), (part,))
    gain_two_sum = lax.dynamic_slice(sums, (width + mine * part,), (part,))
    gain_query_sum = lax.dynamic_slice(sums, (2 * width + mine * gain_part,), (gain_part,))
    gain_key_sum = lax.dynamic_slice(sums, (2 * width + head + mine * gain_part,), (gain_part,))
    return (
        trade(output),
        trade(tokens_grad),
        gain_one_sum,
        q_wgrad,
        k_wgrad,
        v_wgrad,
        gain_query_sum,
        gain_key_sum,
        o_wgrad,
        gain_two_sum,
        gate_wgrad,
        up_wgrad,
        down_wgrad,
    )


def solution(mesh):
    dp, tp = mesh.devices.shape
    sizes = (dp // 4, 2, 2, tp)
    fine = Mesh(mesh.devices.reshape(sizes), ("y", "x", "c", "z"))
    d = ("y", "x", "c")
    rows, weight, gain = P((*d, "z"), None), P(d, "z"), P(d)
    return jax.shard_map(
        functools.partial(shards, sizes),
        mesh=fine,
        in_specs=(rows, P(d, None), rows, gain, weight, weight, weight, gain, gain, weight, gain)
        + (weight,) * 3,
        out_specs=(rows, rows, gain, weight, weight, weight, gain, gain, weight, gain) + (weight,) * 3,
        check_vma=False,
    )
```

```python
import functools

import jax
import jax.numpy as jnp
from jax import lax
from jax.experimental import pallas as pl
from jax.experimental.pallas import tpu as pltpu
from jax.sharding import Mesh, PartitionSpec as P

epsilon = 1e-05
theta_base = 1000000.0
bf16 = jnp.bfloat16
f32 = jnp.float32
tile = 256
span = 512


def cost(flops):
    return pl.CostEstimate(flops=flops, bytes_accessed=10**6, transcendentals=0)


def dot(left, right, left_dim, right_dim):
    return lax.dot_general(
        left, right, (((left_dim,), (right_dim,)), ((), ())), preferred_element_type=f32
    )


def group_sum(value, ones):
    high = value.astype(bf16)
    low = (value - high.astype(f32)).astype(bf16)
    return dot(high, ones, 1, 0) + dot(low, ones, 1, 0)


def ones_by_head(lanes, head):
    row = lax.broadcasted_iota(jnp.int32, (lanes, lanes), 0) // head
    col = lax.broadcasted_iota(jnp.int32, (lanes, lanes), 1) // head
    return jnp.where(row == col, 1.0, 0.0).astype(bf16)


def half_swap(value, head):
    lanes = value.shape[-1]
    lane = lax.broadcasted_iota(jnp.int32, value.shape, 1) % head
    return jnp.where(
        lane < head // 2,
        pltpu.roll(value, lanes - head // 2, 1),
        pltpu.roll(value, head // 2, 1),
    )


def head_norm(raw, ones, head):
    root = lax.rsqrt(group_sum(raw * raw, ones) * (1.0 / head) + epsilon)
    return raw * root, root


def split_block(block, head):
    lanes = 2 * head
    queries = block[:, :lanes]
    both = block[:, lanes:]
    other = pltpu.roll(both, head, 1)
    first = lax.broadcasted_iota(jnp.int32, both.shape, 1) < head
    keys = jnp.where(first, both, other)
    values = jnp.where(first, other, both)
    return queries, keys, values


def stack_heads(block, head):
    first = lax.broadcasted_iota(jnp.int32, block.shape, 1) < head
    zero = jnp.zeros_like(block)
    return jnp.concatenate([jnp.where(first, block, zero), jnp.where(first, zero, block)], axis=0)


def merge_heads(stacked, head):
    half = stacked.shape[0] // 2
    first = lax.broadcasted_iota(jnp.int32, (half, stacked.shape[1]), 1) < head
    return jnp.where(first, stacked[:half], stacked[half:])


def attend_kernel(head, qkv_ref, cos_ref, sin_ref, seg_col, seg_row, gain_ref, ctx_ref, q_s, k_s, v_s):
    length = qkv_ref.shape[0]
    lanes = 2 * head
    ones = ones_by_head(lanes, head)
    queries, keys, values = split_block(qkv_ref[...], head)
    cosine, sine = cos_ref[...], sin_ref[...]

    def rotated(raw, gain):
        hat, _ = head_norm(raw, ones, head)
        scaled = hat * gain
        return (scaled * cosine + half_swap(scaled, head) * sine).astype(bf16)

    q_s[...] = rotated(queries, gain_ref[0:1, :]) * jnp.asarray(head**-0.5, bf16)
    k_s[...] = rotated(keys, gain_ref[1:2, :])
    v_s[...] = values.astype(bf16)
    for top in range(0, length, tile):
        low, high = max(0, top - span), top + tile
        stacked = stack_heads(q_s[top:high, :], head)
        scores = dot(stacked, k_s[low:high, :], 1, 1)
        row = lax.broadcasted_iota(jnp.int32, (tile, high - low), 0) + top
        col = lax.broadcasted_iota(jnp.int32, (tile, high - low), 1) + low
        allowed = (seg_col[top:high, 0:1] == seg_row[0:1, low:high]) & (row >= col)
        allowed = jnp.concatenate([allowed, allowed], axis=0)
        exponent = jnp.where(allowed, jnp.exp(scores), 0.0)
        total = jnp.sum(exponent, axis=1, keepdims=True)
        mixed = dot(exponent.astype(bf16), v_s[low:high, :], 1, 0) / total
        ctx_ref[top:high, :] = merge_heads(mixed, head).astype(bf16)


def attend(qkv, cosine, sine, seg_col, seg_row, gains, head):
    length, width = qkv.shape
    groups = width // (4 * head)
    lanes = 2 * head
    whole = lambda shape: pl.BlockSpec(shape, lambda j: (0, 0))
    return pl.pallas_call(
        functools.partial(attend_kernel, head),
        grid=(groups,),
        in_specs=[
            pl.BlockSpec((length, 2 * lanes), lambda j: (0, j)),
            whole((length, lanes)),
            whole((length, lanes)),
            whole((length, 1)),
            whole((1, length)),
            whole((8, lanes)),
        ],
        out_specs=pl.BlockSpec((length, lanes), lambda j: (0, j)),
        out_shape=jax.ShapeDtypeStruct((length, groups * lanes), bf16),
        scratch_shapes=[pltpu.VMEM((length, lanes), bf16)] * 3,
        compiler_params=pltpu.CompilerParams(vmem_limit_bytes=40 * 2**20),
        cost_estimate=cost(6 * 10**9),
        name="attend",
    )(qkv, cosine, sine, seg_col, seg_row, gains)


def attend_back_kernel(
    head, qkv_ref, cos_ref, sin_ref, seg_col, seg_row, gain_ref, do_ref, out_ref, sums_ref,
    q_s, k_s, v_s, dk_s, dv_s, dq_s,
):
    length = qkv_ref.shape[0]
    lanes = 2 * head
    ones = ones_by_head(lanes, head)
    queries, keys, values = split_block(qkv_ref[...], head)
    cosine, sine = cos_ref[...], sin_ref[...]

    def rotated(raw, gain):
        hat, _ = head_norm(raw, ones, head)
        scaled = hat * gain
        return (scaled * cosine + half_swap(scaled, head) * sine).astype(bf16)

    scale = jnp.asarray(head**-0.5, bf16)
    q_s[...] = rotated(queries, gain_ref[0:1, :]) * scale
    k_s[...] = rotated(keys, gain_ref[1:2, :])
    v_s[...] = values.astype(bf16)
    dk_s[...] = jnp.zeros_like(dk_s)
    dv_s[...] = jnp.zeros_like(dv_s)
    for top in range(0, length, tile):
        low, high = max(0, top - span), top + tile
        stacked = stack_heads(q_s[top:high, :], head)
        grads = stack_heads(do_ref[top:high, :], head)
        near_k, near_v = k_s[low:high, :], v_s[low:high, :]
        scores = dot(near_k, stacked, 1, 1)
        col = lax.broadcasted_iota(jnp.int32, (high - low, tile), 0) + low
        row = lax.broadcasted_iota(jnp.int32, (high - low, tile), 1) + top
        allowed = (seg_col[low:high, 0:1] == seg_row[0:1, top:high]) & (row >= col)
        allowed = jnp.concatenate([allowed, allowed], axis=1)
        exponent = jnp.where(allowed, jnp.exp(scores), 0.0)
        probs = exponent * (1.0 / jnp.sum(exponent, axis=0, keepdims=True))
        grad_probs = dot(near_v, grads, 1, 1)
        weighted = probs * grad_probs
        delta = jnp.sum(weighted, axis=0, keepdims=True)
        grad_scores = (weighted - probs * delta).astype(bf16)
        dv_s[low:high, :] += dot(probs.astype(bf16), grads, 1, 0)
        dk_s[low:high, :] += dot(grad_scores, stacked, 1, 0)
        dq_s[top:high, :] = merge_heads(dot(grad_scores, near_k, 0, 0), head) * head**-0.5

    def back(raw, gain, grad):
        hat, root = head_norm(raw, ones, head)
        normed = grad * cosine - half_swap(grad, head) * sine
        gain_part = jnp.sum(normed * hat, axis=0, keepdims=True)
        scaled = normed * gain
        mean = group_sum(scaled * hat, ones) * (1.0 / head)
        return root * (scaled - hat * mean), gain_part

    grad_q, q_sum = back(queries, gain_ref[0:1, :], dq_s[...])
    folded_k = dk_s[...] + pltpu.roll(dk_s[...], head, 1)
    grad_k, k_sum = back(keys, gain_ref[1:2, :], folded_k)
    folded_v = dv_s[...] + pltpu.roll(dv_s[...], head, 1)
    first = lax.broadcasted_iota(jnp.int32, (length, lanes), 1) < head
    out_ref[:, :lanes] = grad_q.astype(bf16)
    out_ref[:, lanes:] = jnp.where(first, grad_k, folded_v).astype(bf16)
    which = lax.broadcasted_iota(jnp.int32, sums_ref.shape, 0)
    sums_ref[...] = jnp.where(which == 0, q_sum, jnp.where(which == 1, k_sum, 0.0))


def attend_back(qkv, cosine, sine, seg_col, seg_row, gains, grad_context, head):
    length, width = qkv.shape
    groups = width // (4 * head)
    lanes = 2 * head
    whole = lambda shape: pl.BlockSpec(shape, lambda j: (0, 0))
    return pl.pallas_call(
        functools.partial(attend_back_kernel, head),
        grid=(groups,),
        in_specs=[
            pl.BlockSpec((length, 2 * lanes), lambda j: (0, j)),
            whole((length, lanes)),
            whole((length, lanes)),
            whole((length, 1)),
            whole((1, length)),
            whole((8, lanes)),
            pl.BlockSpec((length, lanes), lambda j: (0, j)),
        ],
        out_specs=(
            pl.BlockSpec((length, 2 * lanes), lambda j: (0, j)),
            pl.BlockSpec((8, lanes), lambda j: (j, 0)),
        ),
        out_shape=(
            jax.ShapeDtypeStruct((length, width), bf16),
            jax.ShapeDtypeStruct((8 * groups, lanes), f32),
        ),
        scratch_shapes=[pltpu.VMEM((length, lanes), bf16)] * 3 + [pltpu.VMEM((length, lanes), f32)] * 3,
        compiler_params=pltpu.CompilerParams(vmem_limit_bytes=48 * 2**20),
        cost_estimate=cost(12 * 10**9),
        name="attend_back",
    )(qkv, cosine, sine, seg_col, seg_row, gains, grad_context)


def pull(pairs, sems, start):
    copies = [pltpu.make_async_copy(s, d, sems.at[start + i]) for i, (s, d) in enumerate(pairs)]
    for copy in copies:
        copy.start()
    return copies


def finish(copies):
    for copy in copies:
        copy.wait()


def halves(which_ref, half):
    first = pl.multiple_of(which_ref[0] * half, half)
    second = pl.multiple_of((1 - which_ref[0]) * half, half)
    return pl.ds(first, half), pl.ds(second, half)


def call_local(kernel, which, arrays, outs, out_spaces, scratch, copies, flops, name, limit=58):
    return pl.pallas_call(
        kernel,
        in_specs=[pl.BlockSpec(memory_space=pltpu.SMEM)] + [pl.BlockSpec(memory_space=pltpu.HBM)] * len(arrays),
        out_specs=[pl.BlockSpec(memory_space=space) for space in out_spaces],
        out_shape=outs,
        scratch_shapes=[*scratch, pltpu.SemaphoreType.DMA((copies,))],
        compiler_params=pltpu.CompilerParams(vmem_limit_bytes=limit * 2**20),
        cost_estimate=cost(flops),
        name=name,
    )(which, *arrays)


class Loads:
    def __init__(self, sems):
        self.sems, self.count, self.open = sems, 0, {}

    def start(self, key, *pairs):
        for source, target in pairs:
            copy = pltpu.make_async_copy(source, target, self.sems.at[self.count])
            copy.start()
            self.open.setdefault(key, []).append(copy)
            self.count += 1

    def wait(self, *keys):
        for key in keys:
            for copy in self.open.pop(key, ()):
                copy.wait()

    def close(self):
        self.wait(*list(self.open))


def load_weights(loads, key, near, far, which_ref, gate_up, down, slots):
    size, half = near[0].shape
    top = 2 * size // 3
    first, second = halves(which_ref, half)
    for i in slots:
        for piece, lanes in ((near[i], first), (far[i], second)):
            if gate_up is not None:
                loads.start((key, i), (piece.at[pl.ds(0, top)], gate_up.at[pl.ds(i * top, top), lanes]))
            if down is not None:
                rest = size - top
                loads.start((key, i), (piece.at[pl.ds(top, rest)], down.at[pl.ds(i * rest, rest), lanes]))


def hidden_step(gate_up, down, rows, cot, gu_s, hid_s, slot, columns, sub):
    both = dot(gate_up[2 * slot * sub : 2 * (slot + 1) * sub, :], rows, 1, 1)
    back = dot(down[slot * sub : (slot + 1) * sub, :], cot, 1, 1)
    gate, up = both[:sub], both[sub:]
    sig = 0.5 * jnp.tanh(0.5 * gate) + 0.5
    act = gate * sig
    base = 2 * slot * sub
    gu_s[base : base + sub, columns] = (back * up * (sig + act * (1.0 - sig))).astype(bf16)
    gu_s[base + sub : base + 2 * sub, columns] = (back * act).astype(bf16)
    hid_s[slot * sub : (slot + 1) * sub, columns] = (act * up).astype(bf16)


def weight_step(loads, which_ref, gu_s, hid_s, rows_s, cot_s, out_s, far_out, near_out, order, sub):
    half = far_out[0].shape[1]
    first, second = halves(which_ref, half)
    for side, lanes, outs in ((0, second, far_out), (1, first, near_out)):
        rows, cots = rows_s[:, lanes], cot_s[:, lanes]
        for s in order:
            out_s[side, s, : 2 * sub] = dot(gu_s[2 * s * sub : 2 * (s + 1) * sub, :], rows, 1, 0).astype(bf16)
            out_s[side, s, 2 * sub :] = dot(hid_s[s * sub : (s + 1) * sub, :], cots, 1, 0).astype(bf16)
            loads.start("out", (out_s.at[side, s], outs[s]))


def take(refs, *counts):
    at, out = 0, []
    for count in counts:
        out.append(refs[at : at + count])
        at += count
    return (*out, refs[at:])


def first_kernel(slots, quarters, order, which_ref, *refs):
    near, far, rows, cots, (gu_out, hid_out), far_out, near_out, rest = take(
        refs, slots, slots, quarters, quarters, 2, slots, slots
    )
    gate_up, down, rows_s, cot_s, gu_s, hid_s, out_s, sems = rest
    sub, count = near[0].shape[0] // 3, rows[0].shape[0]
    loads = Loads(sems)
    for q in range(max(slots, quarters)):
        if q < quarters:
            place = pl.ds(q * count, count)
            loads.start(("rows", q), (rows[q], rows_s.at[place]), (cots[q], cot_s.at[place]))
        if q < slots:
            load_weights(loads, "w", near, far, which_ref, gate_up, down, [q])
    for q in range(quarters):
        columns = slice(q * count, (q + 1) * count)
        loads.wait(("rows", q))
        for s in range(slots):
            loads.wait(("w", s))
            hidden_step(gate_up, down, rows_s[columns, :], cot_s[columns, :], gu_s, hid_s, s, columns, sub)
    loads.start("out", (gu_s, gu_out), (hid_s, hid_out))
    weight_step(loads, which_ref, gu_s, hid_s, rows_s, cot_s, out_s, far_out, near_out, order, sub)
    loads.close()


def ffn_first(which, near, far, rows, cots, order):
    slots, quarters = len(near), len(rows)
    size, half = near[0].shape
    sub, count = size // 3, rows[0].shape[0]
    tokens = quarters * count
    gu, hid = (2 * slots * sub, tokens), (slots * sub, tokens)
    out = call_local(
        functools.partial(first_kernel, slots, quarters, order),
        which,
        [*near, *far, *rows, *cots],
        [jax.ShapeDtypeStruct(v, bf16) for v in (gu, hid)]
        + [jax.ShapeDtypeStruct((size, half), bf16)] * (2 * slots),
        [pl.ANY] * (2 + 2 * slots),
        [
            pltpu.VMEM((2 * slots * sub, 2 * half), bf16),
            pltpu.VMEM((slots * sub, 2 * half), bf16),
            pltpu.VMEM((tokens, 2 * half), bf16),
            pltpu.VMEM((tokens, 2 * half), bf16),
            pltpu.VMEM(gu, bf16),
            pltpu.VMEM(hid, bf16),
            pltpu.VMEM((2, slots, size, half), bf16),
        ],
        2 * quarters + 4 * slots + 2 + 2 * slots,
        8 * slots * size * half * tokens,
        "ffn_first",
    )
    return out[0], out[1], out[2 : 2 + slots], out[2 + slots :]


def second_kernel(slots, quarters, which_ref, *refs):
    near, far, near_0, far_0, rows, cots, (gu_0,), (gu_out, hid_out), outs, rest = take(
        refs, slots, slots, slots, slots, quarters, quarters, 1, 2, quarters
    )
    gate_up, down, gate_up_0, rows_s, cot_s, gu_s, hid_s, gu_0s, out_s, sems = rest
    sub, count = near[0].shape[0] // 3, rows[0].shape[0]
    loads = Loads(sems)
    turn = [(i + quarters // 2) % quarters for i in range(quarters)]
    for i in range(max(slots, quarters)):
        if i < quarters:
            q = turn[i]
            place = pl.ds(q * count, count)
            loads.start(("rows", q), (rows[q], rows_s.at[place]), (cots[q], cot_s.at[place]))
        if i < slots:
            load_weights(loads, "w", near, far, which_ref, gate_up, down, [i])
        if i == slots - 1:
            load_weights(loads, "w0", near_0, far_0, which_ref, gate_up_0, None, range(slots))
            loads.start("g0", (gu_0, gu_0s))
    for q in turn:
        columns = slice(q * count, (q + 1) * count)
        loads.wait(("rows", q))
        for s in range(slots):
            loads.wait(("w", s))
            hidden_step(gate_up, down, rows_s[columns, :], cot_s[columns, :], gu_s, hid_s, s, columns, sub)
        loads.wait("g0", *(("w0", s) for s in range(slots)))
        total = dot(gu_0s[:, columns], gate_up_0[...], 0, 0) + dot(gu_s[:, columns], gate_up[...], 0, 0)
        out_s[q] = total.astype(bf16)
        loads.start("out", (out_s.at[q], outs[q]))
    loads.start("out", (gu_s, gu_out), (hid_s, hid_out))
    loads.close()


def ffn_second(which, near, far, rows, cots, gu_0):
    slots, quarters = len(near) // 2, len(rows)
    size, half = near[0].shape
    sub, count = size // 3, rows[0].shape[0]
    tokens = quarters * count
    gu, hid = (2 * slots * sub, tokens), (slots * sub, tokens)
    out = call_local(
        functools.partial(second_kernel, slots, quarters),
        which,
        [*near[slots:], *far[slots:], *near[:slots], *far[:slots], *rows, *cots, gu_0],
        [jax.ShapeDtypeStruct(v, bf16) for v in (gu, hid)]
        + [jax.ShapeDtypeStruct((count, 2 * half), bf16)] * quarters,
        [pl.ANY] * (2 + quarters),
        [
            pltpu.VMEM((2 * slots * sub, 2 * half), bf16),
            pltpu.VMEM((slots * sub, 2 * half), bf16),
            pltpu.VMEM((2 * slots * sub, 2 * half), bf16),
            pltpu.VMEM((tokens, 2 * half), bf16),
            pltpu.VMEM((tokens, 2 * half), bf16),
            pltpu.VMEM(gu, bf16),
            pltpu.VMEM(hid, bf16),
            pltpu.VMEM(gu, bf16),
            pltpu.VMEM((quarters, count, 2 * half), bf16),
        ],
        3 * quarters + 6 * slots + 3,
        10 * slots * size * half * tokens,
        "ffn_second",
    )
    return out[0], out[1], out[2:]


def third_kernel(slots, quarters, order, which_ref, *refs):
    near, far, rows, cots, (gu, hid, hid_0), far_out, near_out, outs, rest = take(
        refs, 2 * slots, 2 * slots, quarters, quarters, 3, slots, slots, quarters
    )
    down, rows_s, cot_s, gu_s, hid_s, hid_0s, grad_s, out_s, sems = rest
    sub, count = near[0].shape[0] // 3, rows[0].shape[0]
    loads = Loads(sems)
    for q in range(quarters):
        loads.start("rows", (rows[q], rows_s.at[pl.ds(q * count, count)]))
    loads.start("rows", (gu, gu_s))
    for q in range(quarters):
        loads.start("rows", (cots[q], cot_s.at[pl.ds(q * count, count)]))
    loads.start("rows", (hid, hid_s))
    load_weights(loads, "w", near, far, which_ref, None, down, range(2 * slots))
    loads.start("h0", (hid_0, hid_0s))
    loads.wait("rows")
    weight_step(loads, which_ref, gu_s, hid_s, rows_s, cot_s, grad_s, far_out, near_out, order, sub)
    loads.wait("h0", *(("w", s) for s in range(2 * slots)))
    for q in range(quarters):
        columns = slice(q * count, (q + 1) * count)
        total = dot(hid_0s[:, columns], down[: slots * sub, :], 0, 0)
        total = total + dot(hid_s[:, columns], down[slots * sub :, :], 0, 0)
        out_s[q] = total.astype(bf16)
        loads.start("out", (out_s.at[q], outs[q]))
    loads.close()


def ffn_third(which, near, far, rows, cots, gu, hid, hid_0, order):
    slots, quarters = len(near) // 2, len(rows)
    size, half = near[0].shape
    sub, count = size // 3, rows[0].shape[0]
    tokens = quarters * count
    out = call_local(
        functools.partial(third_kernel, slots, quarters, order),
        which,
        [*near, *far, *rows, *cots, gu, hid, hid_0],
        [jax.ShapeDtypeStruct((size, half), bf16)] * (2 * slots)
        + [jax.ShapeDtypeStruct((count, 2 * half), bf16)] * quarters,
        [pl.ANY] * (2 * slots + quarters),
        [
            pltpu.VMEM((2 * slots * sub, 2 * half), bf16),
            pltpu.VMEM((tokens, 2 * half), bf16),
            pltpu.VMEM((tokens, 2 * half), bf16),
            pltpu.VMEM((2 * slots * sub, tokens), bf16),
            pltpu.VMEM((slots * sub, tokens), bf16),
            pltpu.VMEM((slots * sub, tokens), bf16),
            pltpu.VMEM((2, slots, size, half), bf16),
            pltpu.VMEM((quarters, count, 2 * half), bf16),
        ],
        3 * quarters + 4 * slots + 3 + 2 * slots,
        6 * slots * size * half * tokens,
        "ffn_third",
    )
    return out[:slots], out[slots : 2 * slots], out[2 * slots :]


def place_kernel(count, starts_ref, *refs):
    width = refs[0].shape[1]
    sems = refs[-1]
    finish(
        pull(
            [(refs[i], refs[count].at[:, pl.ds(pl.multiple_of(starts_ref[i], width), width)]) for i in range(count)],
            sems,
            0,
        )
    )


def place_lanes(blocks, starts):
    rows, width = blocks[0].shape
    return call_local(
        functools.partial(place_kernel, len(blocks)),
        jnp.stack(starts).astype(jnp.int32),
        blocks,
        [jax.ShapeDtypeStruct((rows, len(blocks) * width), bf16)],
        [pl.ANY],
        [],
        len(blocks),
        10**9,
        "place_lanes",
        4,
    )[0]


def after(value, *earlier):
    return lax.optimization_barrier((value, *earlier))[0]


def ring(size, step=1):
    return [(i, (i + step) % size) for i in range(size)]


class Lanes:
    def __init__(self):
        self.last = {}

    def wait(self, value, lane):
        return after(value, *self.last.get(lane, ())) if lane in self.last else value

    def move(self, value, axes, pairs, lane):
        got = lax.ppermute(self.wait(value, lane), axes, pairs)
        if lane:
            self.last[lane] = (got,)
        return got

    def swap(self, value, axis):
        return self.move(value, axis, [(0, 1), (1, 0)], None if axis == "c" else axis)

    def around(self, values, size, signs, lane):
        held = [self.wait(value, lane) for value in values]
        got = [lax.ppermute(v, "z", ring(size, signs * (i + 1))) for i, v in enumerate(held)]
        self.last[lane] = tuple(got)
        return got


def by_index(index, first, second, axis):
    return jnp.where(
        index == 0,
        jnp.concatenate([first, second], axis=axis),
        jnp.concatenate([second, first], axis=axis),
    )


def lane_block(value, index, width):
    start = [0] * (value.ndim - 1) + [index * width]
    return lax.dynamic_slice(value, start, (*value.shape[:-1], width))


def plus(left, *right):
    total = left.astype(f32)
    for value in right:
        total = total + value.astype(f32)
    return total


def plane_gather(value, sizes, lanes):
    y_size, x_size = sizes[:2]
    y, x = lax.axis_index("y"), lax.axis_index("x")
    if y_size > 2:
        wide = by_index(x, value, lanes.swap(value, "x"), -1)
        wide = lax.all_gather(wide, "y", axis=0)
        return jnp.concatenate([wide[i] for i in range(y_size)], axis=-1)
    width = value.shape[1]
    far = lanes.swap(value, "y")
    blocks = [value, lanes.swap(value, "x"), far, lanes.swap(far, "x")]
    starts = [(a * x_size + b) * width for a in (y, 1 - y) for b in (x, 1 - x)]
    return place_lanes(blocks, starts)


def plane_scatter(value, sizes, pair, lanes):
    y_size, x_size = sizes[:2]
    y, x = lax.axis_index("y"), lax.axis_index("x")
    block = lambda y_at, x_at: lane_block(value, y_at * x_size + x_at, pair)
    if y_size > 2:
        per_y = [plus(block(i, x), lanes.swap(block(i, 1 - x), "x")).astype(bf16) for i in range(y_size)]
        return lax.psum_scatter(jnp.stack(per_y), "y", scatter_dimension=0, tiled=False).astype(f32)
    far = plus(block(1 - y, x), lanes.swap(block(1 - y, 1 - x), "x")).astype(bf16)
    near = lanes.swap(block(y, 1 - x), "x")
    return plus(block(y, x), near, lanes.swap(far, "y"))


def z_scatter(blocks, size, lanes):
    return plus(blocks[0], *lanes.around(blocks[1:], size, -1, "z"))


def shards(
    sizes,
    tokens,
    segments,
    cotangent,
    attn_gain,
    q_weight,
    k_weight,
    v_weight,
    query_gain,
    key_gain,
    o_weight,
    ffn_gain,
    gate_weight,
    up_weight,
    down_weight,
):
    y_size, x_size, c_size, z_size = sizes
    y, x, c, z = (lax.axis_index(name) for name in "yxcz")
    own_rows, width = tokens.shape
    part = q_weight.shape[0]
    parts = width // part
    pair, quad = c_size * part, x_size * c_size * part
    gain_part = query_gain.shape[0]
    head = gain_part * parts
    seq_count, length = segments.shape

    lanes = Lanes()

    pairs = []
    for low in range(0, z_size, 2):
        pairs += [(z_size + low, low + 1), (low + 1, z_size + low)]
    trades = (c + z) % 2 == 1

    def trade(value, lane):
        return jnp.where(trades, lanes.move(value, ("c", "z"), pairs, lane), value)

    tokens = trade(tokens, None)

    qt, kt, vt, ot = q_weight.T, k_weight.T, v_weight.T, o_weight.T
    q_rows, k_rows = qt.shape[0] // 2, kt.shape[0] // 2
    qkv_rows = q_rows + 2 * k_rows
    gain_rows = jnp.concatenate(
        [attn_gain[None], ffn_gain[None]]
        + [jnp.pad(g, (0, part - gain_part))[None] for g in (query_gain, key_gain)]
        + [jnp.zeros((12, part), bf16)],
        axis=0,
    )
    seg_rows = seq_count * length // part
    numbers = segments.astype(bf16).reshape(seg_rows, part)
    pack = jnp.concatenate(
        [v.reshape(2, -1, part) for v in (qt, kt, vt)]
        + [
            jnp.broadcast_to(gain_rows, (2, 16, part)),
            ot.reshape(2, q_rows, part),
            jnp.broadcast_to(numbers, (2, seg_rows, part)),
        ],
        axis=1,
    )
    mine = lax.dynamic_index_in_dim(pack, c, 0, keepdims=False)
    other = lax.dynamic_index_in_dim(pack, 1 - c, 0, keepdims=False)
    got = lanes.swap(other, "c")
    pack_end = qkv_rows + 16 + q_rows
    pack = by_index(c, mine[:pack_end], got[:pack_end], -1)
    other_segments = got[pack_end:].astype(jnp.int32).reshape(seq_count, length)

    sub = gate_weight.shape[1] // (x_size * c_size)
    ffn_pack = jnp.stack([after(v, other).T for v in (gate_weight, up_weight, down_weight)]).reshape(
        3, x_size, c_size, sub, part
    )
    mine = lax.dynamic_index_in_dim(ffn_pack, c, 2, keepdims=False)
    other = lax.dynamic_index_in_dim(ffn_pack, 1 - c, 2, keepdims=False)
    ffn_pack = by_index(c, mine, lanes.swap(other, "c"), -1)
    mine = lax.dynamic_index_in_dim(ffn_pack, x, 1, keepdims=False)
    other = lax.dynamic_index_in_dim(ffn_pack, 1 - x, 1, keepdims=False)
    ffn_own = by_index(x, mine, lanes.swap(other, "x"), -1).reshape(3 * sub, quad)

    qkv_own = pack[:qkv_rows]
    qkv_own = jnp.concatenate(
        [qkv_own, *lanes.around([qkv_own] * (z_size - 1), z_size, 1, "z"), pack[qkv_rows : qkv_rows + 16]],
        axis=0,
    )
    all_tokens = by_index(c, tokens, lanes.swap(tokens, "c"), 0).astype(f32)
    qkv_all = plane_gather(qkv_own, sizes, lanes)
    qkv_full = qkv_all[: z_size * qkv_rows]
    gains = qkv_all[z_size * qkv_rows :].astype(f32)
    gain_one, gain_two = gains[0:1], gains[1:2]
    gain_query, gain_key = (
        gains[i].reshape(parts, part)[:, :gain_part].reshape(1, head) for i in (2, 3)
    )
    head_gains = jnp.concatenate(
        [jnp.tile(gain_query, (1, 2)), jnp.tile(gain_key, (1, 2)), jnp.zeros((6, 2 * head), f32)], axis=0
    )

    half = width // 2
    pieces, wide = [ffn_own], []

    def over_y(piece):
        if y_size > 2:
            full = jnp.concatenate(list(lax.all_gather(piece, "y", axis=0)), axis=-1)
            wide.append((full[:, :half], full[:, half:]))
        else:
            wide.append((piece, lanes.swap(piece, "y")))

    over_y(ffn_own)
    lanes.last["more"] = lanes.last["z"]
    o_own = [pack[qkv_rows + 16 :]]
    for _ in range(1, z_size):
        o_own.append(lanes.move(o_own[-1], "z", ring(z_size), "more"))
    o_full = plane_gather(jnp.concatenate(o_own, axis=0), sizes, lanes)
    cotangent = trade(cotangent, "more")
    for _ in range(1, z_size):
        pieces.append(lanes.move(pieces[-1], "z", ring(z_size), "z"))
        over_y(pieces[-1])
    which = (y if y_size == 2 else y * 0).astype(jnp.int32).reshape(1)
    near, far = [w[0] for w in wide], [w[1] for w in wide]

    segment = lax.dynamic_index_in_dim(
        jnp.where(c == z % 2, segments, other_segments), z // 2, 0, keepdims=False
    )
    place = lax.broadcasted_iota(jnp.int32, (length,), 0) - jnp.sum(
        (segment[None, :] < segment[:, None]).astype(jnp.int32), axis=1
    )
    frequency = theta_base ** (-2.0 * jnp.arange(head // 2, dtype=f32) / head)
    angles = place.astype(f32)[:, None] * frequency
    cosine, sine = jnp.cos(angles), jnp.sin(angles)
    cosine = jnp.concatenate([cosine] * 4, axis=1)
    sine = jnp.concatenate([-sine, sine] * 2, axis=1)
    seg_col, seg_row = segment[:, None], segment[None, :]

    inputs = tokens.astype(f32)
    root_one = lax.rsqrt(jnp.mean(inputs * inputs, axis=-1, keepdims=True) + epsilon)
    hat_one = inputs * root_one
    all_root = lax.rsqrt(jnp.mean(all_tokens * all_tokens, axis=-1, keepdims=True) + epsilon)
    normed_one = (all_tokens * all_root * gain_one).astype(bf16)
    qkv = dot(after(normed_one, pieces[1], wide[0][1]), qkv_full, 1, 1)
    context = attend(qkv, cosine, sine, seg_col, seg_row, head_gains, head)

    def half_rows(value, index):
        return lax.dynamic_slice_in_dim(value, index * own_rows, own_rows, 0)

    def core_reduce(left, right, right_dim):
        sent = dot(half_rows(left, 1 - c), right, 1, right_dim).astype(bf16)
        kept = dot(half_rows(left, c), right, 1, right_dim)
        return kept + lanes.swap(sent, "c").astype(f32)

    def spread(value):
        across = lanes.swap(value, "x")
        return [value, lanes.swap(value, "c"), across, lanes.swap(across, "c")]

    cots = spread(cotangent)
    mid = inputs + core_reduce(after(context, pieces[z_size // 2], wide[1][1]), o_full, 0)
    root_two = lax.rsqrt(jnp.mean(mid * mid, axis=-1, keepdims=True) + epsilon)
    hat_two = mid * root_two
    normed_two = (hat_two * gain_two).astype(bf16)
    rows_two = spread(normed_two)

    count = z_size // 2
    slot_grads, arrived = [None] * z_size, [None] * z_size

    def turn(group):
        return sorted(range(count), key=lambda i: (group * count + i - 1) % z_size)

    def send_gradients(group, sent, kept):
        for i in turn(group):
            slot = group * count + i
            if y_size > 2:
                full = jnp.concatenate([kept[i], sent[i]], axis=1)
                full = jnp.stack([full[:, k * quad : (k + 1) * quad] for k in range(y_size)])
                arrived[slot] = lax.psum_scatter(full, "y", scatter_dimension=0, tiled=False)
                slot_grads[slot] = arrived[slot].astype(f32)
            else:
                arrived[slot] = lanes.swap(sent[i], "y")
                slot_grads[slot] = plus(kept[i], arrived[slot])

    gu_0, hid_0, sent, kept = ffn_first(which, near[:count], far[:count], rows_two, cots, turn(0))
    send_gradients(0, sent, kept)
    gu_1, hid_1, (first, second, third, fourth) = ffn_second(which, near, far, rows_two, cots, gu_0)
    third = plus(third, lanes.swap(fourth, "c")).astype(bf16)
    across = lanes.swap(third, "x")
    second = lanes.swap(second, "c")
    sent, kept, (out_first, out_second, out_third, out_fourth) = ffn_third(
        after(which, third, arrived[1]), near, far, rows_two, cots, gu_1, hid_1, hid_0, turn(1)
    )
    send_gradients(1, sent, kept)
    total = lanes.move(slot_grads[1].astype(bf16), "z", ring(z_size), "z")
    grad_normed_two = after(plus(first, second, across), total, arrived[0])


    def norm_back(grad, hat, root):
        return root * (grad - hat * jnp.mean(grad * hat, axis=-1, keepdims=True))

    gain_two_part = jnp.sum(grad_normed_two * hat_two, axis=0)
    grad_mid = cotangent.astype(f32) + norm_back(grad_normed_two * gain_two, hat_two, root_two)

    branch_own = grad_mid.astype(bf16)
    branch = by_index(c, branch_own, lanes.swap(branch_own, "c"), 0)
    grad_context = dot(branch, o_full, 1, 1).astype(bf16)
    o_grad = dot(after(context, grad_context), branch, 0, 0).astype(bf16)
    grad_qkv, head_sums = attend_back(
        qkv, cosine, sine, seg_col, seg_row, head_gains, after(grad_context, o_grad, arrived[2]), head
    )
    out_third = plus(out_third, lanes.swap(out_fourth, "c")).astype(bf16)
    out_across = lanes.swap(out_third, "x")
    output = (mid + plus(out_first, lanes.swap(out_second, "c"), out_across)).astype(bf16)
    o_part = plane_scatter(o_grad, sizes, pair, lanes).astype(bf16)
    for step in range(1, z_size - 1):
        total = plus(total, slot_grads[step + 1]).astype(bf16)
        total = lanes.move(total, "z", ring(z_size), "z")
        if step == 1:
            grad_qkv = after(grad_qkv, total, arrived[-1])
    total = plus(total, slot_grads[0])

    head_sums = jnp.sum(head_sums.reshape(-1, 8, 2 * head), axis=0)
    gain_query_part = head_sums[0, :head] + head_sums[0, head:]
    gain_key_part = head_sums[1, :head]
    qkv_grad = dot(grad_qkv, normed_one, 0, 0).astype(bf16)
    qkv_part = plane_scatter(qkv_grad, sizes, pair, lanes).astype(bf16)
    grad_normed_one = core_reduce(after(grad_qkv, qkv_grad), qkv_full, 0)

    def core_deal(value):
        kept = lane_block(value, c, part)
        sent = lanes.swap(lane_block(value, 1 - c, part), "c")
        return jnp.where(c == 0, jnp.stack([kept, sent]), jnp.stack([sent, kept]))

    wgrads = total.astype(bf16).reshape(3, sub, quad)
    kept = lane_block(wgrads, x, pair)
    sent = lanes.swap(lane_block(wgrads, 1 - x, pair), "x")
    wgrads = jnp.where(x == 0, jnp.stack([kept, sent], 1), jnp.stack([sent, kept], 1))
    kept = lane_block(wgrads, c, part)
    sent = lanes.swap(lane_block(wgrads, 1 - c, part), "c")
    wgrads = jnp.where(c == 0, jnp.stack([kept, sent], 2), jnp.stack([sent, kept], 2))
    wgrads = wgrads.reshape(3, x_size * c_size * sub, part)
    gate_wgrad, up_wgrad, down_wgrad = (wgrads[i].astype(f32).T for i in range(3))


    value = z_scatter([o_part[i * q_rows : (i + 1) * q_rows] for i in range(z_size)], z_size, lanes)
    o_wgrad = core_deal(value.astype(bf16)).astype(f32).reshape(2 * q_rows, part).T

    gain_one_part = jnp.sum(grad_normed_one * hat_one, axis=0)
    tokens_grad = (grad_mid + norm_back(grad_normed_one * gain_one, hat_one, root_one)).astype(bf16)
    spaced = [
        jnp.pad(v.reshape(parts, gain_part), ((0, 0), (0, part - gain_part))).reshape(1, width)
        for v in (gain_query_part, gain_key_part)
    ]
    gain_sums = jnp.concatenate([gain_one_part[None], gain_two_part[None]] + spaced, axis=0)
    gain_sums = plus(gain_sums, lanes.swap(gain_sums, "c")).astype(bf16)
    gain_sums = plane_scatter(jnp.pad(gain_sums, ((0, 12), (0, 0))), sizes, pair, lanes).astype(bf16)
    value = z_scatter(
        [
            jnp.concatenate([qkv_part[i * qkv_rows : (i + 1) * qkv_rows], gain_sums], axis=0)
            for i in range(z_size)
        ],
        z_size,
        lanes,
    )
    gain_sums = lane_block(value[qkv_rows:], c, part)
    qkv_grad = core_deal(value[:qkv_rows].astype(bf16)).astype(f32)
    q_wgrad = qkv_grad[:, :q_rows].reshape(-1, part).T
    k_wgrad = qkv_grad[:, q_rows : q_rows + k_rows].reshape(-1, part).T
    v_wgrad = qkv_grad[:, q_rows + k_rows :].reshape(-1, part).T
    return (
        trade(output, "more"),
        trade(tokens_grad, "more"),
        gain_sums[0],
        q_wgrad,
        k_wgrad,
        v_wgrad,
        gain_sums[2, :gain_part],
        gain_sums[3, :gain_part],
        o_wgrad,
        gain_sums[1],
        gate_wgrad,
        up_wgrad,
        down_wgrad,
    )


def solution(mesh):
    dp, tp = mesh.devices.shape
    sizes = (dp // 4, 2, 2, tp)
    fine = Mesh(mesh.devices.reshape(sizes), ("y", "x", "c", "z"))
    d = ("y", "x", "c")
    rows, weight, gain = P((*d, "z"), None), P(d, "z"), P(d)
    return jax.shard_map(
        functools.partial(shards, sizes),
        mesh=fine,
        in_specs=(rows, P(d, None), rows, gain, weight, weight, weight, gain, gain, weight, gain)
        + (weight,) * 3,
        out_specs=(rows, rows, gain, weight, weight, weight, gain, gain, weight, gain) + (weight,) * 3,
        check_vma=False,
    )
```

```python
import functools

import jax
import jax.numpy as jnp
from jax import lax
from jax.experimental import pallas as pl
from jax.experimental.pallas import tpu as pltpu
from jax.sharding import Mesh, PartitionSpec as P

epsilon = 1e-05
theta_base = 1000000.0
bf16 = jnp.bfloat16
f32 = jnp.float32
tile = 256
span = 512


def cost(flops):
    return pl.CostEstimate(flops=flops // 1000, bytes_accessed=10**5, transcendentals=0)


def dot(left, right, left_dim, right_dim):
    return lax.dot_general(
        left, right, (((left_dim,), (right_dim,)), ((), ())), preferred_element_type=f32
    )


def group_sum(value, ones):
    high = value.astype(bf16)
    low = (value - high.astype(f32)).astype(bf16)
    return dot(high, ones, 1, 0) + dot(low, ones, 1, 0)


def ones_by_head(lanes, head):
    row = lax.broadcasted_iota(jnp.int32, (lanes, lanes), 0) // head
    col = lax.broadcasted_iota(jnp.int32, (lanes, lanes), 1) // head
    return jnp.where(row == col, 1.0, 0.0).astype(bf16)


def half_swap(value, head):
    lanes = value.shape[-1]
    lane = lax.broadcasted_iota(jnp.int32, value.shape, 1) % head
    return jnp.where(
        lane < head // 2,
        pltpu.roll(value, lanes - head // 2, 1),
        pltpu.roll(value, head // 2, 1),
    )


def head_norm(raw, ones, head):
    root = lax.rsqrt(group_sum(raw * raw, ones) * (1.0 / head) + epsilon)
    return raw * root, root


def split_block(block, head):
    lanes = 2 * head
    queries = block[:, :lanes]
    both = block[:, lanes:]
    other = pltpu.roll(both, head, 1)
    first = lax.broadcasted_iota(jnp.int32, both.shape, 1) < head
    keys = jnp.where(first, both, other)
    values = jnp.where(first, other, both)
    return queries, keys, values


def stack_heads(block, head):
    first = lax.broadcasted_iota(jnp.int32, block.shape, 1) < head
    zero = jnp.zeros_like(block)
    return jnp.concatenate([jnp.where(first, block, zero), jnp.where(first, zero, block)], axis=0)


def merge_heads(stacked, head):
    half = stacked.shape[0] // 2
    first = lax.broadcasted_iota(jnp.int32, (half, stacked.shape[1]), 1) < head
    return jnp.where(first, stacked[:half], stacked[half:])


def attend_kernel(head, qkv_ref, cos_ref, sin_ref, seg_col, seg_row, gain_ref, ctx_ref, q_s, k_s, v_s):
    length = qkv_ref.shape[0]
    lanes = 2 * head
    ones = ones_by_head(lanes, head)
    queries, keys, values = split_block(qkv_ref[...], head)
    cosine, sine = cos_ref[...], sin_ref[...]

    def rotated(raw, gain):
        hat, _ = head_norm(raw, ones, head)
        scaled = hat * gain
        return (scaled * cosine + half_swap(scaled, head) * sine).astype(bf16)

    q_s[...] = rotated(queries, gain_ref[0:1, :]) * jnp.asarray(head**-0.5, bf16)
    k_s[...] = rotated(keys, gain_ref[1:2, :])
    v_s[...] = values.astype(bf16)
    for top in range(0, length, tile):
        low, high = max(0, top - span), top + tile
        stacked = stack_heads(q_s[top:high, :], head)
        scores = dot(stacked, k_s[low:high, :], 1, 1)
        row = lax.broadcasted_iota(jnp.int32, (tile, high - low), 0) + top
        col = lax.broadcasted_iota(jnp.int32, (tile, high - low), 1) + low
        allowed = (seg_col[top:high, 0:1] == seg_row[0:1, low:high]) & (row >= col)
        allowed = jnp.concatenate([allowed, allowed], axis=0)
        exponent = jnp.where(allowed, jnp.exp(scores), 0.0)
        total = jnp.sum(exponent, axis=1, keepdims=True)
        mixed = dot(exponent.astype(bf16), v_s[low:high, :], 1, 0) / total
        ctx_ref[top:high, :] = merge_heads(mixed, head).astype(bf16)


def attend(qkv, cosine, sine, seg_col, seg_row, gains, head, first, groups):
    length = qkv.shape[0]
    lanes = 2 * head
    whole = lambda shape: pl.BlockSpec(shape, lambda j: (0, 0))
    return pl.pallas_call(
        functools.partial(attend_kernel, head),
        grid=(groups,),
        in_specs=[
            pl.BlockSpec((length, 2 * lanes), lambda j: (0, j + first)),
            whole((length, lanes)),
            whole((length, lanes)),
            whole((length, 1)),
            whole((1, length)),
            whole((8, lanes)),
        ],
        out_specs=pl.BlockSpec((length, lanes), lambda j: (0, j)),
        out_shape=jax.ShapeDtypeStruct((length, groups * lanes), bf16),
        scratch_shapes=[pltpu.VMEM((length, lanes), bf16)] * 3,
        compiler_params=pltpu.CompilerParams(vmem_limit_bytes=24 * 2**20),
        cost_estimate=cost(6 * 10**9),
        name="attend",
    )(qkv, cosine, sine, seg_col, seg_row, gains)


def attend_back_kernel(
    head, qkv_ref, cos_ref, sin_ref, seg_col, seg_row, gain_ref, do_ref, out_ref, sums_ref,
    q_s, k_s, v_s, dk_s, dv_s, dq_s,
):
    length = qkv_ref.shape[0]
    lanes = 2 * head
    ones = ones_by_head(lanes, head)
    queries, keys, values = split_block(qkv_ref[...], head)
    cosine, sine = cos_ref[...], sin_ref[...]

    def rotated(raw, gain):
        hat, _ = head_norm(raw, ones, head)
        scaled = hat * gain
        return (scaled * cosine + half_swap(scaled, head) * sine).astype(bf16)

    scale = jnp.asarray(head**-0.5, bf16)
    q_s[...] = rotated(queries, gain_ref[0:1, :]) * scale
    k_s[...] = rotated(keys, gain_ref[1:2, :])
    v_s[...] = values.astype(bf16)
    dk_s[...] = jnp.zeros_like(dk_s)
    dv_s[...] = jnp.zeros_like(dv_s)
    for top in range(0, length, tile):
        low, high = max(0, top - span), top + tile
        stacked = stack_heads(q_s[top:high, :], head)
        grads = stack_heads(do_ref[top:high, :], head)
        near_k, near_v = k_s[low:high, :], v_s[low:high, :]
        scores = dot(near_k, stacked, 1, 1)
        col = lax.broadcasted_iota(jnp.int32, (high - low, tile), 0) + low
        row = lax.broadcasted_iota(jnp.int32, (high - low, tile), 1) + top
        allowed = (seg_col[low:high, 0:1] == seg_row[0:1, top:high]) & (row >= col)
        allowed = jnp.concatenate([allowed, allowed], axis=1)
        exponent = jnp.where(allowed, jnp.exp(scores), 0.0)
        probs = exponent * (1.0 / jnp.sum(exponent, axis=0, keepdims=True))
        grad_probs = dot(near_v, grads, 1, 1)
        weighted = probs * grad_probs
        delta = jnp.sum(weighted, axis=0, keepdims=True)
        grad_scores = (weighted - probs * delta).astype(bf16)
        dv_s[low:high, :] += dot(probs.astype(bf16), grads, 1, 0)
        dk_s[low:high, :] += dot(grad_scores, stacked, 1, 0)
        dq_s[top:high, :] = merge_heads(dot(grad_scores, near_k, 0, 0), head) * head**-0.5

    def back(raw, gain, grad):
        hat, root = head_norm(raw, ones, head)
        normed = grad * cosine - half_swap(grad, head) * sine
        gain_part = jnp.sum(normed * hat, axis=0, keepdims=True)
        scaled = normed * gain
        mean = group_sum(scaled * hat, ones) * (1.0 / head)
        return root * (scaled - hat * mean), gain_part

    grad_q, q_sum = back(queries, gain_ref[0:1, :], dq_s[...])
    folded_k = dk_s[...] + pltpu.roll(dk_s[...], head, 1)
    grad_k, k_sum = back(keys, gain_ref[1:2, :], folded_k)
    folded_v = dv_s[...] + pltpu.roll(dv_s[...], head, 1)
    first = lax.broadcasted_iota(jnp.int32, (length, lanes), 1) < head
    out_ref[:, :lanes] = grad_q.astype(bf16)
    out_ref[:, lanes:] = jnp.where(first, grad_k, folded_v).astype(bf16)
    which = lax.broadcasted_iota(jnp.int32, sums_ref.shape, 0)
    sums_ref[...] = jnp.where(which == 0, q_sum, jnp.where(which == 1, k_sum, 0.0))


def attend_back(qkv, cosine, sine, seg_col, seg_row, gains, grad_context, head, first, groups):
    length = qkv.shape[0]
    lanes = 2 * head
    whole = lambda shape: pl.BlockSpec(shape, lambda j: (0, 0))
    return pl.pallas_call(
        functools.partial(attend_back_kernel, head),
        grid=(groups,),
        in_specs=[
            pl.BlockSpec((length, 2 * lanes), lambda j: (0, j + first)),
            whole((length, lanes)),
            whole((length, lanes)),
            whole((length, 1)),
            whole((1, length)),
            whole((8, lanes)),
            pl.BlockSpec((length, lanes), lambda j: (0, j + first)),
        ],
        out_specs=(
            pl.BlockSpec((length, 2 * lanes), lambda j: (0, j)),
            pl.BlockSpec((8, lanes), lambda j: (j, 0)),
        ),
        out_shape=(
            jax.ShapeDtypeStruct((length, groups * 2 * lanes), bf16),
            jax.ShapeDtypeStruct((8 * groups, lanes), f32),
        ),
        scratch_shapes=[pltpu.VMEM((length, lanes), bf16)] * 3 + [pltpu.VMEM((length, lanes), f32)] * 3,
        compiler_params=pltpu.CompilerParams(vmem_limit_bytes=58 * 2**20),
        cost_estimate=cost(12 * 10**9),
        name="attend_back",
    )(qkv, cosine, sine, seg_col, seg_row, gains, grad_context)


def pull(pairs, sems, start):
    copies = [pltpu.make_async_copy(s, d, sems.at[start + i]) for i, (s, d) in enumerate(pairs)]
    for copy in copies:
        copy.start()
    return copies


def finish(copies):
    for copy in copies:
        copy.wait()


def halves(which_ref, half):
    first = pl.multiple_of(which_ref[0] * half, half)
    second = pl.multiple_of((1 - which_ref[0]) * half, half)
    return pl.ds(first, half), pl.ds(second, half)


def call_local(kernel, which, arrays, outs, out_spaces, scratch, copies, flops, name, limit=58):
    return pl.pallas_call(
        kernel,
        in_specs=[pl.BlockSpec(memory_space=pltpu.SMEM)] + [pl.BlockSpec(memory_space=pltpu.HBM)] * len(arrays),
        out_specs=[pl.BlockSpec(memory_space=space) for space in out_spaces],
        out_shape=outs,
        scratch_shapes=[*scratch, pltpu.SemaphoreType.DMA((copies,))],
        compiler_params=pltpu.CompilerParams(vmem_limit_bytes=limit * 2**20),
        cost_estimate=cost(flops),
        name=name,
    )(which, *arrays)


class Loads:
    def __init__(self, sems):
        self.sems, self.count, self.open = sems, 0, {}

    def start(self, key, *pairs):
        for source, target in pairs:
            copy = pltpu.make_async_copy(source, target, self.sems.at[self.count])
            copy.start()
            self.open.setdefault(key, []).append(copy)
            self.count += 1

    def wait(self, *keys):
        for key in keys:
            for copy in self.open.pop(key, ()):
                copy.wait()

    def close(self):
        self.wait(*list(self.open))


def load_gate_up(loads, key, near, far, which_ref, target, slots):
    size, half = near[0].shape
    top = 2 * size // 3
    for at, i in enumerate(slots):
        for pieces, lanes in zip((near, far), halves(which_ref, half)):
            loads.start((key, at), (pieces[i].at[pl.ds(0, top)], target.at[pl.ds(at * top, top), lanes]))


def load_down(loads, key, near, far, which_ref, target, slots):
    size, half = near[0].shape
    rest = size // 3
    for at, i in enumerate(slots):
        for pieces, lanes in zip((near, far), halves(which_ref, half)):
            loads.start(
                (key, at), (pieces[i].at[pl.ds(size - rest, rest)], target.at[pl.ds(at * rest, rest), lanes])
            )


def hidden_step(gate_up, down, rows, cot, gu_s, hid_s, slot, columns, sub):
    both = dot(gate_up[2 * slot * sub : 2 * (slot + 1) * sub, :], rows, 1, 1)
    back = dot(down[slot * sub : (slot + 1) * sub, :], cot, 1, 1)
    gate, up = both[:sub], both[sub:]
    sig = 0.5 * jnp.tanh(0.5 * gate) + 0.5
    act = gate * sig
    base = 2 * slot * sub
    gu_s[base : base + sub, columns] = (back * up * (sig + act * (1.0 - sig))).astype(bf16)
    gu_s[base + sub : base + 2 * sub, columns] = (back * act).astype(bf16)
    hid_s[slot * sub : (slot + 1) * sub, columns] = (act * up).astype(bf16)


def weight_step(loads, which_ref, gu_s, hid_s, rows_s, cot_s, out_s, far_out, near_out, order, sub):
    size, half = 3 * sub, rows_s.shape[1] // 2
    first, second = halves(which_ref, half)
    for side, lanes, outs in ((0, second, far_out), (1, first, near_out)):
        rows, cots = rows_s[:, lanes], cot_s[:, lanes]
        for at, s in enumerate(order):
            out_s[side, s, : 2 * sub] = dot(gu_s[2 * s * sub : 2 * (s + 1) * sub, :], rows, 1, 0).astype(bf16)
            out_s[side, s, 2 * sub :] = dot(hid_s[s * sub : (s + 1) * sub, :], cots, 1, 0).astype(bf16)
            target = outs[s] if len(outs) > 1 else outs[0].at[pl.ds(at * size, size)]
            loads.start("out", (out_s.at[side, s], target))


def take(refs, *counts):
    at, out = 0, []
    for count in counts:
        out.append(refs[at : at + count])
        at += count
    return (*out, refs[at:])


def first_kernel(slots, quarters, order, which_ref, *refs):
    near, far, rows, cots, (gu_out, hid_out), far_out, near_out, rest = take(
        refs, slots, slots, quarters, quarters, 2, 1, 1
    )
    gate_up, down, rows_s, cot_s, gu_s, hid_s, out_s, sems = rest
    sub, count = near[0].shape[0] // 3, rows[0].shape[0]
    loads = Loads(sems)
    for q in range(max(slots, quarters)):
        if q < quarters:
            place = pl.ds(q * count, count)
            loads.start(("rows", q), (rows[q], rows_s.at[place]), (cots[q], cot_s.at[place]))
        if q == 0:
            load_gate_up(loads, "w", near, far, which_ref, gate_up, range(slots))
            load_down(loads, "w", near, far, which_ref, down, range(slots))
    for q in range(quarters):
        columns = slice(q * count, (q + 1) * count)
        loads.wait(("rows", q))
        for s in range(slots):
            loads.wait(("w", s))
            hidden_step(gate_up, down, rows_s[columns, :], cot_s[columns, :], gu_s, hid_s, s, columns, sub)
    loads.start("out", (gu_s, gu_out), (hid_s, hid_out))
    weight_step(loads, which_ref, gu_s, hid_s, rows_s, cot_s, out_s, far_out, near_out, order, sub)
    loads.close()


def ffn_first(which, near, far, rows, cots, order):
    slots, quarters = len(near), len(rows)
    size, half = near[0].shape
    sub, count = size // 3, rows[0].shape[0]
    tokens = quarters * count
    gu, hid = (2 * slots * sub, tokens), (slots * sub, tokens)
    out = call_local(
        functools.partial(first_kernel, slots, quarters, order),
        which,
        [*near, *far, *rows, *cots],
        [jax.ShapeDtypeStruct(v, bf16) for v in (gu, hid)]
        + [jax.ShapeDtypeStruct((slots * size, half), bf16)] * 2,
        [pl.ANY] * 4,
        [
            pltpu.VMEM((2 * slots * sub, 2 * half), bf16),
            pltpu.VMEM((slots * sub, 2 * half), bf16),
            pltpu.VMEM((tokens, 2 * half), bf16),
            pltpu.VMEM((tokens, 2 * half), bf16),
            pltpu.VMEM(gu, bf16),
            pltpu.VMEM(hid, bf16),
            pltpu.VMEM((2, slots, size, half), bf16),
        ],
        2 * quarters + 4 * slots + 2 + 2 * slots,
        8 * slots * size * half * tokens,
        "ffn_first",
    )
    return out


def second_kernel(slots, quarters, which_ref, *refs):
    near, far, rows, cots, (gu_0,), (gu_out, hid_out), outs, rest = take(
        refs, 2 * slots, 2 * slots, quarters, quarters, 1, 2, quarters
    )
    gate_up, down, gate_up_0, rows_s, cot_s, gu_s, hid_s, gu_0s, out_s, sems = rest
    sub, count = near[0].shape[0] // 3, rows[0].shape[0]
    loads = Loads(sems)
    for q in range(quarters):
        place = pl.ds(q * count, count)
        loads.start(("rows", q), (rows[q], rows_s.at[place]), (cots[q], cot_s.at[place]))
        if q == 0:
            load_gate_up(loads, "w", near, far, which_ref, gate_up, range(slots, 2 * slots))
            load_down(loads, "w", near, far, which_ref, down, range(slots, 2 * slots))
    load_gate_up(loads, "w0", near, far, which_ref, gate_up_0, range(slots))
    loads.start("g0", (gu_0, gu_0s))
    for q in range(quarters):
        columns = slice(q * count, (q + 1) * count)
        loads.wait(("rows", q))
        for s in range(slots):
            loads.wait(("w", s))
            hidden_step(gate_up, down, rows_s[columns, :], cot_s[columns, :], gu_s, hid_s, s, columns, sub)
    loads.start("out", (gu_s, gu_out), (hid_s, hid_out))
    loads.wait("g0", *(("w0", s) for s in range(slots)))
    for q in range(quarters):
        columns = slice(q * count, (q + 1) * count)
        total = dot(gu_0s[:, columns], gate_up_0[...], 0, 0) + dot(gu_s[:, columns], gate_up[...], 0, 0)
        out_s[q] = total.astype(bf16)
        loads.start("out", (out_s.at[q], outs[q]))
    loads.close()


def ffn_second(which, near, far, rows, cots, gu_0):
    slots, quarters = len(near) // 2, len(rows)
    size, half = near[0].shape
    sub, count = size // 3, rows[0].shape[0]
    tokens = quarters * count
    gu, hid = (2 * slots * sub, tokens), (slots * sub, tokens)
    out = call_local(
        functools.partial(second_kernel, slots, quarters),
        which,
        [*near, *far, *rows, *cots, gu_0],
        [jax.ShapeDtypeStruct(v, bf16) for v in (gu, hid)]
        + [jax.ShapeDtypeStruct((count, 2 * half), bf16)] * quarters,
        [pl.ANY] * (2 + quarters),
        [
            pltpu.VMEM((2 * slots * sub, 2 * half), bf16),
            pltpu.VMEM((slots * sub, 2 * half), bf16),
            pltpu.VMEM((2 * slots * sub, 2 * half), bf16),
            pltpu.VMEM((tokens, 2 * half), bf16),
            pltpu.VMEM((tokens, 2 * half), bf16),
            pltpu.VMEM(gu, bf16),
            pltpu.VMEM(hid, bf16),
            pltpu.VMEM(gu, bf16),
            pltpu.VMEM((quarters, count, 2 * half), bf16),
        ],
        3 * quarters + 6 * slots + 3,
        10 * slots * size * half * tokens,
        "ffn_second",
    )
    return out[0], out[1], out[2:]


def third_kernel(slots, quarters, order, which_ref, *refs):
    near, far, rows, cots, (gu, hid, hid_0), far_out, near_out, outs, rest = take(
        refs, 2 * slots, 2 * slots, quarters, quarters, 3, slots, slots, quarters
    )
    down, rows_s, cot_s, gu_s, hid_s, hid_0s, grad_s, out_s, sems = rest
    sub, count = far_out[0].shape[0] // 3, rows[0].shape[0]
    loads = Loads(sems)
    load_down(loads, "w", near, far, which_ref, down, range(2 * slots))
    loads.start("h", (hid_0, hid_0s), (hid, hid_s))
    loads.start("rows", (gu, gu_s))
    for q in range(quarters):
        place = pl.ds(q * count, count)
        loads.start("rows", (rows[q], rows_s.at[place]), (cots[q], cot_s.at[place]))
    loads.wait("h", *(("w", s) for s in range(2 * slots)))
    for q in range(quarters):
        columns = slice(q * count, (q + 1) * count)
        total = dot(hid_0s[:, columns], down[: slots * sub, :], 0, 0)
        total = total + dot(hid_s[:, columns], down[slots * sub :, :], 0, 0)
        out_s[q] = total.astype(bf16)
        loads.start("out", (out_s.at[q], outs[q]))
    loads.wait("rows")
    weight_step(loads, which_ref, gu_s, hid_s, rows_s, cot_s, grad_s, far_out, near_out, order, sub)
    loads.close()


def ffn_third(which, near, far, rows, cots, gu, hid, hid_0, order):
    slots, quarters = len(order), len(rows)
    size, half = near[0].shape
    sub, count = size // 3, rows[0].shape[0]
    tokens = quarters * count
    out = call_local(
        functools.partial(third_kernel, slots, quarters, order),
        which,
        [*near, *far, *rows, *cots, gu, hid, hid_0],
        [jax.ShapeDtypeStruct((size, half), bf16)] * (2 * slots)
        + [jax.ShapeDtypeStruct((count, 2 * half), bf16)] * quarters,
        [pl.ANY] * (2 * slots + quarters),
        [
            pltpu.VMEM((2 * slots * sub, 2 * half), bf16),
            pltpu.VMEM((tokens, 2 * half), bf16),
            pltpu.VMEM((tokens, 2 * half), bf16),
            pltpu.VMEM((2 * slots * sub, tokens), bf16),
            pltpu.VMEM((slots * sub, tokens), bf16),
            pltpu.VMEM((slots * sub, tokens), bf16),
            pltpu.VMEM((2, slots, size, half), bf16),
            pltpu.VMEM((quarters, count, 2 * half), bf16),
        ],
        3 * quarters + 4 * slots + 3 + 2 * slots,
        6 * slots * size * half * tokens,
        "ffn_third",
    )
    return out[:slots], out[slots : 2 * slots], out[2 * slots :]


def qkv_grads_kernel(groups, spaced, starts_ref, grads_0, grads_1, rows, weights, extra_ref, gain_ref, sums_0, sums_1, *refs):
    outs, rest = refs[:4], refs[4:]
    grad_s, rows_s, weight_s, extra_s, gain_s, sums_s, out_s, sems = rest
    size = (grads_0.shape[1] + grads_1.shape[1]) // groups
    width = outs[0].shape[1]
    more = extra_ref.shape[0]
    cut = grads_0.shape[1]
    loads = Loads(sems)
    loads.start("a", (grads_0, grad_s.at[:, pl.ds(0, cut)]), (grads_1, grad_s.at[:, pl.ds(cut, grads_1.shape[1])]))
    loads.start("a", (rows, rows_s))
    loads.start("b", (weights.at[pl.ds(0, groups * size)], weight_s), (extra_ref, extra_s), (gain_ref, gain_s))
    loads.start("b", (sums_0, sums_s.at[pl.ds(0, sums_0.shape[0])]))
    loads.start("b", (sums_1, sums_s.at[pl.ds(sums_0.shape[0], sums_1.shape[0])]))
    loads.wait("a")
    for i in range(4):
        lanes = pl.ds(pl.multiple_of(starts_ref[i], width), width)
        block = dot(grad_s[...], rows_s[:, lanes], 0, 0)
        if i == 0:
            loads.wait("b")
        gain_row = jnp.sum(block * weight_s[:, lanes].astype(f32), axis=0, keepdims=True)
        gain_row = gain_row / gain_s[0:1, lanes]
        row = lax.broadcasted_iota(jnp.int32, (more, width), 0)
        extra = jnp.where(row == 0, gain_row, extra_s[:, lanes])
        if not spaced:
            sums = sums_s[0:8, :]
            for g in range(1, groups):
                sums = sums + sums_s[8 * g : 8 * (g + 1), :]
            head = sums.shape[1] // 2
            query = sums[0:1, :] + pltpu.roll(sums[0:1, :], head, 1)
            lane = lax.broadcasted_iota(jnp.int32, query.shape, 1)
            both = jnp.where(lane < head, query, pltpu.roll(sums[1:2, :], head, 1))
            both = jnp.concatenate([both] * (width // (2 * head)), axis=1)
            extra = jnp.where(row == 2, both, extra)
        extra = extra.astype(bf16)
        for g in range(groups):
            base = g * (size + more)
            out_s[i, base : base + size, :] = block[g * size : (g + 1) * size, :].astype(bf16)
            out_s[i, base + size : base + size + more, :] = extra
        loads.start("out", (out_s.at[i], outs[i]))
    loads.close()


def qkv_grads(starts, grads, rows, weights, extra, gains, sums, groups, spaced):
    count, width = rows.shape
    columns, more = grads[0].shape[1] + grads[1].shape[1], extra.shape[0]
    block = (columns + groups * more, width // 4)
    return call_local(
        functools.partial(qkv_grads_kernel, groups, spaced),
        jnp.stack(starts).astype(jnp.int32),
        [*grads, rows, weights, extra, gains, *sums],
        [jax.ShapeDtypeStruct(block, bf16)] * 4,
        [pl.ANY] * 4,
        [
            pltpu.VMEM((count, columns), bf16),
            pltpu.VMEM((count, width), bf16),
            pltpu.VMEM((columns, width), bf16),
            pltpu.VMEM((more, width), f32),
            pltpu.VMEM(gains.shape, f32),
            pltpu.VMEM((8 * groups, sums[0].shape[1]), f32),
            pltpu.VMEM((4, *block), bf16),
        ],
        12,
        10**9,
        "qkv_grads",
    )


def place_kernel(count, parts, starts_ref, *refs):
    width = refs[0].shape[1]
    loads = Loads(refs[-1])
    for i in range(count):
        lanes = pl.ds(pl.multiple_of(starts_ref[i], width), width)
        for low, rows, out, place in parts:
            target = refs[count + out].at[pl.ds(place, rows), lanes]
            loads.start("a", (refs[i].at[pl.ds(low, rows)], target))
    loads.close()


def place_lanes(blocks, starts, parts, sizes):
    width = len(blocks) * blocks[0].shape[1]
    return call_local(
        functools.partial(place_kernel, len(blocks), parts),
        jnp.stack(starts).astype(jnp.int32),
        blocks,
        [jax.ShapeDtypeStruct((rows, width), bf16) for rows in sizes],
        [pl.ANY] * len(sizes),
        [],
        len(blocks) * len(parts),
        10**9,
        "place_lanes",
        4,
    )


def after(value, *earlier):
    return lax.optimization_barrier((value, *earlier))[0]


def ring(size, step=1):
    return [(i, (i + step) % size) for i in range(size)]


class Lanes:
    def __init__(self):
        self.last = {}

    def wait(self, value, lane):
        return after(value, *self.last.get(lane, ())) if lane in self.last else value

    def move(self, value, axes, pairs, lane):
        got = lax.ppermute(self.wait(value, lane), axes, pairs)
        if lane:
            self.last[lane] = (got,)
        return got

    def swap(self, value, axis):
        return self.move(value, axis, [(0, 1), (1, 0)], None if axis == "c" else axis)

    def around(self, values, size, signs, lane):
        held = [self.wait(value, lane) for value in values]
        got = [lax.ppermute(v, "z", ring(size, signs * (i + 1))) for i, v in enumerate(held)]
        self.last[lane] = tuple(got)
        return got


def by_index(index, first, second, axis):
    return jnp.where(
        index == 0,
        jnp.concatenate([first, second], axis=axis),
        jnp.concatenate([second, first], axis=axis),
    )


def lane_block(value, index, width):
    start = [0] * (value.ndim - 1) + [index * width]
    return lax.dynamic_slice(value, start, (*value.shape[:-1], width))


def plus(left, *right):
    total = left.astype(f32)
    for value in right:
        total = total + value.astype(f32)
    return total


def plane_gather(value, sizes, lanes, parts, heights):
    y_size, x_size = sizes[:2]
    y, x = lax.axis_index("y"), lax.axis_index("x")
    if y_size > 2:
        wide = by_index(x, value, lanes.swap(value, "x"), -1)
        wide = lax.all_gather(wide, "y", axis=0)
        wide = jnp.concatenate([wide[i] for i in range(y_size)], axis=-1)
        return [
            jnp.concatenate([wide[low : low + rows] for low, rows, to, _ in parts if to == out], axis=0)
            for out in range(len(heights))
        ]
    width = value.shape[1]
    far = lanes.swap(value, "y")
    blocks = [value, lanes.swap(value, "x"), far, lanes.swap(far, "x")]
    starts = [(a * x_size + b) * width for a in (y, 1 - y) for b in (x, 1 - x)]
    return place_lanes(blocks, starts, parts, heights)


def plane_scatter(value, sizes, pair, lanes):
    y_size, x_size = sizes[:2]
    y, x = lax.axis_index("y"), lax.axis_index("x")
    block = lambda y_at, x_at: lane_block(value, y_at * x_size + x_at, pair)
    if y_size > 2:
        per_y = [plus(block(i, x), lanes.swap(block(i, 1 - x), "x")).astype(bf16) for i in range(y_size)]
        return lax.psum_scatter(jnp.stack(per_y), "y", scatter_dimension=0, tiled=False).astype(f32)
    far = plus(block(1 - y, x), lanes.swap(block(1 - y, 1 - x), "x")).astype(bf16)
    near = lanes.swap(block(y, 1 - x), "x")
    return plus(block(y, x), near, lanes.swap(far, "y"))


def z_scatter(blocks, size, lanes):
    return plus(blocks[0], *lanes.around(blocks[1:], size, -1, "z"))


def shards(
    sizes,
    tokens,
    segments,
    cotangent,
    attn_gain,
    q_weight,
    k_weight,
    v_weight,
    query_gain,
    key_gain,
    o_weight,
    ffn_gain,
    gate_weight,
    up_weight,
    down_weight,
):
    y_size, x_size, c_size, z_size = sizes
    y, x, c, z = (lax.axis_index(name) for name in "yxcz")
    own_rows, width = tokens.shape
    part = q_weight.shape[0]
    parts = width // part
    pair, quad = c_size * part, x_size * c_size * part
    gain_part = query_gain.shape[0]
    head = gain_part * parts
    seq_count, length = segments.shape

    lanes = Lanes()

    pairs = []
    for low in range(0, z_size, 2):
        pairs += [(z_size + low, low + 1), (low + 1, z_size + low)]
    trades = (c + z) % 2 == 1

    def trade(value, lane):
        return jnp.where(trades, lanes.move(value, ("c", "z"), pairs, lane), value)

    tokens = trade(tokens, None)

    qt, kt, vt, ot = q_weight.T, k_weight.T, v_weight.T, o_weight.T
    q_rows, k_rows = qt.shape[0] // 2, kt.shape[0] // 2
    qkv_rows = q_rows + 2 * k_rows
    qkv_pack = jnp.concatenate([v.reshape(2, -1, part) for v in (qt, kt, vt, ot)], axis=1)
    qkv_pack = qkv_pack.reshape(-1, part)
    qkv_slots = [qkv_pack, *lanes.around([qkv_pack] * (z_size - 1), z_size, 1, "z")]

    sub = gate_weight.shape[1] // (x_size * c_size)
    ffn_pack = jnp.stack([v.T for v in (gate_weight, up_weight, down_weight)]).reshape(
        3, x_size, c_size, sub, part
    )
    mine = lax.dynamic_index_in_dim(ffn_pack, x, 1, keepdims=False)
    other = lax.dynamic_index_in_dim(ffn_pack, 1 - x, 1, keepdims=False)
    ffn_pack = by_index(x, mine, lanes.swap(other, "x"), -1)
    mine = lax.dynamic_index_in_dim(ffn_pack, c, 1, keepdims=False)
    other = lax.dynamic_index_in_dim(ffn_pack, 1 - c, 1, keepdims=False)
    ffn_ready = other
    other = lanes.swap(other, "c")
    ffn_own = jnp.concatenate(
        [
            by_index(c, mine[..., i * part : (i + 1) * part], other[..., i * part : (i + 1) * part], -1)
            for i in range(x_size)
        ],
        axis=-1,
    ).reshape(3 * sub, quad)

    gain_rows = jnp.concatenate(
        [attn_gain[None], ffn_gain[None]]
        + [jnp.pad(g, (0, part - gain_part))[None] for g in (query_gain, key_gain)]
        + [jnp.zeros((12, part), bf16)],
        axis=0,
    )
    numbers = segments.astype(bf16).reshape(-1, part)
    slot_rows = qkv_rows + q_rows

    def rows_of(core):
        return [lax.dynamic_slice_in_dim(v, core * slot_rows, slot_rows, 0) for v in qkv_slots]

    height = z_size * slot_rows + 16
    got = jnp.concatenate([*rows_of(1 - c), gain_rows, numbers], axis=0)
    got = lanes.swap(after(got, ffn_ready), "c")
    own = by_index(c, jnp.concatenate([*rows_of(c), gain_rows], axis=0), got[:height], -1)
    other_segments = got[height:].astype(jnp.int32).reshape(seq_count, length)

    all_tokens = by_index(c, tokens, lanes.swap(tokens, "c"), 0).astype(f32)
    gathered = [(i * slot_rows, qkv_rows, 0, i * qkv_rows) for i in range(z_size)]
    gathered += [(i * slot_rows + qkv_rows, q_rows, 2, i * q_rows) for i in range(z_size)]
    gathered += [(z_size * slot_rows, 16, 1, 0)]
    heights = (z_size * qkv_rows, 16, z_size * q_rows)
    qkv_full, gains, o_full = plane_gather(own, sizes, lanes, gathered, heights)
    gains = gains.astype(f32)
    gain_one, gain_two = gains[0:1], gains[1:2]
    gain_query, gain_key = (
        gains[i].reshape(parts, part)[:, :gain_part].reshape(1, head) for i in (2, 3)
    )
    head_gains = jnp.concatenate(
        [jnp.tile(gain_query, (1, 2)), jnp.tile(gain_key, (1, 2)), jnp.zeros((6, 2 * head), f32)], axis=0
    )

    half = width // 2
    pieces, wide = [ffn_own], []

    def over_y(piece):
        if y_size > 2:
            full = jnp.concatenate(list(lax.all_gather(piece, "y", axis=0)), axis=-1)
            wide.append((full[:, :half], full[:, half:]))
        else:
            wide.append((piece, lanes.swap(piece, "y")))

    over_y(ffn_own)
    for _ in range(1, z_size):
        pieces.append(lanes.move(pieces[-1], "z", ring(z_size), "z"))
        over_y(pieces[-1])
    near, far = [w[0] for w in wide], [w[1] for w in wide]
    cotangent = trade(cotangent, None)
    which = (y if y_size == 2 else y * 0).astype(jnp.int32).reshape(1)

    segment = lax.dynamic_index_in_dim(
        jnp.where(c == z % 2, segments, other_segments), z // 2, 0, keepdims=False
    )
    place = lax.broadcasted_iota(jnp.int32, (length,), 0) - jnp.sum(
        (segment[None, :] < segment[:, None]).astype(jnp.int32), axis=1
    )
    frequency = theta_base ** (-2.0 * jnp.arange(head // 2, dtype=f32) / head)
    angles = place.astype(f32)[:, None] * frequency
    cosine, sine = jnp.cos(angles), jnp.sin(angles)
    cosine = jnp.concatenate([cosine] * 4, axis=1)
    sine = jnp.concatenate([-sine, sine] * 2, axis=1)
    seg_col, seg_row = segment[:, None], segment[None, :]

    inputs = tokens.astype(f32)
    root_one = lax.rsqrt(jnp.mean(inputs * inputs, axis=-1, keepdims=True) + epsilon)
    hat_one = inputs * root_one
    all_root = lax.rsqrt(jnp.mean(all_tokens * all_tokens, axis=-1, keepdims=True) + epsilon)
    normed_one = (all_tokens * all_root * gain_one).astype(bf16)
    normed_one = after(normed_one, pieces[1])
    qkv = dot(normed_one, qkv_full, 1, 1)
    qkv = after(qkv, cotangent)
    tables = (cosine, sine, seg_col, seg_row, head_gains, head)
    context = attend(qkv, *tables, 0, z_size // 2)
    qkv = after(qkv, context, pieces[z_size // 2], far[0])
    context = jnp.concatenate([context, attend(qkv, *tables, z_size // 2, z_size - z_size // 2)], axis=1)

    def half_rows(value, index):
        return lax.dynamic_slice_in_dim(value, index * own_rows, own_rows, 0)

    def core_reduce(left, right, right_dim):
        sent = dot(half_rows(left, 1 - c), right, 1, right_dim).astype(bf16)
        kept = dot(half_rows(left, c), right, 1, right_dim)
        return kept + lanes.swap(sent, "c").astype(f32)

    def spread(value, *earlier):
        across = lanes.swap(value, "x")
        over = lanes.swap(after(across, *earlier) if earlier else across, "c")
        return [value, lanes.swap(value, "c"), across, over]

    cots = spread(cotangent)
    mid = inputs + core_reduce(after(context, cots[2], far[1]), o_full, 0)
    root_two = lax.rsqrt(jnp.mean(mid * mid, axis=-1, keepdims=True) + epsilon)
    hat_two = mid * root_two
    normed_two = (hat_two * gain_two).astype(bf16)
    rows_two = spread(normed_two, far[-2])

    count = z_size // 2
    slot_grads, arrived = [None] * z_size, [None] * z_size

    def turn(group):
        return sorted(range(count), key=lambda i: (group * count + i - 1) % z_size)

    def send_gradients(sent, kept):
        if y_size > 2:
            full = jnp.concatenate([kept, sent], axis=1)
            full = jnp.stack([full[:, k * quad : (k + 1) * quad] for k in range(y_size)])
            got = lax.psum_scatter(full, "y", scatter_dimension=0, tiled=False)
            return got, got.astype(f32)
        got = lanes.swap(sent, "y")
        return got, plus(kept, got)

    gu_0, hid_0, sent, kept = ffn_first(which, near[:count], far[:count], rows_two, cots, turn(0))
    arrived[1], value = send_gradients(sent, kept)
    for i, slot in enumerate(turn(0)):
        slot_grads[slot] = value[i * 3 * sub : (i + 1) * 3 * sub]
    gu_1, hid_1, (first, second, third, fourth) = ffn_second(which, near, far, rows_two, cots, gu_0)
    third = plus(third, lanes.swap(fourth, "c")).astype(bf16)
    across = lanes.swap(third, "x")
    second = lanes.swap(second, "c")
    sent, kept, (out_first, out_second, out_third, out_fourth) = ffn_third(
        after(which, third), near, far, rows_two, cots, gu_1, hid_1, hid_0, turn(1)
    )
    for i in turn(1):
        lanes.last.pop("y", None)
        arrived[count + i], slot_grads[count + i] = send_gradients(sent[i], kept[i])
    ring_first = slot_grads[1].astype(bf16)
    total = lanes.move(ring_first, "z", ring(z_size), "z")
    grad_normed_two = after(plus(first, second, across), out_first)


    def norm_back(grad, hat, root):
        return root * (grad - hat * jnp.mean(grad * hat, axis=-1, keepdims=True))

    gain_two_part = jnp.sum(grad_normed_two * hat_two, axis=0)
    grad_mid = cotangent.astype(f32) + norm_back(grad_normed_two * gain_two, hat_two, root_two)

    branch_own = grad_mid.astype(bf16)
    branch = by_index(c, branch_own, lanes.swap(branch_own, "c"), 0)
    grad_context = dot(branch, o_full, 1, 1).astype(bf16)
    o_grad = dot(after(context, grad_context), branch, 0, 0).astype(bf16)
    grad_context = after(grad_context, o_grad, ring_first)
    grad_first, sums_first = attend_back(qkv, *tables[:-1], grad_context, head, 0, z_size // 2)
    if y_size > 2:
        o_part = plane_scatter(o_grad, sizes, pair, lanes).astype(bf16)
        o_far = o_part
    else:
        block = lambda a, b: lane_block(o_grad, a * x_size + b, pair)
        o_far = lanes.move(block(1 - y, 1 - x), "x", [(0, 1), (1, 0)], None)
        o_near = lanes.move(block(y, 1 - x), "x", [(0, 1), (1, 0)], None)
        o_far = plus(block(1 - y, x), after(o_far, grad_first)).astype(bf16)
        o_part = plus(block(y, x), o_near)
    total = plus(after(total, grad_first), slot_grads[2]).astype(bf16)
    grad_last, sums_last = attend_back(
        qkv, *tables[:-1], after(grad_context, total, o_far), head, z_size // 2, z_size - z_size // 2
    )
    if y_size == 2:
        o_far = lanes.move(o_far, "y", [(0, 1), (1, 0)], None)
        o_part = plus(o_part, after(o_far, grad_last)).astype(bf16)
    total = lanes.move(total, "z", ring(z_size), "z")
    out_third = plus(out_third, lanes.swap(out_fourth, "c")).astype(bf16)
    out_third = after(out_third, grad_normed_two)
    out_across = lanes.move(out_third, "x", [(0, 1), (1, 0)], None)
    output = mid + plus(out_first, lanes.swap(out_second, "c"), after(out_across, grad_first))
    output = output.astype(bf16)
    grad_last = after(grad_last, o_part, arrived[-1])
    for step in range(2, z_size - 1):
        total = plus(after(total, grad_last), slot_grads[step + 1]).astype(bf16)
        grad_last = after(grad_last, total)
        total = lanes.move(total, "z", ring(z_size), "z")
    total_last = plus(total, slot_grads[0])
    extra = [jnp.zeros((1, width), f32), gain_two_part[None], jnp.zeros((14, width), f32)]
    spaced = part < 2 * head
    if spaced:
        sums = jnp.sum(jnp.concatenate([sums_first, sums_last]).reshape(-1, 8, 2 * head), axis=0)
        extra[2:] = [
            jnp.pad(v.reshape(parts, gain_part), ((0, 0), (0, part - gain_part))).reshape(1, width)
            for v in (sums[0, :head] + sums[0, head:], sums[1, :head])
        ] + [jnp.zeros((12, width), f32)]
    extra = jnp.concatenate(extra, axis=0)
    if y_size > 2:
        starts = [which[0] + i * (width // 4) for i in range(4)]
    else:
        starts = [(a * x_size + b) * pair for a, b in ((1 - y, 1 - x), (y, 1 - x), (1 - y, x), (y, x))]
    blocks = qkv_grads(
        starts, (grad_first, grad_last), normed_one, qkv_full, extra, gain_one, (sums_first, sums_last), z_size, spaced
    )
    if y_size > 2:
        qkv_part = plane_scatter(jnp.concatenate(blocks, axis=1), sizes, pair, lanes).astype(bf16)
    else:
        far_got = lanes.move(blocks[0], "x", [(0, 1), (1, 0)], None)
        near_got = lanes.move(after(blocks[1], far_got), "x", [(0, 1), (1, 0)], None)
        lanes.last["x"] = (near_got,)
        far_sum = plus(blocks[2], far_got).astype(bf16)
        qkv_part = plus(blocks[3], near_got, lanes.swap(far_sum, "y")).astype(bf16)
    output = trade(output, None)
    grad_first = after(grad_first, blocks[3])
    cut = grad_first.shape[1]

    def two_terms(index):
        return dot(half_rows(grad_first, index), qkv_full[:cut], 1, 0) + dot(
            half_rows(grad_last, index), qkv_full[cut:], 1, 0
        )

    sent = two_terms(1 - c).astype(bf16)
    grad_normed_one = two_terms(c) + lanes.swap(sent, "c").astype(f32)

    def core_deal(value):
        kept = lane_block(value, c, part)
        sent = lanes.swap(lane_block(value, 1 - c, part), "c")
        return jnp.where(c == 0, jnp.stack([kept, sent]), jnp.stack([sent, kept]))

    wgrads = total_last.astype(bf16).reshape(3, sub, quad)
    kept = lane_block(wgrads, x, pair)
    sent = lanes.swap(lane_block(wgrads, 1 - x, pair), "x")
    wgrads = jnp.where(x == 0, jnp.stack([kept, sent], 1), jnp.stack([sent, kept], 1))
    kept = lane_block(wgrads, c, part)
    sent = lanes.swap(lane_block(wgrads, 1 - c, part), "c")
    wgrads = jnp.where(c == 0, jnp.stack([kept, sent], 2), jnp.stack([sent, kept], 2))
    wgrads = wgrads.reshape(3, x_size * c_size * sub, part)
    gate_wgrad, up_wgrad, down_wgrad = (wgrads[i].astype(f32).T for i in range(3))


    tokens_grad = (grad_mid + norm_back(grad_normed_one * gain_one, hat_one, root_one)).astype(bf16)
    rows = qkv_rows + 16
    lanes.last.pop("z", None)
    value = z_scatter(
        [
            jnp.concatenate(
                [qkv_part[i * rows : (i + 1) * rows], o_part[i * q_rows : (i + 1) * q_rows]], axis=0
            )
            for i in range(z_size)
        ],
        z_size,
        lanes,
    )
    value = after(value.astype(bf16), output)
    kept = lane_block(value, c, part)
    sent = lanes.swap(lane_block(value, 1 - c, part), "c")
    gain_sums = plus(kept[qkv_rows:rows], sent[qkv_rows:rows])
    qkv_grad = jnp.where(c == 0, jnp.stack([kept, sent]), jnp.stack([sent, kept])).astype(f32)
    o_wgrad = qkv_grad[:, rows:].reshape(2 * q_rows, part).T
    qkv_grad = qkv_grad[:, :qkv_rows]
    q_wgrad = qkv_grad[:, :q_rows].reshape(-1, part).T
    k_wgrad = qkv_grad[:, q_rows : q_rows + k_rows].reshape(-1, part).T
    v_wgrad = qkv_grad[:, q_rows + k_rows :].reshape(-1, part).T
    if spaced:
        gain_query_sum, gain_key_sum = gain_sums[2, :gain_part], gain_sums[3, :gain_part]
    else:
        mine = ((y * x_size + x) * c_size + c) * gain_part
        gain_query_sum, gain_key_sum = (
            lax.dynamic_slice(gain_sums[2], (mine + at,), (gain_part,)) for at in (0, head)
        )
    return (
        output,
        trade(tokens_grad, None),
        gain_sums[0],
        q_wgrad,
        k_wgrad,
        v_wgrad,
        gain_query_sum,
        gain_key_sum,
        o_wgrad,
        gain_sums[1],
        gate_wgrad,
        up_wgrad,
        down_wgrad,
    )


def solution(mesh):
    dp, tp = mesh.devices.shape
    sizes = (dp // 4, 2, 2, tp)
    fine = Mesh(mesh.devices.reshape(sizes), ("y", "x", "c", "z"))
    d = ("y", "x", "c")
    rows, weight, gain = P((*d, "z"), None), P(d, "z"), P(d)
    return jax.shard_map(
        functools.partial(shards, sizes),
        mesh=fine,
        in_specs=(rows, P(d, None), rows, gain, weight, weight, weight, gain, gain, weight, gain)
        + (weight,) * 3,
        out_specs=(rows, rows, gain, weight, weight, weight, gain, gain, weight, gain) + (weight,) * 3,
        check_vma=False,
    )
```

```python
import functools

import jax
import jax.numpy as jnp
from jax import lax
from jax.experimental import pallas as pl
from jax.experimental.pallas import tpu as pltpu
from jax.sharding import Mesh, PartitionSpec as P

epsilon = 1e-05
theta_base = 1000000.0
bf16 = jnp.bfloat16
f32 = jnp.float32
tile = 256
span = 512


def cost(flops):
    return pl.CostEstimate(flops=flops // 1000, bytes_accessed=10**5, transcendentals=0)


def dot(left, right, left_dim, right_dim):
    return lax.dot_general(
        left, right, (((left_dim,), (right_dim,)), ((), ())), preferred_element_type=f32
    )


def group_sum(value, ones):
    high = value.astype(bf16)
    low = (value - high.astype(f32)).astype(bf16)
    return dot(high, ones, 1, 0) + dot(low, ones, 1, 0)


def ones_by_head(lanes, head):
    row = lax.broadcasted_iota(jnp.int32, (lanes, lanes), 0) // head
    col = lax.broadcasted_iota(jnp.int32, (lanes, lanes), 1) // head
    return jnp.where(row == col, 1.0, 0.0).astype(bf16)


def half_swap(value, head):
    lanes = value.shape[-1]
    lane = lax.broadcasted_iota(jnp.int32, value.shape, 1) % head
    return jnp.where(
        lane < head // 2,
        pltpu.roll(value, lanes - head // 2, 1),
        pltpu.roll(value, head // 2, 1),
    )


def head_norm(raw, ones, head):
    root = lax.rsqrt(group_sum(raw * raw, ones) * (1.0 / head) + epsilon)
    return raw * root, root


def split_block(block, head):
    lanes = 2 * head
    queries = block[:, :lanes]
    both = block[:, lanes:]
    other = pltpu.roll(both, head, 1)
    first = lax.broadcasted_iota(jnp.int32, both.shape, 1) < head
    keys = jnp.where(first, both, other)
    values = jnp.where(first, other, both)
    return queries, keys, values


def stack_heads(block, head):
    first = lax.broadcasted_iota(jnp.int32, block.shape, 1) < head
    zero = jnp.zeros_like(block)
    return jnp.concatenate([jnp.where(first, block, zero), jnp.where(first, zero, block)], axis=0)


def merge_heads(stacked, head):
    half = stacked.shape[0] // 2
    first = lax.broadcasted_iota(jnp.int32, (half, stacked.shape[1]), 1) < head
    return jnp.where(first, stacked[:half], stacked[half:])


def attend_kernel(head, qkv_ref, cos_ref, sin_ref, seg_col, seg_row, gain_ref, ctx_ref, q_s, k_s, v_s):
    length = qkv_ref.shape[0]
    lanes = 2 * head
    ones = ones_by_head(lanes, head)
    queries, keys, values = split_block(qkv_ref[...].astype(f32), head)
    cosine, sine = cos_ref[...], sin_ref[...]

    def rotated(raw, gain):
        hat, _ = head_norm(raw, ones, head)
        scaled = hat * gain
        return (scaled * cosine + half_swap(scaled, head) * sine).astype(bf16)

    q_s[...] = rotated(queries, gain_ref[0:1, :]) * jnp.asarray(head**-0.5, bf16)
    k_s[...] = rotated(keys, gain_ref[1:2, :])
    v_s[...] = values.astype(bf16)
    for top in range(0, length, tile):
        low, high = max(0, top - span), top + tile
        stacked = stack_heads(q_s[top:high, :], head)
        scores = dot(stacked, k_s[low:high, :], 1, 1)
        row = lax.broadcasted_iota(jnp.int32, (tile, high - low), 0) + top
        col = lax.broadcasted_iota(jnp.int32, (tile, high - low), 1) + low
        allowed = (seg_col[top:high, 0:1] == seg_row[0:1, low:high]) & (row >= col)
        allowed = jnp.concatenate([allowed, allowed], axis=0)
        exponent = jnp.where(allowed, jnp.exp(scores), 0.0)
        total = jnp.sum(exponent, axis=1, keepdims=True)
        mixed = dot(exponent.astype(bf16), v_s[low:high, :], 1, 0) / total
        ctx_ref[top:high, :] = merge_heads(mixed, head).astype(bf16)


def attend(qkv, cosine, sine, seg_col, seg_row, gains, head, first, groups):
    length = qkv.shape[0]
    lanes = 2 * head
    whole = lambda shape: pl.BlockSpec(shape, lambda j: (0, 0))
    return pl.pallas_call(
        functools.partial(attend_kernel, head),
        grid=(groups,),
        in_specs=[
            pl.BlockSpec((length, 2 * lanes), lambda j: (0, j + first)),
            whole((length, lanes)),
            whole((length, lanes)),
            whole((length, 1)),
            whole((1, length)),
            whole((8, lanes)),
        ],
        out_specs=pl.BlockSpec((length, lanes), lambda j: (0, j)),
        out_shape=jax.ShapeDtypeStruct((length, groups * lanes), bf16),
        scratch_shapes=[pltpu.VMEM((length, lanes), bf16)] * 3,
        compiler_params=pltpu.CompilerParams(vmem_limit_bytes=24 * 2**20),
        cost_estimate=cost(6 * 10**9),
        name="attend",
    )(qkv, cosine, sine, seg_col, seg_row, gains)


def attend_back_kernel(
    head, qkv_ref, cos_ref, sin_ref, seg_col, seg_row, gain_ref, do_ref, out_ref, sums_ref,
    q_s, k_s, v_s, dk_s, dv_s, dq_s,
):
    length = qkv_ref.shape[0]
    lanes = 2 * head
    ones = ones_by_head(lanes, head)
    queries, keys, values = split_block(qkv_ref[...].astype(f32), head)
    cosine, sine = cos_ref[...], sin_ref[...]

    def rotated(raw, gain):
        hat, _ = head_norm(raw, ones, head)
        scaled = hat * gain
        return (scaled * cosine + half_swap(scaled, head) * sine).astype(bf16)

    scale = jnp.asarray(head**-0.5, bf16)
    q_s[...] = rotated(queries, gain_ref[0:1, :]) * scale
    k_s[...] = rotated(keys, gain_ref[1:2, :])
    v_s[...] = values.astype(bf16)
    dk_s[...] = jnp.zeros_like(dk_s)
    dv_s[...] = jnp.zeros_like(dv_s)
    for top in range(0, length, tile):
        low, high = max(0, top - span), top + tile
        stacked = stack_heads(q_s[top:high, :], head)
        grads = stack_heads(do_ref[top:high, :], head)
        near_k, near_v = k_s[low:high, :], v_s[low:high, :]
        scores = dot(near_k, stacked, 1, 1)
        col = lax.broadcasted_iota(jnp.int32, (high - low, tile), 0) + low
        row = lax.broadcasted_iota(jnp.int32, (high - low, tile), 1) + top
        allowed = (seg_col[low:high, 0:1] == seg_row[0:1, top:high]) & (row >= col)
        allowed = jnp.concatenate([allowed, allowed], axis=1)
        exponent = jnp.where(allowed, jnp.exp(scores), 0.0)
        probs = exponent * (1.0 / jnp.sum(exponent, axis=0, keepdims=True))
        grad_probs = dot(near_v, grads, 1, 1)
        weighted = probs * grad_probs
        delta = jnp.sum(weighted, axis=0, keepdims=True)
        grad_scores = (weighted - probs * delta).astype(bf16)
        dv_s[low:high, :] += dot(probs.astype(bf16), grads, 1, 0)
        dk_s[low:high, :] += dot(grad_scores, stacked, 1, 0)
        dq_s[top:high, :] = merge_heads(dot(grad_scores, near_k, 0, 0), head) * head**-0.5

    def back(raw, gain, grad):
        hat, root = head_norm(raw, ones, head)
        normed = grad * cosine - half_swap(grad, head) * sine
        gain_part = jnp.sum(normed * hat, axis=0, keepdims=True)
        scaled = normed * gain
        mean = group_sum(scaled * hat, ones) * (1.0 / head)
        return root * (scaled - hat * mean), gain_part

    grad_q, q_sum = back(queries, gain_ref[0:1, :], dq_s[...])
    folded_k = dk_s[...] + pltpu.roll(dk_s[...], head, 1)
    grad_k, k_sum = back(keys, gain_ref[1:2, :], folded_k)
    folded_v = dv_s[...] + pltpu.roll(dv_s[...], head, 1)
    first = lax.broadcasted_iota(jnp.int32, (length, lanes), 1) < head
    out_ref[:, :lanes] = grad_q.astype(bf16)
    out_ref[:, lanes:] = jnp.where(first, grad_k, folded_v).astype(bf16)
    which = lax.broadcasted_iota(jnp.int32, sums_ref.shape, 0)
    sums_ref[...] = jnp.where(which == 0, q_sum, jnp.where(which == 1, k_sum, 0.0))


def attend_back(qkv, cosine, sine, seg_col, seg_row, gains, grad_context, head, first, groups):
    length = qkv.shape[0]
    lanes = 2 * head
    whole = lambda shape: pl.BlockSpec(shape, lambda j: (0, 0))
    return pl.pallas_call(
        functools.partial(attend_back_kernel, head),
        grid=(groups,),
        in_specs=[
            pl.BlockSpec((length, 2 * lanes), lambda j: (0, j + first)),
            whole((length, lanes)),
            whole((length, lanes)),
            whole((length, 1)),
            whole((1, length)),
            whole((8, lanes)),
            pl.BlockSpec((length, lanes), lambda j: (0, j + first)),
        ],
        out_specs=(
            pl.BlockSpec((length, 2 * lanes), lambda j: (0, j)),
            pl.BlockSpec((8, lanes), lambda j: (j, 0)),
        ),
        out_shape=(
            jax.ShapeDtypeStruct((length, groups * 2 * lanes), bf16),
            jax.ShapeDtypeStruct((8 * groups, lanes), f32),
        ),
        scratch_shapes=[pltpu.VMEM((length, lanes), bf16)] * 3 + [pltpu.VMEM((length, lanes), f32)] * 3,
        compiler_params=pltpu.CompilerParams(vmem_limit_bytes=58 * 2**20),
        cost_estimate=cost(12 * 10**9),
        name="attend_back",
    )(qkv, cosine, sine, seg_col, seg_row, gains, grad_context)


def pull(pairs, sems, start):
    copies = [pltpu.make_async_copy(s, d, sems.at[start + i]) for i, (s, d) in enumerate(pairs)]
    for copy in copies:
        copy.start()
    return copies


def finish(copies):
    for copy in copies:
        copy.wait()


def halves(which_ref, half):
    first = pl.multiple_of(which_ref[0] * half, half)
    second = pl.multiple_of((1 - which_ref[0]) * half, half)
    return pl.ds(first, half), pl.ds(second, half)


def call_local(kernel, which, arrays, outs, out_spaces, scratch, copies, flops, name, limit=58):
    return pl.pallas_call(
        kernel,
        in_specs=[pl.BlockSpec(memory_space=pltpu.SMEM)] + [pl.BlockSpec(memory_space=pltpu.HBM)] * len(arrays),
        out_specs=[pl.BlockSpec(memory_space=space) for space in out_spaces],
        out_shape=outs,
        scratch_shapes=[*scratch, pltpu.SemaphoreType.DMA((copies,))],
        compiler_params=pltpu.CompilerParams(vmem_limit_bytes=limit * 2**20),
        cost_estimate=cost(flops),
        name=name,
    )(which, *arrays)


class Loads:
    def __init__(self, sems):
        self.sems, self.count, self.open = sems, 0, {}

    def start(self, key, *pairs):
        for source, target in pairs:
            copy = pltpu.make_async_copy(source, target, self.sems.at[self.count])
            copy.start()
            self.open.setdefault(key, []).append(copy)
            self.count += 1

    def wait(self, *keys):
        for key in keys:
            for copy in self.open.pop(key, ()):
                copy.wait()

    def close(self):
        self.wait(*list(self.open))


def load_gate_up(loads, key, near, far, which_ref, target, slots):
    size, half = near[0].shape
    top = 2 * size // 3
    for at, i in enumerate(slots):
        for pieces, lanes in zip((near, far), halves(which_ref, half)):
            loads.start((key, at), (pieces[i].at[pl.ds(0, top)], target.at[pl.ds(at * top, top), lanes]))


def load_down(loads, key, near, far, which_ref, target, slots):
    size, half = near[0].shape
    rest = size // 3
    for at, i in enumerate(slots):
        for pieces, lanes in zip((near, far), halves(which_ref, half)):
            loads.start(
                (key, at), (pieces[i].at[pl.ds(size - rest, rest)], target.at[pl.ds(at * rest, rest), lanes])
            )


def hidden_step(gate_up, down, rows, cot, gu_s, hid_s, slot, columns, sub):
    both = dot(gate_up[2 * slot * sub : 2 * (slot + 1) * sub, :], rows, 1, 1)
    back = dot(down[slot * sub : (slot + 1) * sub, :], cot, 1, 1)
    gate, up = both[:sub], both[sub:]
    sig = 0.5 * jnp.tanh(0.5 * gate) + 0.5
    act = gate * sig
    base = 2 * slot * sub
    gu_s[base : base + sub, columns] = (back * up * (sig + act * (1.0 - sig))).astype(bf16)
    gu_s[base + sub : base + 2 * sub, columns] = (back * act).astype(bf16)
    hid_s[slot * sub : (slot + 1) * sub, columns] = (act * up).astype(bf16)


def weight_step(loads, which_ref, gu_s, hid_s, rows_s, cot_s, out_s, far_out, near_out, order, sub):
    size, half = 3 * sub, rows_s.shape[1] // 2
    first, second = halves(which_ref, half)
    for side, lanes, outs in ((0, second, far_out), (1, first, near_out)):
        rows, cots = rows_s[:, lanes], cot_s[:, lanes]
        for at, s in enumerate(order):
            out_s[side, s, : 2 * sub] = dot(gu_s[2 * s * sub : 2 * (s + 1) * sub, :], rows, 1, 0).astype(bf16)
            out_s[side, s, 2 * sub :] = dot(hid_s[s * sub : (s + 1) * sub, :], cots, 1, 0).astype(bf16)
            target = outs[s] if len(outs) > 1 else outs[0].at[pl.ds(at * size, size)]
            loads.start("out", (out_s.at[side, s], target))


def take(refs, *counts):
    at, out = 0, []
    for count in counts:
        out.append(refs[at : at + count])
        at += count
    return (*out, refs[at:])


def first_kernel(slots, quarters, order, which_ref, *refs):
    near, far, rows, cots, (gu_out, hid_out), far_out, near_out, rest = take(
        refs, slots, slots, quarters, quarters, 2, 1, 1
    )
    gate_up, down, rows_s, cot_s, gu_s, hid_s, out_s, sems = rest
    sub, count = near[0].shape[0] // 3, rows[0].shape[0]
    loads = Loads(sems)
    for q in range(max(slots, quarters)):
        if q < quarters:
            place = pl.ds(q * count, count)
            loads.start(("rows", q), (rows[q], rows_s.at[place]), (cots[q], cot_s.at[place]))
        if q == 0:
            load_gate_up(loads, "w", near, far, which_ref, gate_up, range(slots))
            load_down(loads, "w", near, far, which_ref, down, range(slots))
    for q in range(quarters):
        columns = slice(q * count, (q + 1) * count)
        loads.wait(("rows", q))
        for s in range(slots):
            loads.wait(("w", s))
            hidden_step(gate_up, down, rows_s[columns, :], cot_s[columns, :], gu_s, hid_s, s, columns, sub)
    loads.start("out", (gu_s, gu_out), (hid_s, hid_out))
    weight_step(loads, which_ref, gu_s, hid_s, rows_s, cot_s, out_s, far_out, near_out, order, sub)
    loads.close()


def ffn_first(which, near, far, rows, cots, order):
    slots, quarters = len(near), len(rows)
    size, half = near[0].shape
    sub, count = size // 3, rows[0].shape[0]
    tokens = quarters * count
    gu, hid = (2 * slots * sub, tokens), (slots * sub, tokens)
    out = call_local(
        functools.partial(first_kernel, slots, quarters, order),
        which,
        [*near, *far, *rows, *cots],
        [jax.ShapeDtypeStruct(v, bf16) for v in (gu, hid)]
        + [jax.ShapeDtypeStruct((slots * size, half), bf16)] * 2,
        [pl.ANY] * 4,
        [
            pltpu.VMEM((2 * slots * sub, 2 * half), bf16),
            pltpu.VMEM((slots * sub, 2 * half), bf16),
            pltpu.VMEM((tokens, 2 * half), bf16),
            pltpu.VMEM((tokens, 2 * half), bf16),
            pltpu.VMEM(gu, bf16),
            pltpu.VMEM(hid, bf16),
            pltpu.VMEM((2, slots, size, half), bf16),
        ],
        2 * quarters + 4 * slots + 2 + 2 * slots,
        8 * slots * size * half * tokens,
        "ffn_first",
    )
    return out


def second_kernel(slots, quarters, which_ref, *refs):
    near, far, rows, cots, (gu_0,), (gu_out, hid_out), outs, rest = take(
        refs, 2 * slots, 2 * slots, quarters, quarters, 1, 2, quarters
    )
    gate_up, down, gate_up_0, rows_s, cot_s, gu_s, hid_s, gu_0s, out_s, sems = rest
    sub, count = near[0].shape[0] // 3, rows[0].shape[0]
    loads = Loads(sems)
    for q in range(quarters):
        place = pl.ds(q * count, count)
        loads.start(("rows", q), (rows[q], rows_s.at[place]), (cots[q], cot_s.at[place]))
        if q == 0:
            load_gate_up(loads, "w", near, far, which_ref, gate_up, range(slots, 2 * slots))
            load_down(loads, "w", near, far, which_ref, down, range(slots, 2 * slots))
    load_gate_up(loads, "w0", near, far, which_ref, gate_up_0, range(slots))
    loads.start("g0", (gu_0, gu_0s))
    for q in range(quarters):
        columns = slice(q * count, (q + 1) * count)
        loads.wait(("rows", q))
        for s in range(slots):
            loads.wait(("w", s))
            hidden_step(gate_up, down, rows_s[columns, :], cot_s[columns, :], gu_s, hid_s, s, columns, sub)
    loads.start("out", (gu_s, gu_out), (hid_s, hid_out))
    loads.wait("g0", *(("w0", s) for s in range(slots)))
    for q in range(quarters):
        columns = slice(q * count, (q + 1) * count)
        total = dot(gu_0s[:, columns], gate_up_0[...], 0, 0) + dot(gu_s[:, columns], gate_up[...], 0, 0)
        out_s[q] = total.astype(bf16)
        loads.start("out", (out_s.at[q], outs[q]))
    loads.close()


def ffn_second(which, near, far, rows, cots, gu_0):
    slots, quarters = len(near) // 2, len(rows)
    size, half = near[0].shape
    sub, count = size // 3, rows[0].shape[0]
    tokens = quarters * count
    gu, hid = (2 * slots * sub, tokens), (slots * sub, tokens)
    out = call_local(
        functools.partial(second_kernel, slots, quarters),
        which,
        [*near, *far, *rows, *cots, gu_0],
        [jax.ShapeDtypeStruct(v, bf16) for v in (gu, hid)]
        + [jax.ShapeDtypeStruct((count, 2 * half), bf16)] * quarters,
        [pl.ANY] * (2 + quarters),
        [
            pltpu.VMEM((2 * slots * sub, 2 * half), bf16),
            pltpu.VMEM((slots * sub, 2 * half), bf16),
            pltpu.VMEM((2 * slots * sub, 2 * half), bf16),
            pltpu.VMEM((tokens, 2 * half), bf16),
            pltpu.VMEM((tokens, 2 * half), bf16),
            pltpu.VMEM(gu, bf16),
            pltpu.VMEM(hid, bf16),
            pltpu.VMEM(gu, bf16),
            pltpu.VMEM((quarters, count, 2 * half), bf16),
        ],
        3 * quarters + 6 * slots + 3,
        10 * slots * size * half * tokens,
        "ffn_second",
    )
    return out[0], out[1], out[2:]


def third_kernel(slots, quarters, order, which_ref, *refs):
    near, far, rows, cots, (gu, hid, hid_0), far_out, near_out, outs, rest = take(
        refs, 2 * slots, 2 * slots, quarters, quarters, 3, slots, slots, quarters
    )
    down, rows_s, cot_s, gu_s, hid_s, hid_0s, grad_s, out_s, sems = rest
    sub, count = far_out[0].shape[0] // 3, rows[0].shape[0]
    loads = Loads(sems)
    load_down(loads, "w", near, far, which_ref, down, range(2 * slots))
    loads.start("h", (hid_0, hid_0s), (hid, hid_s))
    loads.start("rows", (gu, gu_s))
    for q in range(quarters):
        place = pl.ds(q * count, count)
        loads.start("rows", (rows[q], rows_s.at[place]), (cots[q], cot_s.at[place]))
    loads.wait("h", *(("w", s) for s in range(2 * slots)))
    for q in range(quarters):
        columns = slice(q * count, (q + 1) * count)
        total = dot(hid_0s[:, columns], down[: slots * sub, :], 0, 0)
        total = total + dot(hid_s[:, columns], down[slots * sub :, :], 0, 0)
        out_s[q] = total.astype(bf16)
        loads.start("out", (out_s.at[q], outs[q]))
    loads.wait("rows")
    weight_step(loads, which_ref, gu_s, hid_s, rows_s, cot_s, grad_s, far_out, near_out, order, sub)
    loads.close()


def ffn_third(which, near, far, rows, cots, gu, hid, hid_0, order):
    slots, quarters = len(order), len(rows)
    size, half = near[0].shape
    sub, count = size // 3, rows[0].shape[0]
    tokens = quarters * count
    out = call_local(
        functools.partial(third_kernel, slots, quarters, order),
        which,
        [*near, *far, *rows, *cots, gu, hid, hid_0],
        [jax.ShapeDtypeStruct((size, half), bf16)] * (2 * slots)
        + [jax.ShapeDtypeStruct((count, 2 * half), bf16)] * quarters,
        [pl.ANY] * (2 * slots + quarters),
        [
            pltpu.VMEM((2 * slots * sub, 2 * half), bf16),
            pltpu.VMEM((tokens, 2 * half), bf16),
            pltpu.VMEM((tokens, 2 * half), bf16),
            pltpu.VMEM((2 * slots * sub, tokens), bf16),
            pltpu.VMEM((slots * sub, tokens), bf16),
            pltpu.VMEM((slots * sub, tokens), bf16),
            pltpu.VMEM((2, slots, size, half), bf16),
            pltpu.VMEM((quarters, count, 2 * half), bf16),
        ],
        3 * quarters + 4 * slots + 3 + 2 * slots,
        6 * slots * size * half * tokens,
        "ffn_third",
    )
    return out[:slots], out[slots : 2 * slots], out[2 * slots :]


def qkv_grads_kernel(groups, spaced, starts_ref, grads_0, grads_1, rows, weights, extra_ref, gain_ref, sums_0, sums_1, *refs):
    outs, rest = refs[:4], refs[4:]
    grad_s, rows_s, weight_s, extra_s, gain_s, sums_s, out_s, sems = rest
    size = (grads_0.shape[1] + grads_1.shape[1]) // groups
    width = outs[0].shape[1]
    more = extra_ref.shape[0]
    cut = grads_0.shape[1]
    loads = Loads(sems)
    loads.start("a", (grads_0, grad_s.at[:, pl.ds(0, cut)]), (grads_1, grad_s.at[:, pl.ds(cut, grads_1.shape[1])]))
    loads.start("a", (rows, rows_s))
    loads.start("b", (weights.at[pl.ds(0, groups * size)], weight_s), (extra_ref, extra_s), (gain_ref, gain_s))
    loads.start("b", (sums_0, sums_s.at[pl.ds(0, sums_0.shape[0])]))
    loads.start("b", (sums_1, sums_s.at[pl.ds(sums_0.shape[0], sums_1.shape[0])]))
    loads.wait("a")
    for i in range(4):
        lanes = pl.ds(pl.multiple_of(starts_ref[i], width), width)
        block = dot(grad_s[...], rows_s[:, lanes], 0, 0)
        if i == 0:
            loads.wait("b")
        gain_row = jnp.sum(block * weight_s[:, lanes].astype(f32), axis=0, keepdims=True)
        gain_row = gain_row / gain_s[0:1, lanes]
        row = lax.broadcasted_iota(jnp.int32, (more, width), 0)
        extra = jnp.where(row == 0, gain_row, extra_s[:, lanes])
        if not spaced:
            sums = sums_s[0:8, :]
            for g in range(1, groups):
                sums = sums + sums_s[8 * g : 8 * (g + 1), :]
            head = sums.shape[1] // 2
            query = sums[0:1, :] + pltpu.roll(sums[0:1, :], head, 1)
            lane = lax.broadcasted_iota(jnp.int32, query.shape, 1)
            both = jnp.where(lane < head, query, pltpu.roll(sums[1:2, :], head, 1))
            both = jnp.concatenate([both] * (width // (2 * head)), axis=1)
            extra = jnp.where(row == 2, both, extra)
        extra = extra.astype(bf16)
        for g in range(groups):
            base = g * (size + more)
            out_s[i, base : base + size, :] = block[g * size : (g + 1) * size, :].astype(bf16)
            out_s[i, base + size : base + size + more, :] = extra
        loads.start("out", (out_s.at[i], outs[i]))
    loads.close()


def qkv_grads(starts, grads, rows, weights, extra, gains, sums, groups, spaced):
    count, width = rows.shape
    columns, more = grads[0].shape[1] + grads[1].shape[1], extra.shape[0]
    block = (columns + groups * more, width // 4)
    return call_local(
        functools.partial(qkv_grads_kernel, groups, spaced),
        jnp.stack(starts).astype(jnp.int32),
        [*grads, rows, weights, extra, gains, *sums],
        [jax.ShapeDtypeStruct(block, bf16)] * 4,
        [pl.ANY] * 4,
        [
            pltpu.VMEM((count, columns), bf16),
            pltpu.VMEM((count, width), bf16),
            pltpu.VMEM((columns, width), bf16),
            pltpu.VMEM((more, width), f32),
            pltpu.VMEM(gains.shape, f32),
            pltpu.VMEM((8 * groups, sums[0].shape[1]), f32),
            pltpu.VMEM((4, *block), bf16),
        ],
        12,
        10**9,
        "qkv_grads",
    )


def place_kernel(count, parts, starts_ref, *refs):
    width = refs[0].shape[1]
    loads = Loads(refs[-1])
    for i in range(count):
        lanes = pl.ds(pl.multiple_of(starts_ref[i], width), width)
        for low, rows, out, place in parts:
            target = refs[count + out].at[pl.ds(place, rows), lanes]
            loads.start("a", (refs[i].at[pl.ds(low, rows)], target))
    loads.close()


def place_lanes(blocks, starts, parts, sizes):
    width = len(blocks) * blocks[0].shape[1]
    return call_local(
        functools.partial(place_kernel, len(blocks), parts),
        jnp.stack(starts).astype(jnp.int32),
        blocks,
        [jax.ShapeDtypeStruct((rows, width), bf16) for rows in sizes],
        [pl.ANY] * len(sizes),
        [],
        len(blocks) * len(parts),
        10**9,
        "place_lanes",
        4,
    )


def after(value, *earlier):
    return lax.optimization_barrier((value, *earlier))[0]


def ring(size, step=1):
    return [(i, (i + step) % size) for i in range(size)]


class Lanes:
    def __init__(self):
        self.last = {}

    def wait(self, value, lane):
        return after(value, *self.last.get(lane, ())) if lane in self.last else value

    def move(self, value, axes, pairs, lane):
        got = lax.ppermute(self.wait(value, lane), axes, pairs)
        if lane:
            self.last[lane] = (got,)
        return got

    def swap(self, value, axis):
        return self.move(value, axis, [(0, 1), (1, 0)], None if axis == "c" else axis)

    def around(self, values, size, signs, lane):
        held = [self.wait(value, lane) for value in values]
        got = [lax.ppermute(v, "z", ring(size, signs * (i + 1))) for i, v in enumerate(held)]
        self.last[lane] = tuple(got)
        return got


def by_index(index, first, second, axis):
    return jnp.where(
        index == 0,
        jnp.concatenate([first, second], axis=axis),
        jnp.concatenate([second, first], axis=axis),
    )


def lane_block(value, index, width):
    start = [0] * (value.ndim - 1) + [index * width]
    return lax.dynamic_slice(value, start, (*value.shape[:-1], width))


def plus(left, *right):
    total = left.astype(f32)
    for value in right:
        total = total + value.astype(f32)
    return total


def plane_gather(value, sizes, lanes, parts, heights):
    y_size, x_size = sizes[:2]
    y, x = lax.axis_index("y"), lax.axis_index("x")
    if y_size > 2:
        wide = by_index(x, value, lanes.swap(value, "x"), -1)
        wide = lax.all_gather(wide, "y", axis=0)
        wide = jnp.concatenate([wide[i] for i in range(y_size)], axis=-1)
        return [
            jnp.concatenate([wide[low : low + rows] for low, rows, to, _ in parts if to == out], axis=0)
            for out in range(len(heights))
        ]
    width = value.shape[1]
    far = lanes.swap(value, "y")
    blocks = [value, lanes.swap(value, "x"), far, lanes.swap(far, "x")]
    starts = [(a * x_size + b) * width for a in (y, 1 - y) for b in (x, 1 - x)]
    return place_lanes(blocks, starts, parts, heights)


def plane_scatter(value, sizes, pair, lanes):
    y_size, x_size = sizes[:2]
    y, x = lax.axis_index("y"), lax.axis_index("x")
    block = lambda y_at, x_at: lane_block(value, y_at * x_size + x_at, pair)
    if y_size > 2:
        per_y = [plus(block(i, x), lanes.swap(block(i, 1 - x), "x")).astype(bf16) for i in range(y_size)]
        return lax.psum_scatter(jnp.stack(per_y), "y", scatter_dimension=0, tiled=False).astype(f32)
    far = plus(block(1 - y, x), lanes.swap(block(1 - y, 1 - x), "x")).astype(bf16)
    near = lanes.swap(block(y, 1 - x), "x")
    return plus(block(y, x), near, lanes.swap(far, "y"))


def z_scatter(blocks, size, lanes):
    return plus(blocks[0], *lanes.around(blocks[1:], size, -1, "z"))


def shards(
    sizes,
    tokens,
    segments,
    cotangent,
    attn_gain,
    q_weight,
    k_weight,
    v_weight,
    query_gain,
    key_gain,
    o_weight,
    ffn_gain,
    gate_weight,
    up_weight,
    down_weight,
):
    y_size, x_size, c_size, z_size = sizes
    y, x, c, z = (lax.axis_index(name) for name in "yxcz")
    own_rows, width = tokens.shape
    part = q_weight.shape[0]
    parts = width // part
    pair, quad = c_size * part, x_size * c_size * part
    gain_part = query_gain.shape[0]
    head = gain_part * parts
    seq_count, length = segments.shape

    lanes = Lanes()

    pairs = []
    for low in range(0, z_size, 2):
        pairs += [(z_size + low, low + 1), (low + 1, z_size + low)]
    trades = (c + z) % 2 == 1

    def trade(value, lane):
        return jnp.where(trades, lanes.move(value, ("c", "z"), pairs, lane), value)

    tokens = trade(tokens, None)

    qt, kt, vt, ot = q_weight.T, k_weight.T, v_weight.T, o_weight.T
    q_rows, k_rows = qt.shape[0] // 2, kt.shape[0] // 2
    qkv_rows = q_rows + 2 * k_rows
    qkv_pack = jnp.concatenate([v.reshape(2, -1, part) for v in (qt, kt, vt, ot)], axis=1)
    qkv_pack = qkv_pack.reshape(-1, part)
    qkv_slots = [qkv_pack, *lanes.around([qkv_pack] * (z_size - 1), z_size, 1, "z")]

    sub = gate_weight.shape[1] // (x_size * c_size)
    ffn_pack = jnp.stack([v.T for v in (gate_weight, up_weight, down_weight)]).reshape(
        3, x_size, c_size, sub, part
    )
    mine = lax.dynamic_index_in_dim(ffn_pack, x, 1, keepdims=False)
    other = lax.dynamic_index_in_dim(ffn_pack, 1 - x, 1, keepdims=False)
    ffn_pack = by_index(x, mine, lanes.swap(other, "x"), -1)
    mine = lax.dynamic_index_in_dim(ffn_pack, c, 1, keepdims=False)
    other = lax.dynamic_index_in_dim(ffn_pack, 1 - c, 1, keepdims=False)
    ffn_ready = other
    other = lanes.swap(other, "c")
    ffn_own = jnp.concatenate(
        [
            by_index(c, mine[..., i * part : (i + 1) * part], other[..., i * part : (i + 1) * part], -1)
            for i in range(x_size)
        ],
        axis=-1,
    ).reshape(3 * sub, quad)

    gain_rows = jnp.concatenate(
        [attn_gain[None], ffn_gain[None]]
        + [jnp.pad(g, (0, part - gain_part))[None] for g in (query_gain, key_gain)]
        + [jnp.zeros((12, part), bf16)],
        axis=0,
    )
    numbers = segments.astype(bf16).reshape(-1, part)
    slot_rows = qkv_rows + q_rows

    def rows_of(core):
        return [lax.dynamic_slice_in_dim(v, core * slot_rows, slot_rows, 0) for v in qkv_slots]

    height = z_size * slot_rows + 16
    got = jnp.concatenate([*rows_of(1 - c), gain_rows, numbers], axis=0)
    got = lanes.swap(after(got, ffn_ready), "c")
    own = by_index(c, jnp.concatenate([*rows_of(c), gain_rows], axis=0), got[:height], -1)
    other_segments = got[height:].astype(jnp.int32).reshape(seq_count, length)

    all_tokens = by_index(c, tokens, lanes.swap(tokens, "c"), 0).astype(f32)
    gathered = [(i * slot_rows, qkv_rows, 0, i * qkv_rows) for i in range(z_size)]
    gathered += [(i * slot_rows + qkv_rows, q_rows, 2, i * q_rows) for i in range(z_size)]
    gathered += [(z_size * slot_rows, 16, 1, 0)]
    heights = (z_size * qkv_rows, 16, z_size * q_rows)
    qkv_full, gains, o_full = plane_gather(own, sizes, lanes, gathered, heights)
    gains = gains.astype(f32)
    gain_one, gain_two = gains[0:1], gains[1:2]
    gain_query, gain_key = (
        gains[i].reshape(parts, part)[:, :gain_part].reshape(1, head) for i in (2, 3)
    )
    head_gains = jnp.concatenate(
        [jnp.tile(gain_query, (1, 2)), jnp.tile(gain_key, (1, 2)), jnp.zeros((6, 2 * head), f32)], axis=0
    )

    half = width // 2
    pieces, wide = [ffn_own], []

    def over_y(piece):
        if y_size > 2:
            full = jnp.concatenate(list(lax.all_gather(piece, "y", axis=0)), axis=-1)
            wide.append((full[:, :half], full[:, half:]))
        else:
            wide.append((piece, lanes.swap(piece, "y")))

    over_y(ffn_own)
    for _ in range(1, z_size):
        pieces.append(lanes.move(pieces[-1], "z", ring(z_size), "z"))
        over_y(pieces[-1])
    near, far = [w[0] for w in wide], [w[1] for w in wide]
    cotangent = trade(cotangent, None)
    which = (y if y_size == 2 else y * 0).astype(jnp.int32).reshape(1)

    segment = lax.dynamic_index_in_dim(
        jnp.where(c == z % 2, segments, other_segments), z // 2, 0, keepdims=False
    )
    place = lax.broadcasted_iota(jnp.int32, (length,), 0) - jnp.sum(
        (segment[None, :] < segment[:, None]).astype(jnp.int32), axis=1
    )
    frequency = theta_base ** (-2.0 * jnp.arange(head // 2, dtype=f32) / head)
    angles = place.astype(f32)[:, None] * frequency
    cosine, sine = jnp.cos(angles), jnp.sin(angles)
    cosine = jnp.concatenate([cosine] * 4, axis=1)
    sine = jnp.concatenate([-sine, sine] * 2, axis=1)
    seg_col, seg_row = segment[:, None], segment[None, :]

    inputs = tokens.astype(f32)
    root_one = lax.rsqrt(jnp.mean(inputs * inputs, axis=-1, keepdims=True) + epsilon)
    hat_one = inputs * root_one
    all_root = lax.rsqrt(jnp.mean(all_tokens * all_tokens, axis=-1, keepdims=True) + epsilon)
    normed_one = (all_tokens * all_root * gain_one).astype(bf16)
    normed_one = after(normed_one, pieces[1])
    qkv = dot(normed_one, qkv_full, 1, 1).astype(bf16)
    qkv = after(qkv, cotangent)
    tables = (cosine, sine, seg_col, seg_row, head_gains, head)
    context = attend(qkv, *tables, 0, z_size // 2)
    qkv = after(qkv, context, pieces[z_size // 2], far[0])
    context = jnp.concatenate([context, attend(qkv, *tables, z_size // 2, z_size - z_size // 2)], axis=1)

    def half_rows(value, index):
        return lax.dynamic_slice_in_dim(value, index * own_rows, own_rows, 0)

    def core_reduce(left, right, right_dim):
        sent = dot(half_rows(left, 1 - c), right, 1, right_dim).astype(bf16)
        kept = dot(half_rows(left, c), right, 1, right_dim)
        return kept + lanes.swap(sent, "c").astype(f32)

    def spread(value, *earlier):
        across = lanes.swap(value, "x")
        over = lanes.swap(after(across, *earlier) if earlier else across, "c")
        return [value, lanes.swap(value, "c"), across, over]

    cots = spread(cotangent)
    mid = inputs + core_reduce(after(context, cots[2], far[1]), o_full, 0)
    root_two = lax.rsqrt(jnp.mean(mid * mid, axis=-1, keepdims=True) + epsilon)
    hat_two = mid * root_two
    normed_two = (hat_two * gain_two).astype(bf16)
    rows_two = spread(normed_two, far[-2])

    count = z_size // 2
    slot_grads, arrived = [None] * z_size, [None] * z_size

    def turn(group):
        return sorted(range(count), key=lambda i: (group * count + i - 1) % z_size)

    def send_gradients(sent, kept):
        if y_size > 2:
            full = jnp.concatenate([kept, sent], axis=1)
            full = jnp.stack([full[:, k * quad : (k + 1) * quad] for k in range(y_size)])
            got = lax.psum_scatter(full, "y", scatter_dimension=0, tiled=False)
            return got, got.astype(f32)
        got = lanes.swap(sent, "y")
        return got, plus(kept, got)

    gu_0, hid_0, sent, kept = ffn_first(which, near[:count], far[:count], rows_two, cots, turn(0))
    arrived[1], value = send_gradients(sent, kept)
    for i, slot in enumerate(turn(0)):
        slot_grads[slot] = value[i * 3 * sub : (i + 1) * 3 * sub]
    gu_1, hid_1, (first, second, third, fourth) = ffn_second(which, near, far, rows_two, cots, gu_0)
    third = plus(third, lanes.swap(fourth, "c")).astype(bf16)
    across = lanes.swap(third, "x")
    second = lanes.swap(second, "c")
    sent, kept, (out_first, out_second, out_third, out_fourth) = ffn_third(
        after(which, third), near, far, rows_two, cots, gu_1, hid_1, hid_0, turn(1)
    )
    for i in turn(1):
        lanes.last.pop("y", None)
        arrived[count + i], slot_grads[count + i] = send_gradients(sent[i], kept[i])
    ring_first = slot_grads[1].astype(bf16)
    total = lanes.move(ring_first, "z", ring(z_size), "z")
    grad_normed_two = after(plus(first, second, across), out_first)


    def norm_back(grad, hat, root):
        return root * (grad - hat * jnp.mean(grad * hat, axis=-1, keepdims=True))

    gain_two_part = jnp.sum(grad_normed_two * hat_two, axis=0)
    grad_mid = cotangent.astype(f32) + norm_back(grad_normed_two * gain_two, hat_two, root_two)

    branch_own = grad_mid.astype(bf16)
    branch = by_index(c, branch_own, lanes.swap(branch_own, "c"), 0)
    grad_context = dot(branch, o_full, 1, 1).astype(bf16)
    o_grad = dot(after(context, grad_context), branch, 0, 0).astype(bf16)
    grad_context = after(grad_context, o_grad, ring_first)
    grad_first, sums_first = attend_back(qkv, *tables[:-1], grad_context, head, 0, z_size // 2)
    out_third = plus(out_third, lanes.swap(out_fourth, "c")).astype(bf16)
    out_third = after(out_third, grad_normed_two)
    out_across = lanes.move(out_third, "x", [(0, 1), (1, 0)], None)
    output = mid + plus(out_first, lanes.swap(out_second, "c"), after(out_across, grad_first))
    output = output.astype(bf16)
    if y_size > 2:
        o_part = plane_scatter(o_grad, sizes, pair, lanes).astype(bf16)
        o_far = o_part
    else:
        block = lambda a, b: lane_block(o_grad, a * x_size + b, pair)
        o_far = lanes.move(block(1 - y, 1 - x), "x", [(0, 1), (1, 0)], None)
        o_near = lanes.move(block(y, 1 - x), "x", [(0, 1), (1, 0)], None)
        o_far = plus(block(1 - y, x), after(o_far, grad_first, output)).astype(bf16)
        o_part = plus(block(y, x), o_near)
    total = plus(after(total, grad_first), slot_grads[2]).astype(bf16)
    grad_last, sums_last = attend_back(
        qkv, *tables[:-1], after(grad_context, total, o_far), head, z_size // 2, z_size - z_size // 2
    )
    if y_size == 2:
        o_far = lanes.move(o_far, "y", [(0, 1), (1, 0)], None)
        o_part = plus(o_part, after(o_far, grad_last)).astype(bf16)
    total = lanes.move(total, "z", ring(z_size), "z")
    output_got = lanes.move(after(output, total), ("c", "z"), pairs, None)
    grad_last = after(grad_last, o_part, arrived[-1])
    for step in range(2, z_size - 1):
        total = plus(after(total, grad_last), slot_grads[step + 1]).astype(bf16)
        grad_last = after(grad_last, total)
        total = lanes.move(total, "z", ring(z_size), "z")
    total_last = plus(total, slot_grads[0])
    extra = [jnp.zeros((1, width), f32), gain_two_part[None], jnp.zeros((14, width), f32)]
    spaced = part < 2 * head
    if spaced:
        sums = jnp.sum(jnp.concatenate([sums_first, sums_last]).reshape(-1, 8, 2 * head), axis=0)
        extra[2:] = [
            jnp.pad(v.reshape(parts, gain_part), ((0, 0), (0, part - gain_part))).reshape(1, width)
            for v in (sums[0, :head] + sums[0, head:], sums[1, :head])
        ] + [jnp.zeros((12, width), f32)]
    extra = jnp.concatenate(extra, axis=0)
    if y_size > 2:
        starts = [which[0] + i * (width // 4) for i in range(4)]
    else:
        starts = [(a * x_size + b) * pair for a, b in ((1 - y, 1 - x), (y, 1 - x), (1 - y, x), (y, x))]
    blocks = qkv_grads(
        starts, (grad_first, grad_last), normed_one, qkv_full, extra, gain_one, (sums_first, sums_last), z_size, spaced
    )
    if y_size == 2:
        far_got = lanes.move(blocks[0], "x", [(0, 1), (1, 0)], None)
    grad_first = after(grad_first, blocks[3])
    cut = grad_first.shape[1]

    def two_terms(index):
        return dot(half_rows(grad_first, index), qkv_full[:cut], 1, 0) + dot(
            half_rows(grad_last, index), qkv_full[cut:], 1, 0
        )

    sent = two_terms(1 - c).astype(bf16)
    grad_normed_one = two_terms(c) + lanes.swap(sent, "c").astype(f32)
    tokens_grad = (grad_mid + norm_back(grad_normed_one * gain_one, hat_one, root_one)).astype(bf16)
    tokens_got = lanes.move(tokens_grad, ("c", "z"), pairs, None)
    if y_size > 2:
        qkv_part = plane_scatter(jnp.concatenate(blocks, axis=1), sizes, pair, lanes).astype(bf16)
    else:
        near_got = lanes.move(after(blocks[1], far_got), "x", [(0, 1), (1, 0)], None)
        lanes.last["x"] = (near_got,)
        far_sum = plus(blocks[2], far_got).astype(bf16)
        y_got = after(lanes.swap(far_sum, "y"), output_got, tokens_grad)
        qkv_part = plus(blocks[3], near_got, y_got).astype(bf16)

    def core_deal(value):
        kept = lane_block(value, c, part)
        sent = lanes.swap(lane_block(value, 1 - c, part), "c")
        return jnp.where(c == 0, jnp.stack([kept, sent]), jnp.stack([sent, kept]))

    wgrads = total_last.astype(bf16).reshape(3, sub, quad)
    kept = lane_block(wgrads, x, pair)
    sent = lanes.swap(lane_block(wgrads, 1 - x, pair), "x")
    dealt = sent
    wgrads = jnp.where(x == 0, jnp.stack([kept, sent], 1), jnp.stack([sent, kept], 1))
    kept = lane_block(wgrads, c, part)
    sent = lanes.swap(lane_block(wgrads, 1 - c, part), "c")
    wgrads = jnp.where(c == 0, jnp.stack([kept, sent], 2), jnp.stack([sent, kept], 2))
    wgrads = wgrads.reshape(3, x_size * c_size * sub, part)
    last_grads = wgrads


    rows = qkv_rows + 16
    lanes.last.pop("z", None)
    value = z_scatter(
        [
            jnp.concatenate(
                [qkv_part[i * rows : (i + 1) * rows], o_part[i * q_rows : (i + 1) * q_rows]], axis=0
            )
            for i in range(z_size)
        ],
        z_size,
        lanes,
    )
    value = after(value.astype(bf16), dealt)
    kept = lane_block(value, c, part)
    sent = lanes.swap(lane_block(value, 1 - c, part), "c")
    gain_sums = plus(kept[qkv_rows:rows], sent[qkv_rows:rows])
    qkv_grad = jnp.where(c == 0, jnp.stack([kept, sent]), jnp.stack([sent, kept])).astype(f32)
    o_wgrad = qkv_grad[:, rows:].reshape(2 * q_rows, part).T
    qkv_grad = qkv_grad[:, :qkv_rows]
    last_grads = after(last_grads, sent)
    gate_wgrad, up_wgrad, down_wgrad = (last_grads[i].astype(f32).T for i in range(3))
    q_wgrad = qkv_grad[:, :q_rows].reshape(-1, part).T
    k_wgrad = qkv_grad[:, q_rows : q_rows + k_rows].reshape(-1, part).T
    v_wgrad = qkv_grad[:, q_rows + k_rows :].reshape(-1, part).T
    if spaced:
        gain_query_sum, gain_key_sum = gain_sums[2, :gain_part], gain_sums[3, :gain_part]
    else:
        mine = ((y * x_size + x) * c_size + c) * gain_part
        gain_query_sum, gain_key_sum = (
            lax.dynamic_slice(gain_sums[2], (mine + at,), (gain_part,)) for at in (0, head)
        )
    return (
        jnp.where(trades, output_got, output),
        jnp.where(trades, tokens_got, tokens_grad),
        gain_sums[0],
        q_wgrad,
        k_wgrad,
        v_wgrad,
        gain_query_sum,
        gain_key_sum,
        o_wgrad,
        gain_sums[1],
        gate_wgrad,
        up_wgrad,
        down_wgrad,
    )


def solution(mesh):
    dp, tp = mesh.devices.shape
    sizes = (dp // 4, 2, 2, tp)
    fine = Mesh(mesh.devices.reshape(sizes), ("y", "x", "c", "z"))
    d = ("y", "x", "c")
    rows, weight, gain = P((*d, "z"), None), P(d, "z"), P(d)
    return jax.shard_map(
        functools.partial(shards, sizes),
        mesh=fine,
        in_specs=(rows, P(d, None), rows, gain, weight, weight, weight, gain, gain, weight, gain)
        + (weight,) * 3,
        out_specs=(rows, rows, gain, weight, weight, weight, gain, gain, weight, gain) + (weight,) * 3,
        check_vma=False,
    )
```

```python
import functools

import jax
import jax.numpy as jnp
from jax import lax
from jax.experimental import pallas as pl
from jax.experimental.pallas import tpu as pltpu
from jax.sharding import Mesh, PartitionSpec as P

epsilon = 1e-05
theta_base = 1000000.0
bf16 = jnp.bfloat16
f32 = jnp.float32
tile = 256
span = 512


def cost(flops):
    return pl.CostEstimate(flops=flops // 1000, bytes_accessed=10**5, transcendentals=0)


def dot(left, right, left_dim, right_dim):
    return lax.dot_general(
        left, right, (((left_dim,), (right_dim,)), ((), ())), preferred_element_type=f32
    )


def group_sum(value, ones):
    high = value.astype(bf16)
    low = (value - high.astype(f32)).astype(bf16)
    return dot(high, ones, 1, 0) + dot(low, ones, 1, 0)


def ones_by_head(lanes, head):
    row = lax.broadcasted_iota(jnp.int32, (lanes, lanes), 0) // head
    col = lax.broadcasted_iota(jnp.int32, (lanes, lanes), 1) // head
    return jnp.where(row == col, 1.0, 0.0).astype(bf16)


def half_swap(value, head):
    lanes = value.shape[-1]
    lane = lax.broadcasted_iota(jnp.int32, value.shape, 1) % head
    return jnp.where(
        lane < head // 2,
        pltpu.roll(value, lanes - head // 2, 1),
        pltpu.roll(value, head // 2, 1),
    )


def head_norm(raw, ones, head):
    root = lax.rsqrt(group_sum(raw * raw, ones) * (1.0 / head) + epsilon)
    return raw * root, root


def split_block(block, head):
    lanes = 2 * head
    queries = block[:, :lanes]
    both = block[:, lanes:]
    other = pltpu.roll(both, head, 1)
    first = lax.broadcasted_iota(jnp.int32, both.shape, 1) < head
    keys = jnp.where(first, both, other)
    values = jnp.where(first, other, both)
    return queries, keys, values


def stack_heads(block, head):
    first = lax.broadcasted_iota(jnp.int32, block.shape, 1) < head
    zero = jnp.zeros_like(block)
    return jnp.concatenate([jnp.where(first, block, zero), jnp.where(first, zero, block)], axis=0)


def merge_heads(stacked, head):
    half = stacked.shape[0] // 2
    first = lax.broadcasted_iota(jnp.int32, (half, stacked.shape[1]), 1) < head
    return jnp.where(first, stacked[:half], stacked[half:])


def attend_kernel(head, qkv_ref, cos_ref, sin_ref, seg_col, seg_row, gain_ref, ctx_ref, q_s, k_s, v_s):
    length = qkv_ref.shape[0]
    lanes = 2 * head
    ones = ones_by_head(lanes, head)
    queries, keys, values = split_block(qkv_ref[...].astype(f32), head)
    cosine, sine = cos_ref[...], sin_ref[...]

    def rotated(raw, gain):
        hat, _ = head_norm(raw, ones, head)
        scaled = hat * gain
        return (scaled * cosine + half_swap(scaled, head) * sine).astype(bf16)

    q_s[...] = rotated(queries, gain_ref[0:1, :]) * jnp.asarray(head**-0.5, bf16)
    k_s[...] = rotated(keys, gain_ref[1:2, :])
    v_s[...] = values.astype(bf16)
    for top in range(0, length, tile):
        low, high = max(0, top - span), top + tile
        stacked = stack_heads(q_s[top:high, :], head)
        scores = dot(stacked, k_s[low:high, :], 1, 1)
        row = lax.broadcasted_iota(jnp.int32, (tile, high - low), 0) + top
        col = lax.broadcasted_iota(jnp.int32, (tile, high - low), 1) + low
        allowed = (seg_col[top:high, 0:1] == seg_row[0:1, low:high]) & (row >= col)
        allowed = jnp.concatenate([allowed, allowed], axis=0)
        exponent = jnp.where(allowed, jnp.exp(scores), 0.0)
        total = jnp.sum(exponent, axis=1, keepdims=True)
        mixed = dot(exponent.astype(bf16), v_s[low:high, :], 1, 0) / total
        ctx_ref[top:high, :] = merge_heads(mixed, head).astype(bf16)


def attend(qkv, cosine, sine, seg_col, seg_row, gains, head, first, groups):
    length = qkv.shape[0]
    lanes = 2 * head
    whole = lambda shape: pl.BlockSpec(shape, lambda j: (0, 0))
    return pl.pallas_call(
        functools.partial(attend_kernel, head),
        grid=(groups,),
        in_specs=[
            pl.BlockSpec((length, 2 * lanes), lambda j: (0, j + first)),
            whole((length, lanes)),
            whole((length, lanes)),
            whole((length, 1)),
            whole((1, length)),
            whole((8, lanes)),
        ],
        out_specs=pl.BlockSpec((length, lanes), lambda j: (0, j)),
        out_shape=jax.ShapeDtypeStruct((length, groups * lanes), bf16),
        scratch_shapes=[pltpu.VMEM((length, lanes), bf16)] * 3,
        compiler_params=pltpu.CompilerParams(vmem_limit_bytes=24 * 2**20),
        cost_estimate=cost(6 * 10**9),
        name="attend",
    )(qkv, cosine, sine, seg_col, seg_row, gains)


def attend_back_kernel(
    head, qkv_ref, cos_ref, sin_ref, seg_col, seg_row, gain_ref, do_ref, out_ref, sums_ref,
    q_s, k_s, v_s, dk_s, dv_s, dq_s,
):
    length = qkv_ref.shape[0]
    lanes = 2 * head
    ones = ones_by_head(lanes, head)
    queries, keys, values = split_block(qkv_ref[...].astype(f32), head)
    cosine, sine = cos_ref[...], sin_ref[...]

    def rotated(raw, gain):
        hat, _ = head_norm(raw, ones, head)
        scaled = hat * gain
        return (scaled * cosine + half_swap(scaled, head) * sine).astype(bf16)

    scale = jnp.asarray(head**-0.5, bf16)
    q_s[...] = rotated(queries, gain_ref[0:1, :]) * scale
    k_s[...] = rotated(keys, gain_ref[1:2, :])
    v_s[...] = values.astype(bf16)
    dk_s[...] = jnp.zeros_like(dk_s)
    dv_s[...] = jnp.zeros_like(dv_s)
    for top in range(0, length, tile):
        low, high = max(0, top - span), top + tile
        stacked = stack_heads(q_s[top:high, :], head)
        grads = stack_heads(do_ref[top:high, :], head)
        near_k, near_v = k_s[low:high, :], v_s[low:high, :]
        scores = dot(near_k, stacked, 1, 1)
        col = lax.broadcasted_iota(jnp.int32, (high - low, tile), 0) + low
        row = lax.broadcasted_iota(jnp.int32, (high - low, tile), 1) + top
        allowed = (seg_col[low:high, 0:1] == seg_row[0:1, top:high]) & (row >= col)
        allowed = jnp.concatenate([allowed, allowed], axis=1)
        exponent = jnp.where(allowed, jnp.exp(scores), 0.0)
        probs = exponent * (1.0 / jnp.sum(exponent, axis=0, keepdims=True))
        grad_probs = dot(near_v, grads, 1, 1)
        weighted = probs * grad_probs
        delta = jnp.sum(weighted, axis=0, keepdims=True)
        grad_scores = (weighted - probs * delta).astype(bf16)
        dv_s[low:high, :] += dot(probs.astype(bf16), grads, 1, 0)
        dk_s[low:high, :] += dot(grad_scores, stacked, 1, 0)
        dq_s[top:high, :] = merge_heads(dot(grad_scores, near_k, 0, 0), head) * head**-0.5

    def back(raw, gain, grad):
        hat, root = head_norm(raw, ones, head)
        normed = grad * cosine - half_swap(grad, head) * sine
        gain_part = jnp.sum(normed * hat, axis=0, keepdims=True)
        scaled = normed * gain
        mean = group_sum(scaled * hat, ones) * (1.0 / head)
        return root * (scaled - hat * mean), gain_part

    grad_q, q_sum = back(queries, gain_ref[0:1, :], dq_s[...])
    folded_k = dk_s[...] + pltpu.roll(dk_s[...], head, 1)
    grad_k, k_sum = back(keys, gain_ref[1:2, :], folded_k)
    folded_v = dv_s[...] + pltpu.roll(dv_s[...], head, 1)
    first = lax.broadcasted_iota(jnp.int32, (length, lanes), 1) < head
    out_ref[:, :lanes] = grad_q.astype(bf16)
    out_ref[:, lanes:] = jnp.where(first, grad_k, folded_v).astype(bf16)
    which = lax.broadcasted_iota(jnp.int32, sums_ref.shape, 0)
    sums_ref[...] = jnp.where(which == 0, q_sum, jnp.where(which == 1, k_sum, 0.0))


def attend_back(qkv, cosine, sine, seg_col, seg_row, gains, grad_context, head, first, groups):
    length = qkv.shape[0]
    lanes = 2 * head
    whole = lambda shape: pl.BlockSpec(shape, lambda j: (0, 0))
    return pl.pallas_call(
        functools.partial(attend_back_kernel, head),
        grid=(groups,),
        in_specs=[
            pl.BlockSpec((length, 2 * lanes), lambda j: (0, j + first)),
            whole((length, lanes)),
            whole((length, lanes)),
            whole((length, 1)),
            whole((1, length)),
            whole((8, lanes)),
            pl.BlockSpec((length, lanes), lambda j: (0, j + first)),
        ],
        out_specs=(
            pl.BlockSpec((length, 2 * lanes), lambda j: (0, j)),
            pl.BlockSpec((8, lanes), lambda j: (j, 0)),
        ),
        out_shape=(
            jax.ShapeDtypeStruct((length, groups * 2 * lanes), bf16),
            jax.ShapeDtypeStruct((8 * groups, lanes), f32),
        ),
        scratch_shapes=[pltpu.VMEM((length, lanes), bf16)] * 3 + [pltpu.VMEM((length, lanes), f32)] * 3,
        compiler_params=pltpu.CompilerParams(vmem_limit_bytes=28 * 2**20),
        cost_estimate=cost(12 * 10**9),
        name="attend_back",
    )(qkv, cosine, sine, seg_col, seg_row, gains, grad_context)


def pull(pairs, sems, start):
    copies = [pltpu.make_async_copy(s, d, sems.at[start + i]) for i, (s, d) in enumerate(pairs)]
    for copy in copies:
        copy.start()
    return copies


def finish(copies):
    for copy in copies:
        copy.wait()


def halves(which_ref, half):
    first = pl.multiple_of(which_ref[0] * half, half)
    second = pl.multiple_of((1 - which_ref[0]) * half, half)
    return pl.ds(first, half), pl.ds(second, half)


def call_local(kernel, which, arrays, outs, out_spaces, scratch, copies, flops, name, limit=58):
    return pl.pallas_call(
        kernel,
        in_specs=[pl.BlockSpec(memory_space=pltpu.SMEM)] + [pl.BlockSpec(memory_space=pltpu.HBM)] * len(arrays),
        out_specs=[pl.BlockSpec(memory_space=space) for space in out_spaces],
        out_shape=outs,
        scratch_shapes=[*scratch, pltpu.SemaphoreType.DMA((copies,))],
        compiler_params=pltpu.CompilerParams(vmem_limit_bytes=limit * 2**20),
        cost_estimate=cost(flops),
        name=name,
    )(which, *arrays)


class Loads:
    def __init__(self, sems):
        self.sems, self.count, self.open = sems, 0, {}

    def start(self, key, *pairs):
        for source, target in pairs:
            copy = pltpu.make_async_copy(source, target, self.sems.at[self.count])
            copy.start()
            self.open.setdefault(key, []).append(copy)
            self.count += 1

    def wait(self, *keys):
        for key in keys:
            for copy in self.open.pop(key, ()):
                copy.wait()

    def close(self):
        self.wait(*list(self.open))


def load_gate_up(loads, key, near, far, which_ref, target, slots):
    size, half = near[0].shape
    top = 2 * size // 3
    for at, i in enumerate(slots):
        for pieces, lanes in zip((near, far), halves(which_ref, half)):
            loads.start((key, at), (pieces[i].at[pl.ds(0, top)], target.at[pl.ds(at * top, top), lanes]))


def load_down(loads, key, near, far, which_ref, target, slots):
    size, half = near[0].shape
    rest = size // 3
    for at, i in enumerate(slots):
        for pieces, lanes in zip((near, far), halves(which_ref, half)):
            loads.start(
                (key, at), (pieces[i].at[pl.ds(size - rest, rest)], target.at[pl.ds(at * rest, rest), lanes])
            )


def hidden_step(gate_up, down, rows, cot, gu_s, hid_s, slot, columns, sub):
    both = dot(gate_up[2 * slot * sub : 2 * (slot + 1) * sub, :], rows, 1, 1)
    back = dot(down[slot * sub : (slot + 1) * sub, :], cot, 1, 1)
    gate, up = both[:sub], both[sub:]
    sig = 0.5 * jnp.tanh(0.5 * gate) + 0.5
    act = gate * sig
    base = 2 * slot * sub
    gu_s[base : base + sub, columns] = (back * up * (sig + act * (1.0 - sig))).astype(bf16)
    gu_s[base + sub : base + 2 * sub, columns] = (back * act).astype(bf16)
    hid_s[slot * sub : (slot + 1) * sub, columns] = (act * up).astype(bf16)


def weight_step(loads, which_ref, gu_s, hid_s, rows_s, cot_s, out_s, far_out, near_out, order, sub):
    size, half = 3 * sub, rows_s.shape[1] // 2
    first, second = halves(which_ref, half)
    for side, lanes, outs in ((0, second, far_out), (1, first, near_out)):
        rows, cots = rows_s[:, lanes], cot_s[:, lanes]
        for at, s in enumerate(order):
            out_s[side, s, : 2 * sub] = dot(gu_s[2 * s * sub : 2 * (s + 1) * sub, :], rows, 1, 0).astype(bf16)
            out_s[side, s, 2 * sub :] = dot(hid_s[s * sub : (s + 1) * sub, :], cots, 1, 0).astype(bf16)
            target = outs[s] if len(outs) > 1 else outs[0].at[pl.ds(at * size, size)]
            loads.start("out", (out_s.at[side, s], target))


def take(refs, *counts):
    at, out = 0, []
    for count in counts:
        out.append(refs[at : at + count])
        at += count
    return (*out, refs[at:])


def first_kernel(slots, quarters, order, which_ref, *refs):
    near, far, rows, cots, (gu_out, hid_out), far_out, near_out, rest = take(
        refs, slots, slots, quarters, quarters, 2, 1, 1
    )
    gate_up, down, rows_s, cot_s, gu_s, hid_s, out_s, sems = rest
    sub, count = near[0].shape[0] // 3, rows[0].shape[0]
    loads = Loads(sems)
    for q in range(max(slots, quarters)):
        if q < quarters:
            place = pl.ds(q * count, count)
            loads.start(("rows", q), (rows[q], rows_s.at[place]), (cots[q], cot_s.at[place]))
        if q == 0:
            load_gate_up(loads, "w", near, far, which_ref, gate_up, range(slots))
            load_down(loads, "w", near, far, which_ref, down, range(slots))
    for q in range(quarters):
        columns = slice(q * count, (q + 1) * count)
        loads.wait(("rows", q))
        for s in range(slots):
            loads.wait(("w", s))
            hidden_step(gate_up, down, rows_s[columns, :], cot_s[columns, :], gu_s, hid_s, s, columns, sub)
    loads.start("out", (gu_s, gu_out), (hid_s, hid_out))
    weight_step(loads, which_ref, gu_s, hid_s, rows_s, cot_s, out_s, far_out, near_out, order, sub)
    loads.close()


def ffn_first(which, near, far, rows, cots, order):
    slots, quarters = len(near), len(rows)
    size, half = near[0].shape
    sub, count = size // 3, rows[0].shape[0]
    tokens = quarters * count
    gu, hid = (2 * slots * sub, tokens), (slots * sub, tokens)
    out = call_local(
        functools.partial(first_kernel, slots, quarters, order),
        which,
        [*near, *far, *rows, *cots],
        [jax.ShapeDtypeStruct(v, bf16) for v in (gu, hid)]
        + [jax.ShapeDtypeStruct((slots * size, half), bf16)] * 2,
        [pl.ANY] * 4,
        [
            pltpu.VMEM((2 * slots * sub, 2 * half), bf16),
            pltpu.VMEM((slots * sub, 2 * half), bf16),
            pltpu.VMEM((tokens, 2 * half), bf16),
            pltpu.VMEM((tokens, 2 * half), bf16),
            pltpu.VMEM(gu, bf16),
            pltpu.VMEM(hid, bf16),
            pltpu.VMEM((2, slots, size, half), bf16),
        ],
        2 * quarters + 4 * slots + 2 + 2 * slots,
        8 * slots * size * half * tokens,
        "ffn_first",
    )
    return out


def second_kernel(slots, quarters, which_ref, *refs):
    near, far, rows, cots, (gu_0,), (gu_out, hid_out), outs, rest = take(
        refs, 2 * slots, 2 * slots, quarters, quarters, 1, 2, quarters
    )
    gate_up, down, gate_up_0, rows_s, cot_s, gu_s, hid_s, gu_0s, out_s, sems = rest
    sub, count = near[0].shape[0] // 3, rows[0].shape[0]
    loads = Loads(sems)
    for q in range(quarters):
        place = pl.ds(q * count, count)
        loads.start(("rows", q), (rows[q], rows_s.at[place]), (cots[q], cot_s.at[place]))
        if q == 0:
            load_gate_up(loads, "w", near, far, which_ref, gate_up, range(slots, 2 * slots))
            load_down(loads, "w", near, far, which_ref, down, range(slots, 2 * slots))
    load_gate_up(loads, "w0", near, far, which_ref, gate_up_0, range(slots))
    loads.start("g0", (gu_0, gu_0s))
    for q in range(quarters):
        columns = slice(q * count, (q + 1) * count)
        loads.wait(("rows", q))
        for s in range(slots):
            loads.wait(("w", s))
            hidden_step(gate_up, down, rows_s[columns, :], cot_s[columns, :], gu_s, hid_s, s, columns, sub)
    loads.start("out", (gu_s, gu_out), (hid_s, hid_out))
    loads.wait("g0", *(("w0", s) for s in range(slots)))
    for q in range(quarters):
        columns = slice(q * count, (q + 1) * count)
        total = dot(gu_0s[:, columns], gate_up_0[...], 0, 0) + dot(gu_s[:, columns], gate_up[...], 0, 0)
        out_s[q] = total.astype(bf16)
        loads.start("out", (out_s.at[q], outs[q]))
    loads.close()


def ffn_second(which, near, far, rows, cots, gu_0):
    slots, quarters = len(near) // 2, len(rows)
    size, half = near[0].shape
    sub, count = size // 3, rows[0].shape[0]
    tokens = quarters * count
    gu, hid = (2 * slots * sub, tokens), (slots * sub, tokens)
    out = call_local(
        functools.partial(second_kernel, slots, quarters),
        which,
        [*near, *far, *rows, *cots, gu_0],
        [jax.ShapeDtypeStruct(v, bf16) for v in (gu, hid)]
        + [jax.ShapeDtypeStruct((count, 2 * half), bf16)] * quarters,
        [pl.ANY] * (2 + quarters),
        [
            pltpu.VMEM((2 * slots * sub, 2 * half), bf16),
            pltpu.VMEM((slots * sub, 2 * half), bf16),
            pltpu.VMEM((2 * slots * sub, 2 * half), bf16),
            pltpu.VMEM((tokens, 2 * half), bf16),
            pltpu.VMEM((tokens, 2 * half), bf16),
            pltpu.VMEM(gu, bf16),
            pltpu.VMEM(hid, bf16),
            pltpu.VMEM(gu, bf16),
            pltpu.VMEM((quarters, count, 2 * half), bf16),
        ],
        3 * quarters + 6 * slots + 3,
        10 * slots * size * half * tokens,
        "ffn_second",
    )
    return out[0], out[1], out[2:]


def third_kernel(slots, quarters, order, which_ref, *refs):
    near, far, rows, cots, (gu, hid, hid_0), far_out, near_out, outs, rest = take(
        refs, 2 * slots, 2 * slots, quarters, quarters, 3, slots, slots, quarters
    )
    down, rows_s, cot_s, gu_s, hid_s, hid_0s, grad_s, out_s, sems = rest
    sub, count = far_out[0].shape[0] // 3, rows[0].shape[0]
    loads = Loads(sems)
    load_down(loads, "w", near, far, which_ref, down, range(2 * slots))
    loads.start("h", (hid_0, hid_0s), (hid, hid_s))
    loads.start("rows", (gu, gu_s))
    for q in range(quarters):
        place = pl.ds(q * count, count)
        loads.start("rows", (rows[q], rows_s.at[place]), (cots[q], cot_s.at[place]))
    loads.wait("h", *(("w", s) for s in range(2 * slots)))
    for q in range(quarters):
        columns = slice(q * count, (q + 1) * count)
        total = dot(hid_0s[:, columns], down[: slots * sub, :], 0, 0)
        total = total + dot(hid_s[:, columns], down[slots * sub :, :], 0, 0)
        out_s[q] = total.astype(bf16)
        loads.start("out", (out_s.at[q], outs[q]))
    loads.wait("rows")
    weight_step(loads, which_ref, gu_s, hid_s, rows_s, cot_s, grad_s, far_out, near_out, order, sub)
    loads.close()


def ffn_third(which, near, far, rows, cots, gu, hid, hid_0, order):
    slots, quarters = len(order), len(rows)
    size, half = near[0].shape
    sub, count = size // 3, rows[0].shape[0]
    tokens = quarters * count
    out = call_local(
        functools.partial(third_kernel, slots, quarters, order),
        which,
        [*near, *far, *rows, *cots, gu, hid, hid_0],
        [jax.ShapeDtypeStruct((size, half), bf16)] * (2 * slots)
        + [jax.ShapeDtypeStruct((count, 2 * half), bf16)] * quarters,
        [pl.ANY] * (2 * slots + quarters),
        [
            pltpu.VMEM((2 * slots * sub, 2 * half), bf16),
            pltpu.VMEM((tokens, 2 * half), bf16),
            pltpu.VMEM((tokens, 2 * half), bf16),
            pltpu.VMEM((2 * slots * sub, tokens), bf16),
            pltpu.VMEM((slots * sub, tokens), bf16),
            pltpu.VMEM((slots * sub, tokens), bf16),
            pltpu.VMEM((2, slots, size, half), bf16),
            pltpu.VMEM((quarters, count, 2 * half), bf16),
        ],
        3 * quarters + 4 * slots + 3 + 2 * slots,
        6 * slots * size * half * tokens,
        "ffn_third",
    )
    return out[:slots], out[slots : 2 * slots], out[2 * slots :]


def qkv_grads_kernel(groups, spaced, starts_ref, grads_0, grads_1, rows, weights, extra_ref, gain_ref, sums_0, sums_1, *refs):
    outs, rest = refs[: len(refs) - 8], refs[len(refs) - 8 :]
    grad_s, rows_s, weight_s, extra_s, gain_s, sums_s, out_s, sems = rest
    size = (grads_0.shape[1] + grads_1.shape[1]) // groups
    width = outs[0].shape[1]
    more = extra_ref.shape[0]
    cut = grads_0.shape[1]
    loads = Loads(sems)
    loads.start("a", (grads_0, grad_s.at[:, pl.ds(0, cut)]), (grads_1, grad_s.at[:, pl.ds(cut, grads_1.shape[1])]))
    loads.start("a", (rows, rows_s))
    loads.start("b", (weights.at[pl.ds(0, groups * size)], weight_s), (extra_ref, extra_s), (gain_ref, gain_s))
    loads.start("b", (sums_0, sums_s.at[pl.ds(0, sums_0.shape[0])]))
    loads.start("b", (sums_1, sums_s.at[pl.ds(sums_0.shape[0], sums_1.shape[0])]))
    loads.wait("a")
    for i in range(len(outs)):
        lanes = pl.ds(pl.multiple_of(starts_ref[i], width), width)
        block = dot(grad_s[...], rows_s[:, lanes], 0, 0)
        if i == 0:
            loads.wait("b")
        gain_row = jnp.sum(block * weight_s[:, lanes].astype(f32), axis=0, keepdims=True)
        gain_row = gain_row / gain_s[0:1, lanes]
        row = lax.broadcasted_iota(jnp.int32, (more, width), 0)
        extra = jnp.where(row == 0, gain_row, extra_s[:, lanes])
        if not spaced:
            sums = sums_s[0:8, :]
            for g in range(1, groups):
                sums = sums + sums_s[8 * g : 8 * (g + 1), :]
            head = sums.shape[1] // 2
            query = sums[0:1, :] + pltpu.roll(sums[0:1, :], head, 1)
            lane = lax.broadcasted_iota(jnp.int32, query.shape, 1)
            both = jnp.where(lane < head, query, pltpu.roll(sums[1:2, :], head, 1))
            both = jnp.concatenate([both] * (width // (2 * head)), axis=1)
            extra = jnp.where(row == 2, both, extra)
        extra = extra.astype(bf16)
        for g in range(groups):
            base = g * (size + more)
            out_s[i, base : base + size, :] = block[g * size : (g + 1) * size, :].astype(bf16)
            out_s[i, base + size : base + size + more, :] = extra
        loads.start("out", (out_s.at[i], outs[i]))
    loads.close()


def qkv_grads(starts, grads, rows, weights, extra, gains, sums, groups, spaced):
    count, width = rows.shape
    columns, more = grads[0].shape[1] + grads[1].shape[1], extra.shape[0]
    block, blocks = (columns + groups * more, width // 4), len(starts)
    return call_local(
        functools.partial(qkv_grads_kernel, groups, spaced),
        jnp.stack(starts).astype(jnp.int32),
        [*grads, rows, weights, extra, gains, *sums],
        [jax.ShapeDtypeStruct(block, bf16)] * blocks,
        [pl.ANY] * blocks,
        [
            pltpu.VMEM((count, columns), bf16),
            pltpu.VMEM((count, width), bf16),
            pltpu.VMEM((columns, width), bf16),
            pltpu.VMEM((more, width), f32),
            pltpu.VMEM(gains.shape, f32),
            pltpu.VMEM((8 * groups, sums[0].shape[1]), f32),
            pltpu.VMEM((blocks, *block), bf16),
        ],
        8 + blocks,
        10**9,
        "qkv_grads",
    )


def place_kernel(count, parts, starts_ref, *refs):
    width = refs[0].shape[1]
    loads = Loads(refs[-1])
    for i in range(count):
        lanes = pl.ds(pl.multiple_of(starts_ref[i], width), width)
        for low, rows, out, place in parts:
            target = refs[count + out].at[pl.ds(place, rows), lanes]
            loads.start("a", (refs[i].at[pl.ds(low, rows)], target))
    loads.close()


def place_lanes(blocks, starts, parts, sizes):
    width = len(blocks) * blocks[0].shape[1]
    return call_local(
        functools.partial(place_kernel, len(blocks), parts),
        jnp.stack(starts).astype(jnp.int32),
        blocks,
        [jax.ShapeDtypeStruct((rows, width), bf16) for rows in sizes],
        [pl.ANY] * len(sizes),
        [],
        len(blocks) * len(parts),
        10**9,
        "place_lanes",
        4,
    )


def after(value, *earlier):
    return lax.optimization_barrier((value, *earlier))[0]


def ring(size, step=1):
    return [(i, (i + step) % size) for i in range(size)]


class Lanes:
    def __init__(self):
        self.last = {}

    def wait(self, value, lane):
        return after(value, *self.last.get(lane, ())) if lane in self.last else value

    def move(self, value, axes, pairs, lane):
        got = lax.ppermute(self.wait(value, lane), axes, pairs)
        if lane:
            self.last[lane] = (got,)
        return got

    def swap(self, value, axis):
        return self.move(value, axis, [(0, 1), (1, 0)], None if axis == "c" else axis)

    def around(self, values, size, signs, lane):
        held = [self.wait(value, lane) for value in values]
        got = [lax.ppermute(v, "z", ring(size, signs * (i + 1))) for i, v in enumerate(held)]
        self.last[lane] = tuple(got)
        return got


def by_index(index, first, second, axis):
    return jnp.where(
        index == 0,
        jnp.concatenate([first, second], axis=axis),
        jnp.concatenate([second, first], axis=axis),
    )


def lane_block(value, index, width):
    start = [0] * (value.ndim - 1) + [index * width]
    return lax.dynamic_slice(value, start, (*value.shape[:-1], width))


def plus(left, *right):
    total = left.astype(f32)
    for value in right:
        total = total + value.astype(f32)
    return total


def plane_gather(value, sizes, lanes, parts, heights):
    y_size, x_size = sizes[:2]
    y, x = lax.axis_index("y"), lax.axis_index("x")
    if y_size > 2:
        wide = by_index(x, value, lanes.swap(value, "x"), -1)
        wide = lax.all_gather(wide, "y", axis=0)
        wide = jnp.concatenate([wide[i] for i in range(y_size)], axis=-1)
        return [
            jnp.concatenate([wide[low : low + rows] for low, rows, to, _ in parts if to == out], axis=0)
            for out in range(len(heights))
        ]
    width = value.shape[1]
    far = lanes.swap(value, "y")
    blocks = [value, lanes.swap(value, "x"), far, lanes.swap(far, "x")]
    starts = [(a * x_size + b) * width for a in (y, 1 - y) for b in (x, 1 - x)]
    return place_lanes(blocks, starts, parts, heights)


def plane_scatter(value, sizes, pair, lanes):
    y_size, x_size = sizes[:2]
    y, x = lax.axis_index("y"), lax.axis_index("x")
    block = lambda y_at, x_at: lane_block(value, y_at * x_size + x_at, pair)
    if y_size > 2:
        per_y = [plus(block(i, x), lanes.swap(block(i, 1 - x), "x")).astype(bf16) for i in range(y_size)]
        return lax.psum_scatter(jnp.stack(per_y), "y", scatter_dimension=0, tiled=False).astype(f32)
    far = plus(block(1 - y, x), lanes.swap(block(1 - y, 1 - x), "x")).astype(bf16)
    near = lanes.swap(block(y, 1 - x), "x")
    return plus(block(y, x), near, lanes.swap(far, "y"))


def z_scatter(blocks, size, lanes):
    return plus(blocks[0], *lanes.around(blocks[1:], size, -1, "z"))


def shards(
    sizes,
    tokens,
    segments,
    cotangent,
    attn_gain,
    q_weight,
    k_weight,
    v_weight,
    query_gain,
    key_gain,
    o_weight,
    ffn_gain,
    gate_weight,
    up_weight,
    down_weight,
):
    y_size, x_size, c_size, z_size = sizes
    y, x, c, z = (lax.axis_index(name) for name in "yxcz")
    own_rows, width = tokens.shape
    part = q_weight.shape[0]
    parts = width // part
    pair, quad = c_size * part, x_size * c_size * part
    gain_part = query_gain.shape[0]
    head = gain_part * parts
    seq_count, length = segments.shape

    lanes = Lanes()

    pairs = []
    for low in range(0, z_size, 2):
        pairs += [(z_size + low, low + 1), (low + 1, z_size + low)]
    trades = (c + z) % 2 == 1

    def trade(value, lane):
        return jnp.where(trades, lanes.move(value, ("c", "z"), pairs, lane), value)

    tokens = trade(tokens, None)

    qt, kt, vt, ot = q_weight.T, k_weight.T, v_weight.T, o_weight.T
    q_rows, k_rows = qt.shape[0] // 2, kt.shape[0] // 2
    qkv_rows = q_rows + 2 * k_rows
    qkv_pack = jnp.concatenate([v.reshape(2, -1, part) for v in (qt, kt, vt, ot)], axis=1)
    qkv_pack = qkv_pack.reshape(-1, part)
    qkv_slots = [qkv_pack, *lanes.around([qkv_pack] * (z_size - 1), z_size, 1, "z")]

    sub = gate_weight.shape[1] // (x_size * c_size)
    ffn_pack = jnp.stack([v.T for v in (gate_weight, up_weight, down_weight)]).reshape(
        3, x_size, c_size, sub, part
    )
    mine = lax.dynamic_index_in_dim(ffn_pack, x, 1, keepdims=False)
    other = lax.dynamic_index_in_dim(ffn_pack, 1 - x, 1, keepdims=False)
    ffn_pack = by_index(x, mine, lanes.swap(other, "x"), -1)
    mine = lax.dynamic_index_in_dim(ffn_pack, c, 1, keepdims=False)
    other = lax.dynamic_index_in_dim(ffn_pack, 1 - c, 1, keepdims=False)
    ffn_ready = other
    other = lanes.swap(other, "c")
    ffn_own = jnp.concatenate(
        [
            by_index(c, mine[..., i * part : (i + 1) * part], other[..., i * part : (i + 1) * part], -1)
            for i in range(x_size)
        ],
        axis=-1,
    ).reshape(3 * sub, quad)

    gain_rows = jnp.concatenate(
        [attn_gain[None], ffn_gain[None]]
        + [jnp.pad(g, (0, part - gain_part))[None] for g in (query_gain, key_gain)]
        + [jnp.zeros((12, part), bf16)],
        axis=0,
    )
    numbers = segments.astype(bf16).reshape(-1, part)
    slot_rows = qkv_rows + q_rows

    def rows_of(core):
        return [lax.dynamic_slice_in_dim(v, core * slot_rows, slot_rows, 0) for v in qkv_slots]

    height = z_size * slot_rows + 16
    got = jnp.concatenate([*rows_of(1 - c), gain_rows, numbers], axis=0)
    got = lanes.swap(after(got, ffn_ready), "c")
    own = by_index(c, jnp.concatenate([*rows_of(c), gain_rows], axis=0), got[:height], -1)
    other_segments = got[height:].astype(jnp.int32).reshape(seq_count, length)

    all_tokens = by_index(c, tokens, lanes.swap(tokens, "c"), 0).astype(f32)
    gathered = [(i * slot_rows, qkv_rows, 0, i * qkv_rows) for i in range(z_size)]
    gathered += [(i * slot_rows + qkv_rows, q_rows, 2, i * q_rows) for i in range(z_size)]
    gathered += [(z_size * slot_rows, 16, 1, 0)]
    heights = (z_size * qkv_rows, 16, z_size * q_rows)
    qkv_full, gains, o_full = plane_gather(own, sizes, lanes, gathered, heights)
    gains = gains.astype(f32)
    gain_one, gain_two = gains[0:1], gains[1:2]
    gain_query, gain_key = (
        gains[i].reshape(parts, part)[:, :gain_part].reshape(1, head) for i in (2, 3)
    )
    head_gains = jnp.concatenate(
        [jnp.tile(gain_query, (1, 2)), jnp.tile(gain_key, (1, 2)), jnp.zeros((6, 2 * head), f32)], axis=0
    )

    half = width // 2
    pieces, wide = [ffn_own], []

    def over_y(piece):
        if y_size > 2:
            full = jnp.concatenate(list(lax.all_gather(piece, "y", axis=0)), axis=-1)
            wide.append((full[:, :half], full[:, half:]))
        else:
            wide.append((piece, lanes.swap(piece, "y")))

    over_y(ffn_own)
    for _ in range(1, z_size):
        pieces.append(lanes.move(pieces[-1], "z", ring(z_size), "z"))
        over_y(pieces[-1])
    near, far = [w[0] for w in wide], [w[1] for w in wide]
    cotangent = trade(cotangent, None)
    which = (y if y_size == 2 else y * 0).astype(jnp.int32).reshape(1)

    segment = lax.dynamic_index_in_dim(
        jnp.where(c == z % 2, segments, other_segments), z // 2, 0, keepdims=False
    )
    place = lax.broadcasted_iota(jnp.int32, (length,), 0) - jnp.sum(
        (segment[None, :] < segment[:, None]).astype(jnp.int32), axis=1
    )
    frequency = theta_base ** (-2.0 * jnp.arange(head // 2, dtype=f32) / head)
    angles = place.astype(f32)[:, None] * frequency
    cosine, sine = jnp.cos(angles), jnp.sin(angles)
    cosine = jnp.concatenate([cosine] * 4, axis=1)
    sine = jnp.concatenate([-sine, sine] * 2, axis=1)
    seg_col, seg_row = segment[:, None], segment[None, :]

    inputs = tokens.astype(f32)
    root_one = lax.rsqrt(jnp.mean(inputs * inputs, axis=-1, keepdims=True) + epsilon)
    hat_one = inputs * root_one
    all_root = lax.rsqrt(jnp.mean(all_tokens * all_tokens, axis=-1, keepdims=True) + epsilon)
    normed_one = (all_tokens * all_root * gain_one).astype(bf16)
    normed_one = after(normed_one, pieces[1])
    qkv = dot(normed_one, qkv_full, 1, 1).astype(bf16)
    qkv = after(qkv, cotangent)
    tables = (cosine, sine, seg_col, seg_row, head_gains, head)
    context = attend(qkv, *tables, 0, z_size // 2)
    qkv = after(qkv, context, pieces[z_size // 2], far[0])
    context = jnp.concatenate([context, attend(qkv, *tables, z_size // 2, z_size - z_size // 2)], axis=1)

    def half_rows(value, index):
        return lax.dynamic_slice_in_dim(value, index * own_rows, own_rows, 0)

    def core_reduce(left, right, right_dim):
        sent = dot(half_rows(left, 1 - c), right, 1, right_dim).astype(bf16)
        kept = dot(half_rows(left, c), right, 1, right_dim)
        return kept + lanes.swap(sent, "c").astype(f32)

    def spread(value, *earlier):
        across = lanes.swap(value, "x")
        over = lanes.swap(after(across, *earlier) if earlier else across, "c")
        return [value, lanes.swap(value, "c"), across, over]

    cots = spread(cotangent)
    mid = inputs + core_reduce(after(context, cots[2], far[1]), o_full, 0)
    root_two = lax.rsqrt(jnp.mean(mid * mid, axis=-1, keepdims=True) + epsilon)
    hat_two = mid * root_two
    normed_two = (hat_two * gain_two).astype(bf16)
    rows_two = spread(normed_two, far[-2])

    count = z_size // 2
    slot_grads, arrived = [None] * z_size, [None] * z_size

    def turn(group):
        return sorted(range(count), key=lambda i: (group * count + i - 1) % z_size)

    def send_gradients(sent, kept):
        if y_size > 2:
            full = jnp.concatenate([kept, sent], axis=1)
            full = jnp.stack([full[:, k * quad : (k + 1) * quad] for k in range(y_size)])
            got = lax.psum_scatter(full, "y", scatter_dimension=0, tiled=False)
            return got, got.astype(f32)
        got = lanes.swap(sent, "y")
        return got, plus(kept, got)

    gu_0, hid_0, sent, kept = ffn_first(which, near[:count], far[:count], rows_two, cots, turn(0))
    arrived[1], value = send_gradients(sent, kept)
    for i, slot in enumerate(turn(0)):
        slot_grads[slot] = value[i * 3 * sub : (i + 1) * 3 * sub]
    gu_1, hid_1, (first, second, third, fourth) = ffn_second(which, near, far, rows_two, cots, gu_0)
    third = plus(third, lanes.swap(fourth, "c")).astype(bf16)
    across = lanes.swap(third, "x")
    second = lanes.swap(second, "c")
    sent, kept, (out_first, out_second, out_third, out_fourth) = ffn_third(
        after(which, third), near, far, rows_two, cots, gu_1, hid_1, hid_0, turn(1)
    )
    for i in turn(1):
        lanes.last.pop("y", None)
        arrived[count + i], slot_grads[count + i] = send_gradients(sent[i], kept[i])
    ring_first = slot_grads[1].astype(bf16)
    total = lanes.move(ring_first, "z", ring(z_size), "z")
    grad_normed_two = after(plus(first, second, across), out_first)


    def norm_back(grad, hat, root):
        return root * (grad - hat * jnp.mean(grad * hat, axis=-1, keepdims=True))

    gain_two_part = jnp.sum(grad_normed_two * hat_two, axis=0)
    grad_mid = cotangent.astype(f32) + norm_back(grad_normed_two * gain_two, hat_two, root_two)

    branch_own = grad_mid.astype(bf16)
    branch = by_index(c, branch_own, lanes.swap(branch_own, "c"), 0)
    grad_context = dot(branch, o_full, 1, 1).astype(bf16)
    o_grad = dot(after(context, grad_context), branch, 0, 0).astype(bf16)
    grad_context = after(grad_context, o_grad, ring_first)
    grad_first, sums_first = attend_back(qkv, *tables[:-1], grad_context, head, 0, z_size // 2)
    out_third = plus(out_third, lanes.swap(out_fourth, "c")).astype(bf16)
    out_third = after(out_third, grad_normed_two)
    out_across = lanes.move(out_third, "x", [(0, 1), (1, 0)], None)
    output = mid + plus(out_first, lanes.swap(out_second, "c"), after(out_across, grad_first))
    output = output.astype(bf16)
    if y_size > 2:
        o_part = plane_scatter(o_grad, sizes, pair, lanes).astype(bf16)
        o_far = o_part
    else:
        block = lambda a, b: lane_block(o_grad, a * x_size + b, pair)
        o_far = lanes.move(block(1 - y, 1 - x), "x", [(0, 1), (1, 0)], None)
        o_near = lanes.move(block(y, 1 - x), "x", [(0, 1), (1, 0)], None)
        o_far = plus(block(1 - y, x), after(o_far, grad_first, output)).astype(bf16)
        o_part = plus(block(y, x), o_near)
    total = plus(after(total, grad_first), slot_grads[2]).astype(bf16)
    grad_last, sums_last = attend_back(
        qkv, *tables[:-1], after(grad_context, total, o_far), head, z_size // 2, z_size - z_size // 2
    )
    if y_size == 2:
        o_far = lanes.move(o_far, "y", [(0, 1), (1, 0)], None)
        o_part = plus(o_part, after(o_far, grad_last)).astype(bf16)
    total = lanes.move(total, "z", ring(z_size), "z")
    output_got = lanes.move(after(output, total), ("c", "z"), pairs, None)
    grad_last = after(grad_last, o_part, arrived[-1])
    for step in range(2, z_size - 1):
        total = plus(after(total, grad_last), slot_grads[step + 1]).astype(bf16)
        grad_last = after(grad_last, total)
        total = lanes.move(total, "z", ring(z_size), "z")
    total_last = plus(total, slot_grads[0])
    extra = [jnp.zeros((1, width), f32), gain_two_part[None], jnp.zeros((14, width), f32)]
    spaced = part < 2 * head
    if spaced:
        sums = jnp.sum(jnp.concatenate([sums_first, sums_last]).reshape(-1, 8, 2 * head), axis=0)
        extra[2:] = [
            jnp.pad(v.reshape(parts, gain_part), ((0, 0), (0, part - gain_part))).reshape(1, width)
            for v in (sums[0, :head] + sums[0, head:], sums[1, :head])
        ] + [jnp.zeros((12, width), f32)]
    extra = jnp.concatenate(extra, axis=0)
    if y_size > 2:
        starts = [which[0] + i * (width // 4) for i in range(4)]
    else:
        starts = [(a * x_size + b) * pair for a, b in ((1 - y, 1 - x), (y, 1 - x), (1 - y, x), (y, x))]
    given = (qkv_full, extra, gain_one, (sums_first, sums_last), z_size, spaced)
    blocks = list(qkv_grads(starts[:1], (grad_first, grad_last), normed_one, *given))
    grad_last = after(grad_last, blocks[0])
    blocks += qkv_grads(starts[1:], (grad_first, grad_last), normed_one, *given)
    if y_size == 2:
        far_got = lanes.move(blocks[0], "x", [(0, 1), (1, 0)], None)
    grad_first = after(grad_first, blocks[3])
    cut = grad_first.shape[1]

    def two_terms(index):
        return dot(half_rows(grad_first, index), qkv_full[:cut], 1, 0) + dot(
            half_rows(grad_last, index), qkv_full[cut:], 1, 0
        )

    sent = two_terms(1 - c).astype(bf16)
    grad_normed_one = two_terms(c) + lanes.swap(sent, "c").astype(f32)
    tokens_grad = (grad_mid + norm_back(grad_normed_one * gain_one, hat_one, root_one)).astype(bf16)
    if y_size > 2:
        qkv_part = plane_scatter(jnp.concatenate(blocks, axis=1), sizes, pair, lanes).astype(bf16)
    else:
        near_got = lanes.move(after(blocks[1], far_got), "x", [(0, 1), (1, 0)], None)
        lanes.last["x"] = (near_got,)
        far_sum = plus(blocks[2], far_got).astype(bf16)
        y_got = after(lanes.swap(far_sum, "y"), output_got, tokens_grad)
        qkv_part = plus(blocks[3], near_got, y_got).astype(bf16)

    def core_deal(value):
        kept = lane_block(value, c, part)
        sent = lanes.swap(lane_block(value, 1 - c, part), "c")
        return jnp.where(c == 0, jnp.stack([kept, sent]), jnp.stack([sent, kept]))

    wgrads = total_last.astype(bf16).reshape(3, sub, quad)
    kept = lane_block(wgrads, x, pair)
    sent = lanes.swap(lane_block(wgrads, 1 - x, pair), "x")
    dealt = sent
    wgrads = jnp.where(x == 0, jnp.stack([kept, sent], 1), jnp.stack([sent, kept], 1))
    kept = lane_block(wgrads, c, part)
    sent = lanes.swap(lane_block(wgrads, 1 - c, part), "c")
    wgrads = jnp.where(c == 0, jnp.stack([kept, sent], 2), jnp.stack([sent, kept], 2))
    wgrads = wgrads.reshape(3, x_size * c_size * sub, part)
    last_grads = wgrads


    rows = qkv_rows + 16
    lanes.last.pop("z", None)
    value = z_scatter(
        [
            jnp.concatenate(
                [qkv_part[i * rows : (i + 1) * rows], o_part[i * q_rows : (i + 1) * q_rows]], axis=0
            )
            for i in range(z_size)
        ],
        z_size,
        lanes,
    )
    tokens_got = lanes.move(after(tokens_grad, lanes.last["z"][0]), ("c", "z"), pairs, None)
    value = after(value.astype(bf16), dealt)
    kept = lane_block(value, c, part)
    sent = lanes.swap(lane_block(value, 1 - c, part), "c")
    gain_sums = plus(kept[qkv_rows:rows], sent[qkv_rows:rows])
    qkv_grad = jnp.where(c == 0, jnp.stack([kept, sent]), jnp.stack([sent, kept])).astype(f32)
    o_wgrad = qkv_grad[:, rows:].reshape(2 * q_rows, part).T
    qkv_grad = qkv_grad[:, :qkv_rows]
    last_grads = after(last_grads, sent)
    gate_wgrad, up_wgrad, down_wgrad = (last_grads[i].astype(f32).T for i in range(3))
    q_wgrad = qkv_grad[:, :q_rows].reshape(-1, part).T
    k_wgrad = qkv_grad[:, q_rows : q_rows + k_rows].reshape(-1, part).T
    v_wgrad = qkv_grad[:, q_rows + k_rows :].reshape(-1, part).T
    if spaced:
        gain_query_sum, gain_key_sum = gain_sums[2, :gain_part], gain_sums[3, :gain_part]
    else:
        mine = ((y * x_size + x) * c_size + c) * gain_part
        gain_query_sum, gain_key_sum = (
            lax.dynamic_slice(gain_sums[2], (mine + at,), (gain_part,)) for at in (0, head)
        )
    return (
        jnp.where(trades, output_got, output),
        jnp.where(trades, tokens_got, tokens_grad),
        gain_sums[0],
        q_wgrad,
        k_wgrad,
        v_wgrad,
        gain_query_sum,
        gain_key_sum,
        o_wgrad,
        gain_sums[1],
        gate_wgrad,
        up_wgrad,
        down_wgrad,
    )


def solution(mesh):
    dp, tp = mesh.devices.shape
    sizes = (dp // 4, 2, 2, tp)
    fine = Mesh(mesh.devices.reshape(sizes), ("y", "x", "c", "z"))
    d = ("y", "x", "c")
    rows, weight, gain = P((*d, "z"), None), P(d, "z"), P(d)
    return jax.shard_map(
        functools.partial(shards, sizes),
        mesh=fine,
        in_specs=(rows, P(d, None), rows, gain, weight, weight, weight, gain, gain, weight, gain)
        + (weight,) * 3,
        out_specs=(rows, rows, gain, weight, weight, weight, gain, gain, weight, gain) + (weight,) * 3,
        check_vma=False,
    )
```

```python
import functools

import jax
import jax.numpy as jnp
from jax import lax
from jax.experimental import pallas as pl
from jax.experimental.pallas import tpu as pltpu
from jax.sharding import Mesh, PartitionSpec as P

epsilon = 1e-05
theta_base = 1000000.0
bf16 = jnp.bfloat16
f32 = jnp.float32
tile = 256
span = 512


def cost(flops):
    return pl.CostEstimate(flops=flops // 1000, bytes_accessed=10**5, transcendentals=0)


def dot(left, right, left_dim, right_dim):
    return lax.dot_general(
        left, right, (((left_dim,), (right_dim,)), ((), ())), preferred_element_type=f32
    )


def group_sum(value, ones):
    high = value.astype(bf16)
    low = (value - high.astype(f32)).astype(bf16)
    return dot(high, ones, 1, 0) + dot(low, ones, 1, 0)


def ones_by_head(lanes, head):
    row = lax.broadcasted_iota(jnp.int32, (lanes, lanes), 0) // head
    col = lax.broadcasted_iota(jnp.int32, (lanes, lanes), 1) // head
    return jnp.where(row == col, 1.0, 0.0).astype(bf16)


def half_swap(value, head):
    lanes = value.shape[-1]
    lane = lax.broadcasted_iota(jnp.int32, value.shape, 1) % head
    return jnp.where(
        lane < head // 2,
        pltpu.roll(value, lanes - head // 2, 1),
        pltpu.roll(value, head // 2, 1),
    )


def head_norm(raw, ones, head):
    root = lax.rsqrt(group_sum(raw * raw, ones) * (1.0 / head) + epsilon)
    return raw * root, root


def split_block(block, head):
    lanes = 2 * head
    queries = block[:, :lanes]
    both = block[:, lanes:]
    other = pltpu.roll(both, head, 1)
    first = lax.broadcasted_iota(jnp.int32, both.shape, 1) < head
    keys = jnp.where(first, both, other)
    values = jnp.where(first, other, both)
    return queries, keys, values


def stack_heads(block, head):
    first = lax.broadcasted_iota(jnp.int32, block.shape, 1) < head
    zero = jnp.zeros_like(block)
    return jnp.concatenate([jnp.where(first, block, zero), jnp.where(first, zero, block)], axis=0)


def merge_heads(stacked, head):
    half = stacked.shape[0] // 2
    first = lax.broadcasted_iota(jnp.int32, (half, stacked.shape[1]), 1) < head
    return jnp.where(first, stacked[:half], stacked[half:])


def attend_kernel(head, qkv_ref, cos_ref, sin_ref, seg_col, seg_row, gain_ref, ctx_ref, q_s, k_s, v_s):
    length = qkv_ref.shape[0]
    lanes = 2 * head
    ones = ones_by_head(lanes, head)
    queries, keys, values = split_block(qkv_ref[...].astype(f32), head)
    cosine, sine = cos_ref[...], sin_ref[...]

    def rotated(raw, gain):
        hat, _ = head_norm(raw, ones, head)
        scaled = hat * gain
        return (scaled * cosine + half_swap(scaled, head) * sine).astype(bf16)

    q_s[...] = rotated(queries, gain_ref[0:1, :]) * jnp.asarray(head**-0.5, bf16)
    k_s[...] = rotated(keys, gain_ref[1:2, :])
    v_s[...] = values.astype(bf16)
    for top in range(0, length, tile):
        low, high = max(0, top - span), top + tile
        stacked = stack_heads(q_s[top:high, :], head)
        scores = dot(stacked, k_s[low:high, :], 1, 1)
        row = lax.broadcasted_iota(jnp.int32, (tile, high - low), 0) + top
        col = lax.broadcasted_iota(jnp.int32, (tile, high - low), 1) + low
        allowed = (seg_col[top:high, 0:1] == seg_row[0:1, low:high]) & (row >= col)
        allowed = jnp.concatenate([allowed, allowed], axis=0)
        exponent = jnp.where(allowed, jnp.exp(scores), 0.0)
        total = jnp.sum(exponent, axis=1, keepdims=True)
        mixed = dot(exponent.astype(bf16), v_s[low:high, :], 1, 0) / total
        ctx_ref[top:high, :] = merge_heads(mixed, head).astype(bf16)


def attend(qkv, cosine, sine, seg_col, seg_row, gains, head, first, groups):
    length = qkv.shape[0]
    lanes = 2 * head
    whole = lambda shape: pl.BlockSpec(shape, lambda j: (0, 0))
    return pl.pallas_call(
        functools.partial(attend_kernel, head),
        grid=(groups,),
        in_specs=[
            pl.BlockSpec((length, 2 * lanes), lambda j: (0, j + first)),
            whole((length, lanes)),
            whole((length, lanes)),
            whole((length, 1)),
            whole((1, length)),
            whole((8, lanes)),
        ],
        out_specs=pl.BlockSpec((length, lanes), lambda j: (0, j)),
        out_shape=jax.ShapeDtypeStruct((length, groups * lanes), bf16),
        scratch_shapes=[pltpu.VMEM((length, lanes), bf16)] * 3,
        compiler_params=pltpu.CompilerParams(vmem_limit_bytes=24 * 2**20),
        cost_estimate=cost(6 * 10**9),
        name="attend",
    )(qkv, cosine, sine, seg_col, seg_row, gains)


def attend_back_kernel(
    head, qkv_ref, cos_ref, sin_ref, seg_col, seg_row, gain_ref, do_ref, out_ref, sums_ref,
    q_s, k_s, v_s, dk_s, dv_s, dq_s,
):
    length = qkv_ref.shape[0]
    lanes = 2 * head
    ones = ones_by_head(lanes, head)
    queries, keys, values = split_block(qkv_ref[...].astype(f32), head)
    cosine, sine = cos_ref[...], sin_ref[...]

    def rotated(raw, gain):
        hat, _ = head_norm(raw, ones, head)
        scaled = hat * gain
        return (scaled * cosine + half_swap(scaled, head) * sine).astype(bf16)

    scale = jnp.asarray(head**-0.5, bf16)
    q_s[...] = rotated(queries, gain_ref[0:1, :]) * scale
    k_s[...] = rotated(keys, gain_ref[1:2, :])
    v_s[...] = values.astype(bf16)
    dk_s[...] = jnp.zeros_like(dk_s)
    dv_s[...] = jnp.zeros_like(dv_s)
    for top in range(0, length, tile):
        low, high = max(0, top - span), top + tile
        stacked = stack_heads(q_s[top:high, :], head)
        grads = stack_heads(do_ref[top:high, :], head)
        near_k, near_v = k_s[low:high, :], v_s[low:high, :]
        scores = dot(near_k, stacked, 1, 1)
        col = lax.broadcasted_iota(jnp.int32, (high - low, tile), 0) + low
        row = lax.broadcasted_iota(jnp.int32, (high - low, tile), 1) + top
        allowed = (seg_col[low:high, 0:1] == seg_row[0:1, top:high]) & (row >= col)
        allowed = jnp.concatenate([allowed, allowed], axis=1)
        exponent = jnp.where(allowed, jnp.exp(scores), 0.0)
        probs = exponent * (1.0 / jnp.sum(exponent, axis=0, keepdims=True))
        grad_probs = dot(near_v, grads, 1, 1)
        weighted = probs * grad_probs
        delta = jnp.sum(weighted, axis=0, keepdims=True)
        grad_scores = (weighted - probs * delta).astype(bf16)
        dv_s[low:high, :] += dot(probs.astype(bf16), grads, 1, 0)
        dk_s[low:high, :] += dot(grad_scores, stacked, 1, 0)
        dq_s[top:high, :] = merge_heads(dot(grad_scores, near_k, 0, 0), head) * head**-0.5

    def back(raw, gain, grad):
        hat, root = head_norm(raw, ones, head)
        normed = grad * cosine - half_swap(grad, head) * sine
        gain_part = jnp.sum(normed * hat, axis=0, keepdims=True)
        scaled = normed * gain
        mean = group_sum(scaled * hat, ones) * (1.0 / head)
        return root * (scaled - hat * mean), gain_part

    grad_q, q_sum = back(queries, gain_ref[0:1, :], dq_s[...])
    folded_k = dk_s[...] + pltpu.roll(dk_s[...], head, 1)
    grad_k, k_sum = back(keys, gain_ref[1:2, :], folded_k)
    folded_v = dv_s[...] + pltpu.roll(dv_s[...], head, 1)
    first = lax.broadcasted_iota(jnp.int32, (length, lanes), 1) < head
    out_ref[:, :lanes] = grad_q.astype(bf16)
    out_ref[:, lanes:] = jnp.where(first, grad_k, folded_v).astype(bf16)
    which = lax.broadcasted_iota(jnp.int32, sums_ref.shape, 0)
    sums_ref[...] = jnp.where(which == 0, q_sum, jnp.where(which == 1, k_sum, 0.0))


def attend_back(qkv, cosine, sine, seg_col, seg_row, gains, grad_context, head, first, groups):
    length = qkv.shape[0]
    lanes = 2 * head
    whole = lambda shape: pl.BlockSpec(shape, lambda j: (0, 0))
    return pl.pallas_call(
        functools.partial(attend_back_kernel, head),
        grid=(groups,),
        in_specs=[
            pl.BlockSpec((length, 2 * lanes), lambda j: (0, j + first)),
            whole((length, lanes)),
            whole((length, lanes)),
            whole((length, 1)),
            whole((1, length)),
            whole((8, lanes)),
            pl.BlockSpec((length, lanes), lambda j: (0, j + first)),
        ],
        out_specs=(
            pl.BlockSpec((length, 2 * lanes), lambda j: (0, j)),
            pl.BlockSpec((8, lanes), lambda j: (j, 0)),
        ),
        out_shape=(
            jax.ShapeDtypeStruct((length, groups * 2 * lanes), bf16),
            jax.ShapeDtypeStruct((8 * groups, lanes), f32),
        ),
        scratch_shapes=[pltpu.VMEM((length, lanes), bf16)] * 3 + [pltpu.VMEM((length, lanes), f32)] * 3,
        compiler_params=pltpu.CompilerParams(vmem_limit_bytes=28 * 2**20),
        cost_estimate=cost(12 * 10**9),
        name="attend_back",
    )(qkv, cosine, sine, seg_col, seg_row, gains, grad_context)


def pull(pairs, sems, start):
    copies = [pltpu.make_async_copy(s, d, sems.at[start + i]) for i, (s, d) in enumerate(pairs)]
    for copy in copies:
        copy.start()
    return copies


def finish(copies):
    for copy in copies:
        copy.wait()


def halves(which_ref, half):
    first = pl.multiple_of(which_ref[0] * half, half)
    second = pl.multiple_of((1 - which_ref[0]) * half, half)
    return pl.ds(first, half), pl.ds(second, half)


def call_local(kernel, which, arrays, outs, out_spaces, scratch, copies, flops, name, limit=44):
    return pl.pallas_call(
        kernel,
        in_specs=[pl.BlockSpec(memory_space=pltpu.SMEM)] + [pl.BlockSpec(memory_space=pltpu.HBM)] * len(arrays),
        out_specs=[pl.BlockSpec(memory_space=space) for space in out_spaces],
        out_shape=outs,
        scratch_shapes=[*scratch, pltpu.SemaphoreType.DMA((copies,))],
        compiler_params=pltpu.CompilerParams(vmem_limit_bytes=limit * 2**20),
        cost_estimate=cost(flops),
        name=name,
    )(which, *arrays)


class Loads:
    def __init__(self, sems):
        self.sems, self.count, self.open = sems, 0, {}

    def start(self, key, *pairs):
        for source, target in pairs:
            copy = pltpu.make_async_copy(source, target, self.sems.at[self.count])
            copy.start()
            self.open.setdefault(key, []).append(copy)
            self.count += 1

    def wait(self, *keys):
        for key in keys:
            for copy in self.open.pop(key, ()):
                copy.wait()

    def close(self):
        self.wait(*list(self.open))


def load_gate_up(loads, key, near, far, which_ref, target, slots):
    size, half = near[0].shape
    top = 2 * size // 3
    for at, i in enumerate(slots):
        for pieces, lanes in zip((near, far), halves(which_ref, half)):
            loads.start((key, at), (pieces[i].at[pl.ds(0, top)], target.at[pl.ds(at * top, top), lanes]))


def load_down(loads, key, near, far, which_ref, target, slots):
    size, half = near[0].shape
    rest = size // 3
    for at, i in enumerate(slots):
        for pieces, lanes in zip((near, far), halves(which_ref, half)):
            loads.start(
                (key, at), (pieces[i].at[pl.ds(size - rest, rest)], target.at[pl.ds(at * rest, rest), lanes])
            )


def hidden_step(gate_up, down, rows, cot, gu_s, hid_s, slot, columns, sub):
    both = dot(gate_up[2 * slot * sub : 2 * (slot + 1) * sub, :], rows, 1, 1)
    back = dot(down[slot * sub : (slot + 1) * sub, :], cot, 1, 1)
    gate, up = both[:sub], both[sub:]
    sig = 0.5 * jnp.tanh(0.5 * gate) + 0.5
    act = gate * sig
    base = 2 * slot * sub
    gu_s[base : base + sub, columns] = (back * up * (sig + act * (1.0 - sig))).astype(bf16)
    gu_s[base + sub : base + 2 * sub, columns] = (back * act).astype(bf16)
    hid_s[slot * sub : (slot + 1) * sub, columns] = (act * up).astype(bf16)


def weight_step(loads, which_ref, gu_s, hid_s, rows_s, cot_s, out_s, far_out, near_out, order, sub):
    size, half = 3 * sub, rows_s.shape[1] // 2
    first, second = halves(which_ref, half)
    for side, lanes, outs in ((0, second, far_out), (1, first, near_out)):
        rows, cots = rows_s[:, lanes], cot_s[:, lanes]
        for at, s in enumerate(order):
            out_s[side, s, : 2 * sub] = dot(gu_s[2 * s * sub : 2 * (s + 1) * sub, :], rows, 1, 0).astype(bf16)
            out_s[side, s, 2 * sub :] = dot(hid_s[s * sub : (s + 1) * sub, :], cots, 1, 0).astype(bf16)
            target = outs[s] if len(outs) > 1 else outs[0].at[pl.ds(at * size, size)]
            loads.start("out", (out_s.at[side, s], target))


def take(refs, *counts):
    at, out = 0, []
    for count in counts:
        out.append(refs[at : at + count])
        at += count
    return (*out, refs[at:])


def first_kernel(slots, quarters, order, which_ref, *refs):
    near, far, rows, cots, (gu_out, hid_out), far_out, near_out, rest = take(
        refs, slots, slots, quarters, quarters, 2, 1, 1
    )
    gate_up, down, rows_s, cot_s, gu_s, hid_s, out_s, sems = rest
    sub, count = near[0].shape[0] // 3, rows[0].shape[0]
    loads = Loads(sems)
    for q in range(max(slots, quarters)):
        if q < quarters:
            place = pl.ds(q * count, count)
            loads.start(("rows", q), (rows[q], rows_s.at[place]), (cots[q], cot_s.at[place]))
        if q == 0:
            load_gate_up(loads, "w", near, far, which_ref, gate_up, range(slots))
            load_down(loads, "w", near, far, which_ref, down, range(slots))
    for q in range(quarters):
        columns = slice(q * count, (q + 1) * count)
        loads.wait(("rows", q))
        for s in range(slots):
            loads.wait(("w", s))
            hidden_step(gate_up, down, rows_s[columns, :], cot_s[columns, :], gu_s, hid_s, s, columns, sub)
    loads.start("out", (gu_s, gu_out), (hid_s, hid_out))
    weight_step(loads, which_ref, gu_s, hid_s, rows_s, cot_s, out_s, far_out, near_out, order, sub)
    loads.close()


def ffn_first(which, near, far, rows, cots, order):
    slots, quarters = len(near), len(rows)
    size, half = near[0].shape
    sub, count = size // 3, rows[0].shape[0]
    tokens = quarters * count
    gu, hid = (2 * slots * sub, tokens), (slots * sub, tokens)
    out = call_local(
        functools.partial(first_kernel, slots, quarters, order),
        which,
        [*near, *far, *rows, *cots],
        [jax.ShapeDtypeStruct(v, bf16) for v in (gu, hid)]
        + [jax.ShapeDtypeStruct((slots * size, half), bf16)] * 2,
        [pl.ANY] * 4,
        [
            pltpu.VMEM((2 * slots * sub, 2 * half), bf16),
            pltpu.VMEM((slots * sub, 2 * half), bf16),
            pltpu.VMEM((tokens, 2 * half), bf16),
            pltpu.VMEM((tokens, 2 * half), bf16),
            pltpu.VMEM(gu, bf16),
            pltpu.VMEM(hid, bf16),
            pltpu.VMEM((2, slots, size, half), bf16),
        ],
        2 * quarters + 4 * slots + 2 + 2 * slots,
        8 * slots * size * half * tokens,
        "ffn_first",
    )
    return out


def second_kernel(slots, quarters, which_ref, *refs):
    near, far, rows, cots, (gu_0,), (gu_out, hid_out), outs, rest = take(
        refs, 2 * slots, 2 * slots, quarters, quarters, 1, 2, quarters
    )
    gate_up, down, gate_up_0, rows_s, cot_s, gu_s, hid_s, gu_0s, out_s, sems = rest
    sub, count = near[0].shape[0] // 3, rows[0].shape[0]
    loads = Loads(sems)
    for q in range(quarters):
        place = pl.ds(q * count, count)
        loads.start(("rows", q), (rows[q], rows_s.at[place]), (cots[q], cot_s.at[place]))
        if q == 0:
            load_gate_up(loads, "w", near, far, which_ref, gate_up, range(slots, 2 * slots))
            load_down(loads, "w", near, far, which_ref, down, range(slots, 2 * slots))
    load_gate_up(loads, "w0", near, far, which_ref, gate_up_0, range(slots))
    loads.start("g0", (gu_0, gu_0s))
    for q in range(quarters):
        columns = slice(q * count, (q + 1) * count)
        loads.wait(("rows", q))
        for s in range(slots):
            loads.wait(("w", s))
            hidden_step(gate_up, down, rows_s[columns, :], cot_s[columns, :], gu_s, hid_s, s, columns, sub)
    loads.start("out", (gu_s, gu_out), (hid_s, hid_out))
    loads.wait("g0", *(("w0", s) for s in range(slots)))
    for q in range(quarters):
        columns = slice(q * count, (q + 1) * count)
        total = dot(gu_0s[:, columns], gate_up_0[...], 0, 0) + dot(gu_s[:, columns], gate_up[...], 0, 0)
        out_s[q] = total.astype(bf16)
        loads.start("out", (out_s.at[q], outs[q]))
    loads.close()


def ffn_second(which, near, far, rows, cots, gu_0):
    slots, quarters = len(near) // 2, len(rows)
    size, half = near[0].shape
    sub, count = size // 3, rows[0].shape[0]
    tokens = quarters * count
    gu, hid = (2 * slots * sub, tokens), (slots * sub, tokens)
    out = call_local(
        functools.partial(second_kernel, slots, quarters),
        which,
        [*near, *far, *rows, *cots, gu_0],
        [jax.ShapeDtypeStruct(v, bf16) for v in (gu, hid)]
        + [jax.ShapeDtypeStruct((count, 2 * half), bf16)] * quarters,
        [pl.ANY] * (2 + quarters),
        [
            pltpu.VMEM((2 * slots * sub, 2 * half), bf16),
            pltpu.VMEM((slots * sub, 2 * half), bf16),
            pltpu.VMEM((2 * slots * sub, 2 * half), bf16),
            pltpu.VMEM((tokens, 2 * half), bf16),
            pltpu.VMEM((tokens, 2 * half), bf16),
            pltpu.VMEM(gu, bf16),
            pltpu.VMEM(hid, bf16),
            pltpu.VMEM(gu, bf16),
            pltpu.VMEM((quarters, count, 2 * half), bf16),
        ],
        3 * quarters + 6 * slots + 3,
        10 * slots * size * half * tokens,
        "ffn_second",
    )
    return out[0], out[1], out[2:]


def third_kernel(slots, quarters, order, which_ref, *refs):
    near, far, rows, cots, (gu, hid, hid_0), far_out, near_out, outs, rest = take(
        refs, 2 * slots, 2 * slots, quarters, quarters, 3, slots, slots, quarters
    )
    down, rows_s, cot_s, gu_s, hid_s, hid_0s, grad_s, out_s, sems = rest
    sub, count = far_out[0].shape[0] // 3, rows[0].shape[0]
    loads = Loads(sems)
    load_down(loads, "w", near, far, which_ref, down, range(2 * slots))
    loads.start("h", (hid_0, hid_0s), (hid, hid_s))
    loads.start("rows", (gu, gu_s))
    for q in range(quarters):
        place = pl.ds(q * count, count)
        loads.start("rows", (rows[q], rows_s.at[place]), (cots[q], cot_s.at[place]))
    loads.wait("h", *(("w", s) for s in range(2 * slots)))
    for q in range(quarters):
        columns = slice(q * count, (q + 1) * count)
        total = dot(hid_0s[:, columns], down[: slots * sub, :], 0, 0)
        total = total + dot(hid_s[:, columns], down[slots * sub :, :], 0, 0)
        out_s[q] = total.astype(bf16)
        loads.start("out", (out_s.at[q], outs[q]))
    loads.wait("rows")
    weight_step(loads, which_ref, gu_s, hid_s, rows_s, cot_s, grad_s, far_out, near_out, order, sub)
    loads.close()


def ffn_third(which, near, far, rows, cots, gu, hid, hid_0, order):
    slots, quarters = len(order), len(rows)
    size, half = near[0].shape
    sub, count = size // 3, rows[0].shape[0]
    tokens = quarters * count
    out = call_local(
        functools.partial(third_kernel, slots, quarters, order),
        which,
        [*near, *far, *rows, *cots, gu, hid, hid_0],
        [jax.ShapeDtypeStruct((size, half), bf16)] * (2 * slots)
        + [jax.ShapeDtypeStruct((count, 2 * half), bf16)] * quarters,
        [pl.ANY] * (2 * slots + quarters),
        [
            pltpu.VMEM((2 * slots * sub, 2 * half), bf16),
            pltpu.VMEM((tokens, 2 * half), bf16),
            pltpu.VMEM((tokens, 2 * half), bf16),
            pltpu.VMEM((2 * slots * sub, tokens), bf16),
            pltpu.VMEM((slots * sub, tokens), bf16),
            pltpu.VMEM((slots * sub, tokens), bf16),
            pltpu.VMEM((2, slots, size, half), bf16),
            pltpu.VMEM((quarters, count, 2 * half), bf16),
        ],
        3 * quarters + 4 * slots + 3 + 2 * slots,
        6 * slots * size * half * tokens,
        "ffn_third",
    )
    return out[:slots], out[slots : 2 * slots], out[2 * slots :]


def qkv_grads_kernel(groups, spaced, starts_ref, grads_0, grads_1, rows, weights, extra_ref, gain_ref, sums_0, sums_1, *refs):
    outs, rest = refs[: len(refs) - 8], refs[len(refs) - 8 :]
    grad_s, rows_s, weight_s, extra_s, gain_s, sums_s, out_s, sems = rest
    size = (grads_0.shape[1] + grads_1.shape[1]) // groups
    width = outs[0].shape[1]
    more = extra_ref.shape[0]
    cut = grads_0.shape[1]
    loads = Loads(sems)
    loads.start("a", (grads_0, grad_s.at[:, pl.ds(0, cut)]), (grads_1, grad_s.at[:, pl.ds(cut, grads_1.shape[1])]))
    loads.start("a", (rows, rows_s))
    loads.start("b", (weights.at[pl.ds(0, groups * size)], weight_s), (extra_ref, extra_s), (gain_ref, gain_s))
    loads.start("b", (sums_0, sums_s.at[pl.ds(0, sums_0.shape[0])]))
    loads.start("b", (sums_1, sums_s.at[pl.ds(sums_0.shape[0], sums_1.shape[0])]))
    loads.wait("a")
    for i in range(len(outs)):
        lanes = pl.ds(pl.multiple_of(starts_ref[i], width), width)
        block = dot(grad_s[...], rows_s[:, lanes], 0, 0)
        if i == 0:
            loads.wait("b")
        gain_row = jnp.sum(block * weight_s[:, lanes].astype(f32), axis=0, keepdims=True)
        gain_row = gain_row / gain_s[0:1, lanes]
        row = lax.broadcasted_iota(jnp.int32, (more, width), 0)
        extra = jnp.where(row == 0, gain_row, extra_s[:, lanes])
        if not spaced:
            sums = sums_s[0:8, :]
            for g in range(1, groups):
                sums = sums + sums_s[8 * g : 8 * (g + 1), :]
            head = sums.shape[1] // 2
            query = sums[0:1, :] + pltpu.roll(sums[0:1, :], head, 1)
            lane = lax.broadcasted_iota(jnp.int32, query.shape, 1)
            both = jnp.where(lane < head, query, pltpu.roll(sums[1:2, :], head, 1))
            both = jnp.concatenate([both] * (width // (2 * head)), axis=1)
            extra = jnp.where(row == 2, both, extra)
        extra = extra.astype(bf16)
        for g in range(groups):
            base = g * (size + more)
            out_s[i, base : base + size, :] = block[g * size : (g + 1) * size, :].astype(bf16)
            out_s[i, base + size : base + size + more, :] = extra
        loads.start("out", (out_s.at[i], outs[i]))
    loads.close()


def qkv_grads(starts, grads, rows, weights, extra, gains, sums, groups, spaced):
    count, width = rows.shape
    columns, more = grads[0].shape[1] + grads[1].shape[1], extra.shape[0]
    block, blocks = (columns + groups * more, width // 4), len(starts)
    return call_local(
        functools.partial(qkv_grads_kernel, groups, spaced),
        jnp.stack(starts).astype(jnp.int32),
        [*grads, rows, weights, extra, gains, *sums],
        [jax.ShapeDtypeStruct(block, bf16)] * blocks,
        [pl.ANY] * blocks,
        [
            pltpu.VMEM((count, columns), bf16),
            pltpu.VMEM((count, width), bf16),
            pltpu.VMEM((columns, width), bf16),
            pltpu.VMEM((more, width), f32),
            pltpu.VMEM(gains.shape, f32),
            pltpu.VMEM((8 * groups, sums[0].shape[1]), f32),
            pltpu.VMEM((blocks, *block), bf16),
        ],
        8 + blocks,
        10**9,
        "qkv_grads",
    )


def place_kernel(count, parts, starts_ref, *refs):
    width = refs[0].shape[1]
    loads = Loads(refs[-1])
    for i in range(count):
        lanes = pl.ds(pl.multiple_of(starts_ref[i], width), width)
        for low, rows, out, place in parts:
            target = refs[count + out].at[pl.ds(place, rows), lanes]
            loads.start("a", (refs[i].at[pl.ds(low, rows)], target))
    loads.close()


def place_lanes(blocks, starts, parts, sizes):
    width = len(blocks) * blocks[0].shape[1]
    return call_local(
        functools.partial(place_kernel, len(blocks), parts),
        jnp.stack(starts).astype(jnp.int32),
        blocks,
        [jax.ShapeDtypeStruct((rows, width), bf16) for rows in sizes],
        [pl.ANY] * len(sizes),
        [],
        len(blocks) * len(parts),
        10**9,
        "place_lanes",
        4,
    )


def after(value, *earlier):
    return lax.optimization_barrier((value, *earlier))[0]


def ring(size, step=1):
    return [(i, (i + step) % size) for i in range(size)]


class Lanes:
    def __init__(self):
        self.last = {}

    def wait(self, value, lane):
        return after(value, *self.last.get(lane, ())) if lane in self.last else value

    def move(self, value, axes, pairs, lane):
        got = lax.ppermute(self.wait(value, lane), axes, pairs)
        if lane:
            self.last[lane] = (got,)
        return got

    def swap(self, value, axis):
        return self.move(value, axis, [(0, 1), (1, 0)], None if axis == "c" else axis)

    def around(self, values, size, signs, lane):
        held = [self.wait(value, lane) for value in values]
        got = [lax.ppermute(v, "z", ring(size, signs * (i + 1))) for i, v in enumerate(held)]
        self.last[lane] = tuple(got)
        return got


def by_index(index, first, second, axis):
    return jnp.where(
        index == 0,
        jnp.concatenate([first, second], axis=axis),
        jnp.concatenate([second, first], axis=axis),
    )


def lane_block(value, index, width):
    start = [0] * (value.ndim - 1) + [index * width]
    return lax.dynamic_slice(value, start, (*value.shape[:-1], width))


def plus(left, *right):
    total = left.astype(f32)
    for value in right:
        total = total + value.astype(f32)
    return total


def plane_gather(value, sizes, lanes, parts, heights):
    y_size, x_size = sizes[:2]
    y, x = lax.axis_index("y"), lax.axis_index("x")
    if y_size > 2:
        wide = by_index(x, value, lanes.swap(value, "x"), -1)
        wide = lax.all_gather(wide, "y", axis=0)
        wide = jnp.concatenate([wide[i] for i in range(y_size)], axis=-1)
        return [
            jnp.concatenate([wide[low : low + rows] for low, rows, to, _ in parts if to == out], axis=0)
            for out in range(len(heights))
        ]
    width = value.shape[1]
    far = lanes.swap(value, "y")
    blocks = [value, lanes.swap(value, "x"), far, lanes.swap(far, "x")]
    starts = [(a * x_size + b) * width for a in (y, 1 - y) for b in (x, 1 - x)]
    return place_lanes(blocks, starts, parts, heights)


def plane_scatter(value, sizes, pair, lanes):
    y_size, x_size = sizes[:2]
    y, x = lax.axis_index("y"), lax.axis_index("x")
    block = lambda y_at, x_at: lane_block(value, y_at * x_size + x_at, pair)
    if y_size > 2:
        per_y = [plus(block(i, x), lanes.swap(block(i, 1 - x), "x")).astype(bf16) for i in range(y_size)]
        return lax.psum_scatter(jnp.stack(per_y), "y", scatter_dimension=0, tiled=False).astype(f32)
    far = plus(block(1 - y, x), lanes.swap(block(1 - y, 1 - x), "x")).astype(bf16)
    near = lanes.swap(block(y, 1 - x), "x")
    return plus(block(y, x), near, lanes.swap(far, "y"))


def z_scatter(blocks, size, lanes):
    return plus(blocks[0], *lanes.around(blocks[1:], size, -1, "z"))


def shards(
    sizes,
    tokens,
    segments,
    cotangent,
    attn_gain,
    q_weight,
    k_weight,
    v_weight,
    query_gain,
    key_gain,
    o_weight,
    ffn_gain,
    gate_weight,
    up_weight,
    down_weight,
):
    y_size, x_size, c_size, z_size = sizes
    y, x, c, z = (lax.axis_index(name) for name in "yxcz")
    own_rows, width = tokens.shape
    part = q_weight.shape[0]
    parts = width // part
    pair, quad = c_size * part, x_size * c_size * part
    gain_part = query_gain.shape[0]
    head = gain_part * parts
    seq_count, length = segments.shape

    lanes = Lanes()

    pairs = []
    for low in range(0, z_size, 2):
        pairs += [(z_size + low, low + 1), (low + 1, z_size + low)]
    trades = (c + z) % 2 == 1

    def trade(value, lane):
        return jnp.where(trades, lanes.move(value, ("c", "z"), pairs, lane), value)

    tokens = trade(tokens, None)

    qt, kt, vt, ot = q_weight.T, k_weight.T, v_weight.T, o_weight.T
    q_rows, k_rows = qt.shape[0] // 2, kt.shape[0] // 2
    qkv_rows = q_rows + 2 * k_rows
    qkv_pack = jnp.concatenate([v.reshape(2, -1, part) for v in (qt, kt, vt, ot)], axis=1)
    qkv_pack = qkv_pack.reshape(-1, part)
    qkv_slots = [qkv_pack, *lanes.around([qkv_pack] * (z_size - 1), z_size, 1, "z")]

    sub = gate_weight.shape[1] // (x_size * c_size)
    ffn_pack = jnp.stack([v.T for v in (gate_weight, up_weight, down_weight)]).reshape(
        3, x_size, c_size, sub, part
    )
    mine = lax.dynamic_index_in_dim(ffn_pack, x, 1, keepdims=False)
    other = lax.dynamic_index_in_dim(ffn_pack, 1 - x, 1, keepdims=False)
    ffn_pack = by_index(x, mine, lanes.swap(other, "x"), -1)
    mine = lax.dynamic_index_in_dim(ffn_pack, c, 1, keepdims=False)
    other = lax.dynamic_index_in_dim(ffn_pack, 1 - c, 1, keepdims=False)
    ffn_ready = other
    other = lanes.swap(other, "c")
    ffn_own = jnp.concatenate(
        [
            by_index(c, mine[..., i * part : (i + 1) * part], other[..., i * part : (i + 1) * part], -1)
            for i in range(x_size)
        ],
        axis=-1,
    ).reshape(3 * sub, quad)

    gain_rows = jnp.concatenate(
        [attn_gain[None], ffn_gain[None]]
        + [jnp.pad(g, (0, part - gain_part))[None] for g in (query_gain, key_gain)]
        + [jnp.zeros((12, part), bf16)],
        axis=0,
    )
    numbers = segments.astype(bf16).reshape(-1, part)
    slot_rows = qkv_rows + q_rows

    def rows_of(core):
        return [lax.dynamic_slice_in_dim(v, core * slot_rows, slot_rows, 0) for v in qkv_slots]

    height = z_size * slot_rows + 16
    got = jnp.concatenate([*rows_of(1 - c), gain_rows, numbers], axis=0)
    got = lanes.swap(after(got, ffn_ready), "c")
    own = by_index(c, jnp.concatenate([*rows_of(c), gain_rows], axis=0), got[:height], -1)
    other_segments = got[height:].astype(jnp.int32).reshape(seq_count, length)

    all_tokens = by_index(c, tokens, lanes.swap(tokens, "c"), 0).astype(f32)
    gathered = [(i * slot_rows, qkv_rows, 0, i * qkv_rows) for i in range(z_size)]
    gathered += [(i * slot_rows + qkv_rows, q_rows, 2, i * q_rows) for i in range(z_size)]
    gathered += [(z_size * slot_rows, 16, 1, 0)]
    heights = (z_size * qkv_rows, 16, z_size * q_rows)
    qkv_full, gains, o_full = plane_gather(own, sizes, lanes, gathered, heights)
    gains = gains.astype(f32)
    gain_one, gain_two = gains[0:1], gains[1:2]
    gain_query, gain_key = (
        gains[i].reshape(parts, part)[:, :gain_part].reshape(1, head) for i in (2, 3)
    )
    head_gains = jnp.concatenate(
        [jnp.tile(gain_query, (1, 2)), jnp.tile(gain_key, (1, 2)), jnp.zeros((6, 2 * head), f32)], axis=0
    )

    half = width // 2
    pieces, wide = [ffn_own], []

    def over_y(piece):
        if y_size > 2:
            full = jnp.concatenate(list(lax.all_gather(piece, "y", axis=0)), axis=-1)
            wide.append((full[:, :half], full[:, half:]))
        else:
            wide.append((piece, lanes.swap(piece, "y")))

    over_y(ffn_own)
    for _ in range(1, z_size):
        pieces.append(lanes.move(pieces[-1], "z", ring(z_size), "z"))
        over_y(pieces[-1])
    near, far = [w[0] for w in wide], [w[1] for w in wide]
    cotangent = trade(cotangent, None)
    which = (y if y_size == 2 else y * 0).astype(jnp.int32).reshape(1)

    segment = lax.dynamic_index_in_dim(
        jnp.where(c == z % 2, segments, other_segments), z // 2, 0, keepdims=False
    )
    place = lax.broadcasted_iota(jnp.int32, (length,), 0) - jnp.sum(
        (segment[None, :] < segment[:, None]).astype(jnp.int32), axis=1
    )
    frequency = theta_base ** (-2.0 * jnp.arange(head // 2, dtype=f32) / head)
    angles = place.astype(f32)[:, None] * frequency
    cosine, sine = jnp.cos(angles), jnp.sin(angles)
    cosine = jnp.concatenate([cosine] * 4, axis=1)
    sine = jnp.concatenate([-sine, sine] * 2, axis=1)
    seg_col, seg_row = segment[:, None], segment[None, :]

    inputs = tokens.astype(f32)
    root_one = lax.rsqrt(jnp.mean(inputs * inputs, axis=-1, keepdims=True) + epsilon)
    hat_one = inputs * root_one
    all_root = lax.rsqrt(jnp.mean(all_tokens * all_tokens, axis=-1, keepdims=True) + epsilon)
    normed_one = (all_tokens * all_root * gain_one).astype(bf16)
    normed_one = after(normed_one, pieces[1])
    qkv = dot(normed_one, qkv_full, 1, 1).astype(bf16)
    qkv = after(qkv, cotangent)
    tables = (cosine, sine, seg_col, seg_row, head_gains, head)
    context = attend(qkv, *tables, 0, z_size // 2)
    qkv = after(qkv, context, pieces[z_size // 2], far[0])
    context = jnp.concatenate([context, attend(qkv, *tables, z_size // 2, z_size - z_size // 2)], axis=1)

    def half_rows(value, index):
        return lax.dynamic_slice_in_dim(value, index * own_rows, own_rows, 0)

    def core_reduce(left, right, right_dim):
        sent = dot(half_rows(left, 1 - c), right, 1, right_dim).astype(bf16)
        kept = dot(half_rows(left, c), right, 1, right_dim)
        return kept + lanes.swap(sent, "c").astype(f32)

    def spread(value, *earlier):
        across = lanes.swap(value, "x")
        over = lanes.swap(after(across, *earlier) if earlier else across, "c")
        return [value, lanes.swap(value, "c"), across, over]

    cots = spread(cotangent)
    mid = inputs + core_reduce(after(context, cots[2], far[1]), o_full, 0)
    root_two = lax.rsqrt(jnp.mean(mid * mid, axis=-1, keepdims=True) + epsilon)
    hat_two = mid * root_two
    normed_two = (hat_two * gain_two).astype(bf16)
    rows_two = spread(normed_two, far[-2])

    count = z_size // 2
    slot_grads, arrived = [None] * z_size, [None] * z_size

    def turn(group):
        return sorted(range(count), key=lambda i: (group * count + i - 1) % z_size)

    def send_gradients(sent, kept):
        if y_size > 2:
            full = jnp.concatenate([kept, sent], axis=1)
            full = jnp.stack([full[:, k * quad : (k + 1) * quad] for k in range(y_size)])
            got = lax.psum_scatter(full, "y", scatter_dimension=0, tiled=False)
            return got, got.astype(f32)
        got = lanes.swap(sent, "y")
        return got, plus(kept, got)

    gu_0, hid_0, sent, kept = ffn_first(which, near[:count], far[:count], rows_two, cots, turn(0))
    arrived[1], value = send_gradients(sent, kept)
    for i, slot in enumerate(turn(0)):
        slot_grads[slot] = value[i * 3 * sub : (i + 1) * 3 * sub]
    gu_1, hid_1, (first, second, third, fourth) = ffn_second(which, near, far, rows_two, cots, gu_0)
    third = plus(third, lanes.swap(fourth, "c")).astype(bf16)
    across = lanes.swap(third, "x")
    second = lanes.swap(second, "c")
    sent, kept, (out_first, out_second, out_third, out_fourth) = ffn_third(
        after(which, third), near, far, rows_two, cots, gu_1, hid_1, hid_0, turn(1)
    )
    for i in turn(1):
        lanes.last.pop("y", None)
        arrived[count + i], slot_grads[count + i] = send_gradients(sent[i], kept[i])
    ring_first = slot_grads[1].astype(bf16)
    total = lanes.move(ring_first, "z", ring(z_size), "z")
    grad_normed_two = after(plus(first, second, across), out_first)


    def norm_back(grad, hat, root):
        return root * (grad - hat * jnp.mean(grad * hat, axis=-1, keepdims=True))

    gain_two_part = jnp.sum(grad_normed_two * hat_two, axis=0)
    grad_mid = cotangent.astype(f32) + norm_back(grad_normed_two * gain_two, hat_two, root_two)

    branch_own = grad_mid.astype(bf16)
    branch = by_index(c, branch_own, lanes.swap(branch_own, "c"), 0)
    grad_context = dot(branch, o_full, 1, 1).astype(bf16)
    o_grad = dot(after(context, grad_context), branch, 0, 0).astype(bf16)
    grad_context = after(grad_context, o_grad, ring_first)
    grad_first, sums_first = attend_back(qkv, *tables[:-1], grad_context, head, 0, z_size // 2)
    out_third = plus(out_third, lanes.swap(out_fourth, "c")).astype(bf16)
    out_third = after(out_third, grad_normed_two)
    out_across = lanes.move(out_third, "x", [(0, 1), (1, 0)], None)
    output = mid + plus(out_first, lanes.swap(out_second, "c"), after(out_across, grad_first))
    output = output.astype(bf16)
    if y_size > 2:
        o_part = plane_scatter(o_grad, sizes, pair, lanes).astype(bf16)
        o_far = o_part
    else:
        block = lambda a, b: lane_block(o_grad, a * x_size + b, pair)
        o_far = lanes.move(block(1 - y, 1 - x), "x", [(0, 1), (1, 0)], None)
        o_near = lanes.move(block(y, 1 - x), "x", [(0, 1), (1, 0)], None)
        o_far = plus(block(1 - y, x), after(o_far, grad_first, output)).astype(bf16)
        o_part = plus(block(y, x), o_near)
    total = plus(after(total, grad_first), slot_grads[2]).astype(bf16)
    grad_last, sums_last = attend_back(
        qkv, *tables[:-1], after(grad_context, total, o_far), head, z_size // 2, z_size - z_size // 2
    )
    if y_size == 2:
        o_far = lanes.move(o_far, "y", [(0, 1), (1, 0)], None)
        o_part = plus(o_part, after(o_far, grad_last)).astype(bf16)
    total = lanes.move(total, "z", ring(z_size), "z")
    output_got = lanes.move(after(output, total), ("c", "z"), pairs, None)
    grad_last = after(grad_last, o_part, arrived[-1])
    for step in range(2, z_size - 1):
        total = plus(after(total, grad_last), slot_grads[step + 1]).astype(bf16)
        grad_last = after(grad_last, total)
        total = lanes.move(total, "z", ring(z_size), "z")
    total_last = plus(total, slot_grads[0])
    extra = [jnp.zeros((1, width), f32), gain_two_part[None], jnp.zeros((14, width), f32)]
    spaced = part < 2 * head
    if spaced:
        sums = jnp.sum(jnp.concatenate([sums_first, sums_last]).reshape(-1, 8, 2 * head), axis=0)
        extra[2:] = [
            jnp.pad(v.reshape(parts, gain_part), ((0, 0), (0, part - gain_part))).reshape(1, width)
            for v in (sums[0, :head] + sums[0, head:], sums[1, :head])
        ] + [jnp.zeros((12, width), f32)]
    extra = jnp.concatenate(extra, axis=0)
    if y_size > 2:
        starts = [which[0] + i * (width // 4) for i in range(4)]
    else:
        starts = [(a * x_size + b) * pair for a, b in ((1 - y, 1 - x), (y, 1 - x), (1 - y, x), (y, x))]
    given = (qkv_full, extra, gain_one, (sums_first, sums_last), z_size, spaced)
    blocks = list(qkv_grads(starts[:1], (grad_first, grad_last), normed_one, *given))
    grad_last = after(grad_last, blocks[0])
    blocks += qkv_grads(starts[1:], (grad_first, grad_last), normed_one, *given)
    if y_size == 2:
        far_got = lanes.move(blocks[0], "x", [(0, 1), (1, 0)], None)
    grad_first = after(grad_first, blocks[3])
    cut = grad_first.shape[1]

    def two_terms(index):
        return dot(half_rows(grad_first, index), qkv_full[:cut], 1, 0) + dot(
            half_rows(grad_last, index), qkv_full[cut:], 1, 0
        )

    sent = two_terms(1 - c).astype(bf16)
    grad_normed_one = two_terms(c) + lanes.swap(sent, "c").astype(f32)
    tokens_grad = (grad_mid + norm_back(grad_normed_one * gain_one, hat_one, root_one)).astype(bf16)
    if y_size > 2:
        qkv_part = plane_scatter(jnp.concatenate(blocks, axis=1), sizes, pair, lanes).astype(bf16)
    else:
        near_got = lanes.move(after(blocks[1], far_got), "x", [(0, 1), (1, 0)], None)
        lanes.last["x"] = (near_got,)
        far_sum = plus(blocks[2], far_got).astype(bf16)
        y_got = after(lanes.swap(far_sum, "y"), output_got, tokens_grad)
        qkv_part = plus(blocks[3], near_got, y_got).astype(bf16)

    def core_deal(value):
        kept = lane_block(value, c, part)
        sent = lanes.swap(lane_block(value, 1 - c, part), "c")
        return jnp.where(c == 0, jnp.stack([kept, sent]), jnp.stack([sent, kept]))

    wgrads = total_last.astype(bf16).reshape(3, sub, quad)
    kept = lane_block(wgrads, x, pair)
    sent = lanes.swap(lane_block(wgrads, 1 - x, pair), "x")
    dealt = sent
    wgrads = jnp.where(x == 0, jnp.stack([kept, sent], 1), jnp.stack([sent, kept], 1))
    kept = lane_block(wgrads, c, part)
    sent = lanes.swap(lane_block(wgrads, 1 - c, part), "c")
    wgrads = jnp.where(c == 0, jnp.stack([kept, sent], 2), jnp.stack([sent, kept], 2))
    wgrads = wgrads.reshape(3, x_size * c_size * sub, part)
    last_grads = wgrads


    rows = qkv_rows + 16
    lanes.last.pop("z", None)
    value = z_scatter(
        [
            jnp.concatenate(
                [qkv_part[i * rows : (i + 1) * rows], o_part[i * q_rows : (i + 1) * q_rows]], axis=0
            )
            for i in range(z_size)
        ],
        z_size,
        lanes,
    )
    tokens_got = lanes.move(after(tokens_grad, lanes.last["z"][0]), ("c", "z"), pairs, None)
    value = after(value.astype(bf16), dealt)
    kept = lane_block(value, c, part)
    sent = lanes.swap(lane_block(value, 1 - c, part), "c")
    gain_sums = plus(kept[qkv_rows:rows], sent[qkv_rows:rows])
    qkv_grad = jnp.where(c == 0, jnp.stack([kept, sent]), jnp.stack([sent, kept])).astype(f32)
    o_wgrad = qkv_grad[:, rows:].reshape(2 * q_rows, part).T
    qkv_grad = qkv_grad[:, :qkv_rows]
    last_grads = after(last_grads, sent)
    gate_wgrad, up_wgrad, down_wgrad = (last_grads[i].astype(f32).T for i in range(3))
    q_wgrad = qkv_grad[:, :q_rows].reshape(-1, part).T
    k_wgrad = qkv_grad[:, q_rows : q_rows + k_rows].reshape(-1, part).T
    v_wgrad = qkv_grad[:, q_rows + k_rows :].reshape(-1, part).T
    if spaced:
        gain_query_sum, gain_key_sum = gain_sums[2, :gain_part], gain_sums[3, :gain_part]
    else:
        mine = ((y * x_size + x) * c_size + c) * gain_part
        gain_query_sum, gain_key_sum = (
            lax.dynamic_slice(gain_sums[2], (mine + at,), (gain_part,)) for at in (0, head)
        )
    return (
        jnp.where(trades, output_got, output),
        jnp.where(trades, tokens_got, tokens_grad),
        gain_sums[0],
        q_wgrad,
        k_wgrad,
        v_wgrad,
        gain_query_sum,
        gain_key_sum,
        o_wgrad,
        gain_sums[1],
        gate_wgrad,
        up_wgrad,
        down_wgrad,
    )


def solution(mesh):
    dp, tp = mesh.devices.shape
    sizes = (dp // 4, 2, 2, tp)
    fine = Mesh(mesh.devices.reshape(sizes), ("y", "x", "c", "z"))
    d = ("y", "x", "c")
    rows, weight, gain = P((*d, "z"), None), P(d, "z"), P(d)
    return jax.shard_map(
        functools.partial(shards, sizes),
        mesh=fine,
        in_specs=(rows, P(d, None), rows, gain, weight, weight, weight, gain, gain, weight, gain)
        + (weight,) * 3,
        out_specs=(rows, rows, gain, weight, weight, weight, gain, gain, weight, gain) + (weight,) * 3,
        check_vma=False,
    )
```
